256 devices in a mesh: slide: 2 (over y_hi), ty: 4 (over x), tx: 32 (over z, y_lo, core).
Axes of the slice: x: 4, y: 4 (y_hi: 2, y_lo: 2; y = y_hi * 2 + y_lo), z: 8, core: 2. Of those that a mesh axis runs over, the one named last changes fastest.
Arguments:
- features: bfloat16 [2, 128, 512, 192], P('slide', 'ty', 'tx'), may hold values from -6 to 6
- cotangent: bfloat16 [2, 128, 512, 192], P('slide', 'ty', 'tx'), may hold values from -6 to 6
- dw_kernel: float32 [2, 7, 7, 192], replicated, may hold values from -0.875 to 0.875
- conv_bias: float32 [2, 192], replicated, may hold values from -3 to 3
- ln_gain: float32 [2, 192], replicated, may hold values from 0.25 to 1.75
- ln_shift: float32 [2, 192], replicated, may hold values from -3 to 3
- up_weight: bfloat16 [2, 192, 768], replicated, may hold values from -0.4375 to 0.4375
- up_bias: float32 [2, 768], replicated, may hold values from -3 to 3
- down_weight: bfloat16 [2, 768, 192], replicated, may hold values from -0.21875 to 0.21875
- down_bias: float32 [2, 192], replicated, may hold values from -3 to 3
- layer_scale: float32 [2, 192], replicated, may hold values from 0.25 to 1
Outputs:
- out_features: bfloat16 [2, 128, 512, 192], P('slide', 'ty', 'tx')
- grad_features: float32 [2, 128, 512, 192], P('slide', 'ty', 'tx')
- grad_kernel: float32 [2, 7, 7, 192], replicated
- grad_conv_bias: float32 [2, 192], replicated
- grad_ln_gain: float32 [2, 192], replicated
- grad_ln_shift: float32 [2, 192], replicated
- grad_up_weight: float32 [2, 192, 768], replicated
- grad_up_bias: float32 [2, 768], replicated
- grad_down_weight: float32 [2, 768, 192], replicated
- grad_down_bias: float32 [2, 192], replicated
- grad_layer_scale: float32 [2, 192], replicated
The draws below stay inside these ranges and needn't reach their ends.
All inputs are finite; a program needn't handle non-finite values.
Results may differ from the reference program's by a relative error of at most 0.011.
Values may be sent and summed in bfloat16 or wider, within the bound.
A program may use at most 128 MiB of HBM per device.

```python
import math
import jax
import jax.numpy as jnp
from jax import lax

C = 192
HID = 768
TAPS = 7
LAYERS = 2
TH = 32
TW = 16
SLIDES = 2
H = 128
W = 512


def level_of(stream_key, extent, split, low, top_value):
    def one(dim, blocks):
        draws = jax.random.uniform(jax.random.fold_in(jax.random.fold_in(stream_key, 6), dim), (blocks,), jnp.float32, low / len(split), top_value / len(split))
        return jnp.repeat(jnp.exp(draws), extent[dim] // blocks).reshape((-1,) + (1,) * (len(extent) - dim - 1))

    loudness = one(*split[0])
    for cut in split[1:]:
        loudness = loudness * one(*cut)
    return loudness


def scatter_about(stream_key, extent, width, bound, cuts=(), kind=jnp.bfloat16):
    level = level_of(stream_key, extent, cuts, -0.22, 0.18) if cuts else 1.0
    array = jax.random.normal(stream_key, extent, jnp.float32) * width * level
    return jnp.minimum(jnp.maximum(array, -bound), bound).astype(kind)


def setup_inputs(seed: int = 0) -> dict:
    splits = jax.random.split(jax.random.key(seed), 12)
    return {
        "features": scatter_about(splits[0], (SLIDES, H, W, C), 1.0, 6.0, ((0, 2), (1, 4), (2, 32))),
        "cotangent": scatter_about(splits[1], (SLIDES, H, W, C), 1.0, 6.0, ((0, 2), (1, 4), (2, 32))),
        "dw_kernel": scatter_about(splits[2], (LAYERS, TAPS, TAPS, C), (TAPS * TAPS) ** -0.5, 0.875, (), jnp.float32),
        "conv_bias": scatter_about(splits[3], (LAYERS, C), 0.5, 3.0, (), jnp.float32),
        "ln_gain": jnp.clip(1.0 + 0.15 * jax.random.normal(splits[4], (LAYERS, C), jnp.float32), 0.25, 1.75),
        "ln_shift": scatter_about(splits[5], (LAYERS, C), 0.5, 3.0, (), jnp.float32),
        "up_weight": scatter_about(splits[6], (LAYERS, C, HID), C ** -0.5, 0.4375),
        "up_bias": scatter_about(splits[7], (LAYERS, HID), 0.5, 3.0, (), jnp.float32),
        "down_weight": scatter_about(splits[8], (LAYERS, HID, C), HID ** -0.5, 0.21875),
        "down_bias": scatter_about(splits[9], (LAYERS, C), 0.5, 3.0, (), jnp.float32),
        "layer_scale": jnp.clip(jnp.exp(jax.random.uniform(splits[10], (LAYERS, C), jnp.float32, math.log(0.25), math.log(1.0))), 0.25, 1.0),
    }


ROOT_HALF = 0.7071067811865476
INV_ROOT_TAU = 0.3989422804014327
EPSILON = 1e-06

def gelu_value(argument):
    return argument * 0.5 * (1.0 + lax.erf(argument * ROOT_HALF))

def gelu_slope(argument):
    return 0.5 * (1.0 + lax.erf(argument * ROOT_HALF)) + argument * INV_ROOT_TAU * jnp.exp(-0.5 * argument * argument)

def conv_valid(padded, tap_weights):
    kernel_span = tap_weights.shape[0]
    out_rows = padded.shape[-3] - kernel_span + 1
    out_cols = padded.shape[-2] - kernel_span + 1
    running = jnp.zeros(padded.shape[:-3] + (out_rows, out_cols, padded.shape[-1]), jnp.float32)
    for tap_row in range(kernel_span):
        for tap_col in range(kernel_span):
            window = padded[..., tap_row:tap_row + out_rows, tap_col:tap_col + out_cols, :]
            running = running + window.astype(jnp.float32) * tap_weights[tap_row, tap_col]
    return running

def point_forward(conv_rows, weights):
    tap_weights, conv_shift, norm_gain, norm_shift, up_weight, up_bias, down_weight, down_bias, layer_scale = weights
    row_mean = lax.optimization_barrier(jnp.mean(conv_rows, axis=-1, keepdims=True))
    centred = conv_rows - row_mean
    inv_std = lax.rsqrt(lax.optimization_barrier(jnp.mean(centred * centred, axis=-1, keepdims=True)) + EPSILON)
    unit_rows = centred * inv_std
    normed = (unit_rows * norm_gain + norm_shift).astype(jnp.bfloat16)
    pre_act = jnp.dot(normed, up_weight, preferred_element_type=jnp.float32) + up_bias
    activated = gelu_value(pre_act).astype(jnp.bfloat16)
    branch = jnp.dot(activated, down_weight, preferred_element_type=jnp.float32) + down_bias
    return (unit_rows, inv_std, normed, pre_act, activated, branch)

def point_backward(grad_rows, saved, weights):
    tap_weights, conv_shift, norm_gain, norm_shift, up_weight, up_bias, down_weight, down_bias, layer_scale = weights
    unit_rows, inv_std, normed, pre_act, activated, branch = saved
    grad_scale = lax.optimization_barrier(jnp.sum(grad_rows * branch, axis=0))
    grad_branch = (grad_rows * layer_scale).astype(jnp.bfloat16)
    grad_down_bias = lax.optimization_barrier(jnp.sum(grad_branch.astype(jnp.float32), axis=0))
    grad_down = lax.dot_general(activated, grad_branch, (((0,), (0,)), ((), ())), preferred_element_type=jnp.float32)
    grad_act = lax.dot_general(grad_branch, down_weight, (((1,), (1,)), ((), ())), preferred_element_type=jnp.float32)
    grad_pre = (grad_act * gelu_slope(pre_act)).astype(jnp.bfloat16)
    grad_up_bias = lax.optimization_barrier(jnp.sum(grad_pre.astype(jnp.float32), axis=0))
    grad_up = lax.dot_general(normed, grad_pre, (((0,), (0,)), ((), ())), preferred_element_type=jnp.float32)
    grad_normed = lax.dot_general(grad_pre, up_weight, (((1,), (1,)), ((), ())), preferred_element_type=jnp.float32)
    grad_gain = lax.optimization_barrier(jnp.sum(grad_normed * unit_rows, axis=0))
    grad_shift = lax.optimization_barrier(jnp.sum(grad_normed, axis=0))
    scaled = grad_normed * norm_gain
    centred_grad = scaled - lax.optimization_barrier(jnp.mean(scaled, axis=-1, keepdims=True)) - unit_rows * lax.optimization_barrier(jnp.mean(scaled * unit_rows, axis=-1, keepdims=True))
    grad_conv = (inv_std * centred_grad).astype(jnp.bfloat16)
    return (grad_conv, (grad_gain, grad_shift, grad_up, grad_up_bias, grad_down, grad_down_bias, grad_scale))

def layer_params(params, layer_no):
    return tuple((member[layer_no] for member in params))

def reference(features, cotangent, dw_kernel, conv_bias, ln_gain, ln_shift, up_weight, up_bias, down_weight, down_bias, layer_scale):
    params = (dw_kernel, conv_bias, ln_gain, ln_shift, up_weight, up_bias, down_weight, down_bias, layer_scale)
    margin = TAPS // 2
    block_rows = TH * TW
    channels = features.shape[3]
    hidden = up_weight.shape[2]
    map_rows = features.shape[1]
    map_cols = features.shape[2]
    pad_spec = ((0, 0), (margin, margin), (margin, margin), (0, 0))
    current = features
    layer_inputs = []
    for layer_no in range(LAYERS):
        weights = layer_params(params, layer_no)
        layer_inputs.append(current)
        padded = jnp.pad(current.astype(jnp.float32), pad_spec)
        conv_map = conv_valid(padded, weights[0]) + weights[1]
        conv_blocks = conv_map.reshape(-1, block_rows, channels)
        branch = lax.map(lambda conv_rows: point_forward(conv_rows, weights)[5], conv_blocks)
        current = (current.astype(jnp.float32) + weights[8] * branch.reshape(conv_map.shape)).astype(jnp.bfloat16)
    gradient = cotangent.astype(jnp.float32)
    collected = [None] * LAYERS
    for layer_no in reversed(range(LAYERS)):
        weights = layer_params(params, layer_no)
        padded = jnp.pad(layer_inputs[layer_no].astype(jnp.float32), pad_spec)
        conv_map = conv_valid(padded, weights[0]) + weights[1]
        conv_blocks = conv_map.reshape(-1, block_rows, channels)
        grad_blocks = gradient.reshape(-1, block_rows, channels)

        def step_block(carried, pieces):
            saved = point_forward(pieces[0], weights)
            grad_conv, terms = point_backward(pieces[1], saved, weights)
            return (jax.tree.map(jnp.add, carried, terms), grad_conv)
        zero_terms = (jnp.zeros((channels,), jnp.float32), jnp.zeros((channels,), jnp.float32), jnp.zeros((channels, hidden), jnp.float32), jnp.zeros((hidden,), jnp.float32), jnp.zeros((hidden, channels), jnp.float32), jnp.zeros((channels,), jnp.float32), jnp.zeros((channels,), jnp.float32))
        summed, grad_conv = lax.scan(step_block, zero_terms, (conv_blocks, grad_blocks))
        conv_grad_f = grad_conv.reshape(conv_map.shape).astype(jnp.float32)
        grad_cbias = lax.optimization_barrier(jnp.sum(conv_grad_f, axis=(0, 1, 2)))
        grad_taps = jnp.stack([jnp.stack([lax.optimization_barrier(jnp.sum(conv_grad_f * padded[:, tap_row:tap_row + map_rows, tap_col:tap_col + map_cols, :], axis=(0, 1, 2))) for tap_col in range(TAPS)]) for tap_row in range(TAPS)])
        grad_padded = jnp.pad(conv_grad_f, pad_spec)
        gradient = gradient + conv_valid(grad_padded, weights[0][::-1, ::-1])
        collected[layer_no] = (grad_taps, grad_cbias) + summed
    factor = 1.0 / math.sqrt(features.shape[0] * map_rows * map_cols)
    stacked = tuple((jnp.stack([collected[layer_no][member] for layer_no in range(LAYERS)]) * factor for member in range(9)))
    return (current, gradient, stacked[0], stacked[1], stacked[2], stacked[3], stacked[4], stacked[5], stacked[6], stacked[7], stacked[8])
```

```python
import functools
import math

import jax
import jax.numpy as jnp
import numpy as np
from jax import lax
from jax.experimental import pallas as pl
from jax.experimental.pallas import tpu as pltpu
from jax.sharding import PartitionSpec as P

MESH = pl.DeviceIdType.MESH
F32 = jnp.float32
BF16 = jnp.bfloat16
ROOT_HALF = 0.7071067811865476
INV_ROOT_TAU = 0.3989422804014327
EPSILON = 1e-06

TR, TC, CH, HID = 32, 16, 192, 768
PX = TR * TC
NI, NS = 4, 8
MARGIN = 3
SPAN = 7
TAPS = SPAN * SPAN
LANES = 128
REST = CH - LANES
PACK = TC + TC // 2
WIDE = (TC + 2 * MARGIN) + (TC // 2 + 2 * MARGIN)
BIG = 72
ROWS = 80
CHUNKS = 16
NZ = 8
HALOS = ((-1, -1), (-1, 0), (-1, 1), (1, -1), (1, 0), (1, 1), (0, -1), (0, 1))

ROW_CBIAS, ROW_GAIN, ROW_SHIFT, ROW_DBIAS, ROW_SCALE, ROW_UBIAS = 98, 100, 102, 104, 106, 108


def pixel_order():
    q = np.arange(PX)
    return (4 * (q % NS) + q // (TC * NS)) * TC + (q // NS) % TC


def one_hots():
    order = pixel_order()
    place = np.zeros((PX, PX), np.float32)
    place[np.arange(PX), order] = 1.0
    inverse = np.argsort(order)
    edge_rows = np.concatenate([np.arange(3 * TC), np.arange((TR - 3) * TC, TR * TC)])
    edges = np.zeros((6 * TC, PX), np.float32)
    edges[np.arange(6 * TC), inverse[edge_rows]] = 1.0
    spread = np.zeros((2, 3, TC + 6, NS, 3, 3, TC), np.float32)
    for cc in range(TC + 6):
        source, column = (0, TC - 3 + cc) if cc < 3 else (1, cc - 3) if cc < TC + 3 else (2, cc - TC - 3)
        for u in range(3):
            spread[0, u, cc, 0, source, u, column] = 1.0
            spread[1, u, cc, NS - 1, source, u, column] = 1.0
    spread = spread.reshape(2, 3 * (TC + 6) * NS, 9 * TC)
    return place, edges, spread


def tn(a, b):
    return lax.dot_general(a, b, (((0,), (0,)), ((), ())), preferred_element_type=F32)


def nt(a, b):
    return lax.dot_general(a, b, (((1,), (1,)), ((), ())), preferred_element_type=F32)


def nn(a, b):
    return jnp.dot(a, b, preferred_element_type=F32)


def kernel(
    factor,
    feat, cot, wexp, wflip, cbias, gain, shift, up, ubias, down, dbias, scale, place, edges, spread,
    out_ref, gfeat_ref, result,
    xp, gx, qa, qg, cbuf, conv, unit, inv, normed, act, slope, branch, gbr, gpre, gcp, tq, taps, small,
    grad, outq, pay, corebuf, sbuf, rbuf, zbuf,
    csend, rsend, crecv, rrecv,
    hs, hr, cs, cr, xs, xr, zs, zr, gs, gr, ls, lr,
):
    yh = lax.axis_index("slide")
    ty = lax.axis_index("ty")
    tx = lax.axis_index("tx")
    core = lax.rem(tx, 2)
    yl = lax.rem(lax.div(tx, 2), 2)
    z = lax.div(tx, 4)
    other = 1 - core
    me = ty * 4 + yh * 2 + yl
    sibling = (yh, ty, z * 4 + yl * 2 + other)

    def plane_peer(d):
        py = lax.rem(ty + lax.div(d, 4), 4)
        ph = lax.rem(yh + lax.rem(lax.div(d, 2), 2), 2)
        pl_ = lax.rem(yl + lax.rem(d, 2), 2)
        return py * 4 + ph * 2 + pl_, (ph, py, z * 4 + pl_ * 2 + core)

    def z_peer(d):
        pz = lax.rem(z + d, NZ)
        return pz, (yh, ty, pz * 4 + yl * 2 + core)

    barrier = pltpu.get_barrier_semaphore()

    def greet(device):
        pl.semaphore_signal(barrier, inc=1, device_id=device, device_id_type=MESH)

    for dy, dx in HALOS:
        greet((yh, lax.rem(ty + dy + 4, 4), lax.rem(tx + dx + 32, 32)))
    greet(sibling)

    @pl.loop(1, CHUNKS)
    def _(d):
        greet(plane_peer(d)[1])

    @pl.loop(1, NZ)
    def _(d):
        greet(z_peer(d)[1])

    def there(dy, dx):
        flags = []
        if dy:
            flags.append(jnp.logical_and(ty + dy >= 0, ty + dy < 4))
        if dx:
            flags.append(jnp.logical_and(tx + dx >= 0, tx + dx < 32))
        return functools.reduce(jnp.logical_and, flags)

    def halo_copy(n, dy, dx):
        if dy == 0:
            slot = 6 if dx > 0 else 7
            src, dst = csend.at[n, 0 if dx < 0 else 1], crecv.at[n, slot - 6]
        else:
            slot = (1 if dy > 0 else 4) - dx
            src, dst = rsend.at[n, 0 if dy < 0 else 1], rrecv.at[n, slot]
        return pltpu.make_async_remote_copy(
            src_ref=src, dst_ref=dst, send_sem=hs.at[n, slot], recv_sem=hr.at[n, slot],
            device_id=(yh, ty + dy, tx + dx), device_id_type=MESH,
        )

    def halo_start(n, plane):
        flat = jnp.concatenate([plane[i, 3 : 3 + TC].reshape(TC * NS, CH) for i in range(NI)], axis=0)
        strips = nn(edges[...], flat.astype(BF16)).astype(BF16)
        rsend[n] = strips.reshape(2, 3, TC, CH)
        for c in range(3):
            csend[n, 0, c] = plane[:, 3 + c].reshape(TR, CH).astype(BF16)
            csend[n, 1, c] = plane[:, TC + c].reshape(TR, CH).astype(BF16)
        if n == 0:
            pl.semaphore_wait(barrier, 8 + 1 + CHUNKS - 1 + NZ - 1)
        for dy, dx in HALOS:

            @pl.when(there(dy, dx))
            def _(dy=dy, dx=dx):
                halo_copy(n, dy, dx).start()

    def halo_wait(n):
        for dy, dx in HALOS:

            @pl.when(there(-dy, -dx))
            def _(dy=dy, dx=dx):
                halo_copy(n, dy, dx).wait_recv()

            @pl.when(jnp.logical_not(there(-dy, -dx)))
            def _(dy=dy, dx=dx):
                if dy == 0:
                    crecv[n, 0 if dx > 0 else 1] = jnp.zeros((3, TR, CH), BF16)
                else:
                    rrecv[n, (1 if dy > 0 else 4) - dx] = jnp.zeros((3, TC, CH), BF16)

    def halo_done(n):
        for dy, dx in HALOS:

            @pl.when(there(dy, dx))
            def _(dy=dy, dx=dx):
                halo_copy(n, dy, dx).wait_send()

    def assemble(n, plane, q):
        for c in range(3):
            plane[:, c] = crecv[n, 0, c].astype(F32).reshape(NI, NS, CH)
            plane[:, TC + 3 + c] = crecv[n, 1, c].astype(F32).reshape(NI, NS, CH)
        for side in range(2):
            strips = jnp.concatenate([rrecv[n, 3 * side + k].reshape(3 * TC, CH) for k in range(3)], axis=0)
            tq[side] = nn(spread[side], strips).reshape(3, TC + 6, NS, CH)
        row = lax.broadcasted_iota(jnp.int32, (3, NS, LANES), 1)

        def fill(slot, mid, top, low):
            q[3:7, slot] = mid
            q[0:3, slot] = jnp.where(row == 0, top, pltpu.roll(mid[1:4], 1, 1))
            q[7:10, slot] = jnp.where(row == NS - 1, low, pltpu.roll(mid[0:3], NS - 1, 1))

        @pl.loop(0, TC + 6)
        def _(cc):
            fill(cc, plane[:, cc, :, :LANES], tq[0, :, cc, :, :LANES], tq[1, :, cc, :, :LANES])

        def pair(ref, *at):
            return jnp.concatenate([ref[(*at[:-1], at[-1], slice(None), slice(LANES, CH))],
                                    ref[(*at[:-1], at[-1] + 8, slice(None), slice(LANES, CH))]], axis=-1)

        @pl.loop(0, TC // 2 + 6)
        def _(k):
            fill(TC + 6 + k, pair(plane, slice(None), k), pair(tq, 0, slice(None), k), pair(tq, 1, slice(None), k))

    def convolve(q, weights, l):
        def columns(part, t, base):
            sums = [[None, None] for _ in range(NI)]
            for j2 in range(SPAN + 1):
                for r in range(NI + SPAN - 1):
                    x = q[r, base + j2]
                    for i in range(NI):
                        if not 0 <= r - i < SPAN:
                            continue
                        for o in range(2):
                            if not 0 <= j2 - o < SPAN:
                                continue
                            term = x * weights[l, part, (r - i) * SPAN + j2 - o]
                            sums[i][o] = term if sums[i][o] is None else sums[i][o] + term
            for i in range(NI):
                for o in range(2):
                    cbuf[i, t + o] = sums[i][o]

        @pl.loop(0, TC // 2)
        def _(k):
            columns(0, 2 * k, 2 * k)

        @pl.loop(0, TC // 4)
        def _(k):
            columns(1, TC + 2 * k, TC + 6 + 2 * k)

    def conv_rows(i):
        half = TC * NS // 2
        conv[:, :LANES] = cbuf[i, :TC].reshape(TC * NS, LANES)
        rest = cbuf[i, TC:].reshape(half, LANES)
        conv[:half, LANES:] = rest[:, :REST]
        conv[half:, LANES:] = rest[:, REST:]
        return conv[...]

    blk = TC * NS

    def rows_of(i):
        return pl.ds(pl.multiple_of(i * blk, blk), blk)

    def forward(l, plane, into, i):
        c = conv_rows(i) + cbias[l : l + 1]
        mid = c - jnp.mean(c, axis=1, keepdims=True)
        rstd = lax.rsqrt(jnp.mean(mid * mid, axis=1, keepdims=True) + EPSILON)
        u = mid * rstd
        rows = rows_of(i)
        unit[l, rows] = u
        inv[l, rows] = rstd
        nb = (u * gain[l : l + 1] + shift[l : l + 1]).astype(BF16)
        normed[l, rows] = nb
        pre = nn(nb, up[l]) + ubias[l : l + 1]
        cdf = 0.5 * (1.0 + lax.erf(pre * ROOT_HALF))
        slope[l, rows] = cdf + pre * INV_ROOT_TAU * jnp.exp(-0.5 * pre * pre)
        ab = (pre * cdf).astype(BF16)
        act[l, rows] = ab
        br = nn(ab, down[l]) + dbias[l : l + 1]
        branch[l, rows] = br
        before = plane[i, 3 : 3 + TC].reshape(blk, CH)
        new = (before + scale[l : l + 1] * br).astype(BF16)
        into(i, new)

    def backward(l, grad_rows, i, sums):
        rows = rows_of(i)
        g = grad_rows(i)
        s_gain, s_shift, s_dbias, s_scale, s_ubias, s_cbias = sums

        def fold(v):
            return jnp.sum(v.reshape(blk // 8, 8, v.shape[1]), axis=0)

        s_scale = s_scale + fold(g * branch[l, rows])
        gb = (g * scale[l : l + 1]).astype(BF16)
        gbr[rows] = gb
        s_dbias = s_dbias + fold(gb.astype(F32))
        gp = (nt(gb, down[l]) * slope[l, rows]).astype(BF16)
        gpre[rows] = gp
        s_ubias = s_ubias + fold(gp.astype(F32))
        gn = nt(gp, up[l])
        u = unit[l, rows]
        gnu = gn * u
        s_gain = s_gain + fold(gnu)
        s_shift = s_shift + fold(gn)
        q = gn * gain[l : l + 1]
        centred = q - jnp.mean(q, axis=1, keepdims=True) - u * jnp.mean(q * u, axis=1, keepdims=True)
        gc = (inv[l, rows] * centred).astype(BF16).astype(F32)
        s_cbias = s_cbias + fold(gc)
        gx[i, 3 : 3 + TC] = gc.reshape(TC, NS, CH)
        gcp[i, :TC] = gc[:, :LANES].reshape(TC, NS, LANES)
        half = blk // 2
        gcp[i, TC:, :, :REST] = gc[:half, LANES:].reshape(TC // 2, NS, REST)
        gcp[i, TC:, :, REST:] = gc[half:, LANES:].reshape(TC // 2, NS, REST)
        return s_gain, s_shift, s_dbias, s_scale, s_ubias, s_cbias

    def backward_all(l, grad_rows):
        zero = jnp.zeros((8, CH), F32)
        start = (zero, zero, zero, zero, jnp.zeros((8, HID), F32), zero)
        return lax.fori_loop(0, NI, lambda i, sums: backward(l, grad_rows, i, sums), start)

    def weight_grads(l):
        for m, (a, b) in enumerate(((normed.at[l], gpre), (gbr, act.at[l]))):
            for t in range(3):
                part = tn(a[...], b[:, 256 * t : 256 * t + 256])
                for v in range(2):
                    for r in range(8):
                        piece = m * 48 + (2 * t + v) * 8 + r
                        chunk, slot = divmod(piece, 3)
                        pay[l, chunk // CHUNKS, chunk % CHUNKS, 24 * slot : 24 * slot + 24] = part[
                            24 * r : 24 * r + 24, LANES * v : LANES * v + LANES
                        ]

    def tap_grads(l):
        for part, (cols, base, first) in enumerate(((TC, 0, 0), (TC // 2, TC + 6, TC))):

            @pl.loop(0, SPAN)
            def _(j):
                def body(c, sums):
                    sums = list(sums)
                    for o in range(2):
                        col = 2 * c + o
                        gcs = [gcp[i, first + col] for i in range(NI)]
                        for r in range(NI + SPAN - 1):
                            x = qa[l, r, base + col + j]
                            for i in range(NI):
                                if 0 <= r - i < SPAN:
                                    sums[r - i] = sums[r - i] + gcs[i] * x
                    return tuple(sums)

                zero = jnp.zeros((NS, LANES), F32)
                sums = lax.fori_loop(0, cols // 2, body, (zero,) * SPAN)
                for r in range(SPAN):
                    taps[part, r * SPAN + j] = sums[r]

    def small_grads(l, sums):
        s_gain, s_shift, s_dbias, s_scale, s_ubias, s_cbias = sums
        small[...] = jnp.zeros((LANES, LANES), F32)
        small[:TAPS] = jnp.sum(taps[0], axis=1)
        rest = jnp.sum(taps[1], axis=1)
        small[TAPS : 2 * TAPS, :REST] = rest[:, :REST] + rest[:, REST:]
        for at, v in ((ROW_CBIAS, s_cbias), (ROW_GAIN, s_gain), (ROW_SHIFT, s_shift),
                      (ROW_DBIAS, s_dbias), (ROW_SCALE, s_scale)):
            v = jnp.sum(v, axis=0, keepdims=True)
            small[at : at + 1] = v[:, :LANES]
            small[at + 1 : at + 2, :REST] = v[:, LANES:]
        v = jnp.sum(s_ubias, axis=0, keepdims=True)
        for t in range(6):
            small[ROW_UBIAS + t : ROW_UBIAS + t + 1] = v[:, LANES * t : LANES * t + LANES]
        upper = lax.broadcasted_iota(jnp.int32, (8, LANES), 0) < 4
        for k in range(2 * CHUNKS):
            v = small[8 * (k // 2) : 8 * (k // 2) + 8]
            if k % 2:
                v = pltpu.roll(v, 4, 0)
            pay[l, k // CHUNKS, k % CHUNKS, BIG:] = jnp.where(upper, v, 0.0)

    upper = lax.broadcasted_iota(jnp.int32, (8, LANES), 0) < 4

    def rounded(v, store):
        s = v[BIG:]
        s = s + pltpu.roll(s, 4, 0)
        high = s.astype(BF16).astype(F32)
        store(jnp.concatenate([v[:BIG], jnp.where(upper, high, s - high)], axis=0).astype(BF16))

    def core_copy(l):
        return pltpu.make_async_remote_copy(
            src_ref=pay.at[l, other], dst_ref=corebuf.at[l], send_sem=cs.at[l], recv_sem=cr.at[l],
            device_id=sibling, device_id_type=MESH,
        )

    def plane_copy(l, d):
        index, device = plane_peer(d)
        return pltpu.make_async_remote_copy(
            src_ref=sbuf.at[l, index], dst_ref=rbuf.at[l, d], send_sem=xs.at[l, d], recv_sem=xr.at[l, d],
            device_id=device, device_id_type=MESH,
        )

    def z_copy(l, d):
        return pltpu.make_async_remote_copy(
            src_ref=zbuf.at[l, z], dst_ref=zbuf.at[l, z], send_sem=zs.at[l, d], recv_sem=zr.at[l, z],
            device_id=z_peer(d)[1], device_id_type=MESH,
        )

    def z_arrival(l, d):
        pz, device = z_peer(d)
        return pltpu.make_async_remote_copy(
            src_ref=zbuf.at[l, pz], dst_ref=zbuf.at[l, pz], send_sem=zs.at[l, d], recv_sem=zr.at[l, pz],
            device_id=device, device_id_type=MESH,
        )

    def gather_copy(l, d):
        return pltpu.make_async_remote_copy(
            src_ref=result.at[l, core, me], dst_ref=result.at[l, core, me], send_sem=gs.at[l, d],
            recv_sem=gr.at[l, me], device_id=plane_peer(d)[1], device_id_type=MESH,
        )

    def gather_arrival(l, d):
        index, device = plane_peer(d)
        return pltpu.make_async_remote_copy(
            src_ref=result.at[l, core, index], dst_ref=result.at[l, core, index], send_sem=gs.at[l, d],
            recv_sem=gr.at[l, index], device_id=device, device_id_type=MESH,
        )

    def relay_copy(l, index):
        return pltpu.make_async_remote_copy(
            src_ref=result.at[l, core, index], dst_ref=result.at[l, core, index], send_sem=ls.at[l, index],
            recv_sem=lr.at[l, index], device_id=sibling, device_id_type=MESH,
        )

    def relay_arrival(l, index):
        return pltpu.make_async_remote_copy(
            src_ref=result.at[l, other, index], dst_ref=result.at[l, other, index], send_sem=ls.at[l, index],
            recv_sem=lr.at[l, index], device_id=sibling, device_id_type=MESH,
        )

    def to_plane(l):
        core_copy(l).wait_recv()

        @pl.loop(0, CHUNKS)
        def _(k):
            d = lax.rem(k + 1, CHUNKS)
            index, _ = plane_peer(d)
            v = pay[l, core, index] + corebuf[l, index]

            def store(r):
                sbuf[l, index] = r

            rounded(v, store)

            @pl.when(d > 0)
            def _():
                plane_copy(l, d).start()

    def to_z(l):
        @pl.loop(1, CHUNKS)
        def _(d):
            plane_copy(l, d).wait_recv()

        v = lax.fori_loop(1, CHUNKS, lambda d, v: v + rbuf[l, d].astype(F32), sbuf[l, me].astype(F32))

        def store(r):
            zbuf[l, z] = r

        rounded(v, store)

        @pl.loop(1, NZ)
        def _(d):
            z_copy(l, d).start()

    def to_all(l):
        @pl.loop(1, NZ)
        def _(d):
            z_arrival(l, d).wait_recv()

        v = zbuf[l, 0].astype(F32)
        for k in range(1, NZ):
            v = v + zbuf[l, k].astype(F32)

        def store(r):
            result[l, core, me] = r

        rounded(v * factor, store)

        @pl.loop(1, CHUNKS)
        def _(d):
            gather_copy(l, d).start()

        relay_copy(l, me).start()

    def to_sibling(l):
        @pl.loop(1, CHUNKS)
        def _(d):
            gather_arrival(l, d).wait_recv()
            relay_copy(l, plane_peer(d)[0]).start()

    def finish(l):
        @pl.loop(0, CHUNKS)
        def _(k):
            relay_arrival(l, k).wait_recv()
            relay_copy(l, k).wait_send()

        core_copy(l).wait_send()

        @pl.loop(1, CHUNKS)
        def _(d):
            plane_copy(l, d).wait_send()
            gather_copy(l, d).wait_send()

        @pl.loop(1, NZ)
        def _(d):
            z_copy(l, d).wait_send()

    def flat_rows(plane, i):
        return plane[i, 3 : 3 + TC].reshape(blk, CH)

    def cot_rows(i):
        return grad[rows_of(i)]

    def step_back(l):
        @pl.loop(0, NI)
        def _(i):
            rows = rows_of(i)
            grad[rows] = grad[rows] + conv_rows(i)

    xp[0, :, 3 : 3 + TC] = nn(place[...], feat[...]).reshape(NI, TC, NS, CH)
    halo_start(0, xp.at[0])
    grad[...] = nn(place[...], cot[...])
    halo_wait(0)
    assemble(0, xp.at[0], qa.at[0])
    convolve(qa.at[0], wexp, 0)

    def keep(i, new):
        xp[1, i, 3 : 3 + TC] = new.astype(F32).reshape(TC, NS, CH)

    @pl.loop(0, NI)
    def _(i):
        forward(0, xp.at[0], keep, i)

    halo_start(1, xp.at[1])
    halo_wait(1)
    assemble(1, xp.at[1], qa.at[1])
    convolve(qa.at[1], wexp, 1)

    def keep_out(i, new):
        outq[rows_of(i)] = new

    @pl.loop(0, NI)
    def _(i):
        forward(1, xp.at[1], keep_out, i)

    sums = backward_all(1, cot_rows)
    halo_start(2, gx)
    weight_grads(1)
    tap_grads(1)
    small_grads(1, sums)
    core_copy(1).start()
    out_ref[...] = tn(place[...], outq[...]).astype(BF16)
    halo_wait(2)
    assemble(2, gx, qg)
    convolve(qg, wflip, 1)
    step_back(1)
    to_plane(1)
    sums = backward_all(0, cot_rows)
    halo_start(3, gx)
    to_z(1)
    weight_grads(0)
    to_all(1)
    tap_grads(0)
    small_grads(0, sums)
    core_copy(0).start()
    to_sibling(1)
    halo_wait(3)
    assemble(3, gx, qg)
    to_plane(0)
    convolve(qg, wflip, 0)
    step_back(0)
    to_z(0)
    g = grad[...]
    high = g.astype(BF16)
    g = g - high.astype(F32)
    mid = g.astype(BF16)
    low = (g - mid.astype(F32)).astype(BF16)
    gfeat_ref[...] = tn(place[...], high) + (tn(place[...], mid) + tn(place[...], low))
    to_all(0)
    to_sibling(0)
    for n in range(4):
        halo_done(n)
    finish(1)
    finish(0)


def on_device(features, cotangent, dw_kernel, conv_bias, ln_gain, ln_shift, up_weight, up_bias,
              down_weight, down_bias, layer_scale):
    depth = dw_kernel.shape[0]
    pixel_total = PX * lax.axis_size("slide") * lax.axis_size("ty") * lax.axis_size("tx")
    place, edges, spread = (jnp.asarray(v, BF16) for v in one_hots())
    flat = dw_kernel.reshape(depth, TAPS, CH)
    wexp = jnp.stack([flat[..., :LANES], jnp.concatenate([flat[..., LANES:]] * 2, axis=-1)], axis=1)
    wexp = jnp.broadcast_to(wexp[:, :, :, None, :], (depth, 2, TAPS, NS, LANES))
    wflip = wexp[:, :, ::-1]
    vmem = pl.BlockSpec(memory_space=pltpu.VMEM)
    dma = pltpu.SemaphoreType.DMA
    plane = (NI, TC + 6, NS, CH)
    wide = (NI + 6, WIDE, NS, LANES)
    out, gfeat, result = pl.pallas_call(
        functools.partial(kernel, 1.0 / math.sqrt(pixel_total)),
        out_shape=(
            jax.ShapeDtypeStruct((PX, CH), BF16),
            jax.ShapeDtypeStruct((PX, CH), F32),
            jax.ShapeDtypeStruct((depth, 2, CHUNKS, ROWS, LANES), BF16),
        ),
        in_specs=[vmem] * 15,
        out_specs=(vmem,) * 3,
        scratch_shapes=[
            pltpu.VMEM((2, *plane), F32),
            pltpu.VMEM(plane, F32),
            pltpu.VMEM((2, *wide), F32),
            pltpu.VMEM(wide, F32),
            pltpu.VMEM((NI, PACK, NS, LANES), F32),
            pltpu.VMEM((TC * NS, CH), F32),
            pltpu.VMEM((2, PX, CH), F32),
            pltpu.VMEM((2, PX, 1), F32),
            pltpu.VMEM((2, PX, CH), BF16),
            pltpu.VMEM((2, PX, HID), BF16),
            pltpu.VMEM((2, PX, HID), F32),
            pltpu.VMEM((2, PX, CH), F32),
            pltpu.VMEM((PX, CH), BF16),
            pltpu.VMEM((PX, HID), BF16),
            pltpu.VMEM((NI, PACK, NS, LANES), F32),
            pltpu.VMEM((2, 3, TC + 6, NS, CH), F32),
            pltpu.VMEM((2, TAPS, NS, LANES), F32),
            pltpu.VMEM((LANES, LANES), F32),
            pltpu.VMEM((PX, CH), F32),
            pltpu.VMEM((PX, CH), BF16),
            pltpu.VMEM((2, 2, CHUNKS, ROWS, LANES), F32),
            pltpu.VMEM((2, CHUNKS, ROWS, LANES), F32),
            pltpu.VMEM((2, CHUNKS, ROWS, LANES), BF16),
            pltpu.VMEM((2, CHUNKS, ROWS, LANES), BF16),
            pltpu.VMEM((2, NZ, ROWS, LANES), BF16),
            pltpu.VMEM((4, 2, 3, TR, CH), BF16),
            pltpu.VMEM((4, 2, 3, TC, CH), BF16),
            pltpu.VMEM((4, 2, 3, TR, CH), BF16),
            pltpu.VMEM((4, 6, 3, TC, CH), BF16),
            dma((4, 8)), dma((4, 8)),
            dma((2,)), dma((2,)),
            dma((2, CHUNKS)), dma((2, CHUNKS)),
            dma((2, NZ)), dma((2, NZ)),
            dma((2, CHUNKS)), dma((2, CHUNKS)),
            dma((2, CHUNKS)), dma((2, CHUNKS)),
        ],
        compiler_params=pltpu.CompilerParams(
            collective_id=0, has_side_effects=True, vmem_limit_bytes=56 * 2**20
        ),
    )(
        features.reshape(PX, CH), cotangent.reshape(PX, CH), wexp, wflip, conv_bias, ln_gain, ln_shift,
        up_weight, up_bias, down_weight, down_bias, layer_scale, place, edges, spread,
    )
    result = result.reshape(depth, 2 * CHUNKS, ROWS, LANES)
    big = result[:, :, :BIG].reshape(depth, 2, 6, CH, LANES).astype(F32)
    grad_up = big[:, 0].transpose(0, 2, 1, 3).reshape(depth, CH, HID)
    grad_down = big[:, 1].transpose(0, 1, 3, 2).reshape(depth, HID, CH)
    few = result[:, :, BIG:].astype(F32)
    few = (few[:, :, :4] + few[:, :, 4:]).reshape(depth, LANES, LANES)
    grad_taps = jnp.concatenate([few[:, :TAPS], few[:, TAPS : 2 * TAPS, :REST]], axis=-1)

    def vector(at):
        return jnp.concatenate([few[:, at], few[:, at + 1, :REST]], axis=-1)

    return (
        out.reshape(1, TR, TC, CH),
        gfeat.reshape(1, TR, TC, CH),
        grad_taps.reshape(depth, SPAN, SPAN, CH),
        vector(ROW_CBIAS),
        vector(ROW_GAIN),
        vector(ROW_SHIFT),
        grad_up,
        few[:, ROW_UBIAS : ROW_UBIAS + 6].reshape(depth, HID),
        grad_down,
        vector(ROW_DBIAS),
        vector(ROW_SCALE),
    )


def solution(mesh):
    tiled = P("slide", "ty", "tx", None)
    return jax.shard_map(
        on_device,
        mesh=mesh,
        in_specs=(tiled, tiled) + (P(),) * 9,
        out_specs=(tiled, tiled) + (P(),) * 9,
        check_vma=False,
    )
```

```python
import functools
import math

import jax
import jax.numpy as jnp
import numpy as np
from jax import lax
from jax.experimental import pallas as pl
from jax.experimental.pallas import tpu as pltpu
from jax.sharding import PartitionSpec as P

MESH = pl.DeviceIdType.MESH
F32 = jnp.float32
BF16 = jnp.bfloat16
ROOT_HALF = 0.7071067811865476
INV_ROOT_TAU = 0.3989422804014327
EPSILON = 1e-06

TR, TC, CH, HID = 32, 16, 192, 768
PX = TR * TC
NI, NS = 4, 8
MARGIN = 3
SPAN = 7
TAPS = SPAN * SPAN
LANES = 128
REST = CH - LANES
PACK = TC + TC // 2
WIDE = (TC + 2 * MARGIN) + (TC // 2 + 2 * MARGIN)
BIG = 72
ROWS = 80
CHUNKS = 16
NZ = 8
HALOS = ((-1, -1), (-1, 0), (-1, 1), (1, -1), (1, 0), (1, 1), (0, -1), (0, 1))

ROW_CBIAS, ROW_GAIN, ROW_SHIFT, ROW_DBIAS, ROW_SCALE, ROW_UBIAS = 98, 100, 102, 104, 106, 108


def pixel_order():
    q = np.arange(PX)
    return (4 * (q % NS) + q // (TC * NS)) * TC + (q // NS) % TC


def one_hots():
    order = pixel_order()
    place = np.zeros((PX, PX), np.float32)
    place[np.arange(PX), order] = 1.0
    inverse = np.argsort(order)
    edge_rows = np.concatenate([np.arange(3 * TC), np.arange((TR - 3) * TC, TR * TC)])
    edges = np.zeros((6 * TC, PX), np.float32)
    edges[np.arange(6 * TC), inverse[edge_rows]] = 1.0
    spread = np.zeros((2, 3, TC + 6, NS, 3, 3, TC), np.float32)
    for cc in range(TC + 6):
        source, column = (0, TC - 3 + cc) if cc < 3 else (1, cc - 3) if cc < TC + 3 else (2, cc - TC - 3)
        for u in range(3):
            spread[0, u, cc, 0, source, u, column] = 1.0
            spread[1, u, cc, NS - 1, source, u, column] = 1.0
    spread = spread.reshape(2, 3 * (TC + 6) * NS, 9 * TC)
    return place, edges, spread


def tn(a, b):
    return lax.dot_general(a, b, (((0,), (0,)), ((), ())), preferred_element_type=F32)


def nt(a, b):
    return lax.dot_general(a, b, (((1,), (1,)), ((), ())), preferred_element_type=F32)


def nn(a, b):
    return jnp.dot(a, b, preferred_element_type=F32)


def kernel(
    factor,
    feat, cot, dw, cbias, gain, shift, up, ubias, down, dbias, scale, place, edges, spread,
    out_ref, gfeat_ref, result,
    xp, gx, qa, qg, cbuf, conv, unit, inv, normed, act, slope, branch, gbr, gpre, gcp, tq, taps, small,
    grad, outq, wexp, pay, corebuf, sbuf, rbuf, zbuf,
    csend, rsend, crecv, rrecv,
    hs, hr, cs, cr, xs, xr, zs, zr, gs, gr, ls, lr,
):
    yh = lax.axis_index("slide")
    ty = lax.axis_index("ty")
    tx = lax.axis_index("tx")
    core = lax.rem(tx, 2)
    yl = lax.rem(lax.div(tx, 2), 2)
    z = lax.div(tx, 4)
    other = 1 - core
    me = ty * 4 + yh * 2 + yl
    sibling = (yh, ty, z * 4 + yl * 2 + other)

    def plane_peer(d):
        py = lax.rem(ty + lax.div(d, 4), 4)
        ph = lax.rem(yh + lax.rem(lax.div(d, 2), 2), 2)
        pl_ = lax.rem(yl + lax.rem(d, 2), 2)
        return py * 4 + ph * 2 + pl_, (ph, py, z * 4 + pl_ * 2 + core)

    def z_peer(d):
        pz = lax.rem(z + d, NZ)
        return pz, (yh, ty, pz * 4 + yl * 2 + core)

    barrier = pltpu.get_barrier_semaphore()

    def greet(device):
        pl.semaphore_signal(barrier, inc=1, device_id=device, device_id_type=MESH)

    for dy, dx in HALOS:
        greet((yh, lax.rem(ty + dy + 4, 4), lax.rem(tx + dx + 32, 32)))
    greet(sibling)

    @pl.loop(1, CHUNKS)
    def _(d):
        greet(plane_peer(d)[1])

    @pl.loop(1, NZ)
    def _(d):
        greet(z_peer(d)[1])

    def there(dy, dx):
        flags = []
        if dy:
            flags.append(jnp.logical_and(ty + dy >= 0, ty + dy < 4))
        if dx:
            flags.append(jnp.logical_and(tx + dx >= 0, tx + dx < 32))
        return functools.reduce(jnp.logical_and, flags)

    def halo_copy(n, dy, dx):
        if dy == 0:
            slot = 6 if dx > 0 else 7
            src, dst = csend.at[n, 0 if dx < 0 else 1], crecv.at[n, slot - 6]
        else:
            slot = (1 if dy > 0 else 4) - dx
            src, dst = rsend.at[n, 0 if dy < 0 else 1], rrecv.at[n, slot]
        return pltpu.make_async_remote_copy(
            src_ref=src, dst_ref=dst, send_sem=hs.at[n, slot], recv_sem=hr.at[n, slot],
            device_id=(yh, ty + dy, tx + dx), device_id_type=MESH,
        )

    def halo_start(n, plane):
        flat = jnp.concatenate([plane[i, 3 : 3 + TC].reshape(TC * NS, CH) for i in range(NI)], axis=0)
        strips = nn(edges[...], flat.astype(BF16)).astype(BF16)
        rsend[n] = strips.reshape(2, 3, TC, CH)
        for c in range(3):
            csend[n, 0, c] = plane[:, 3 + c].reshape(TR, CH).astype(BF16)
            csend[n, 1, c] = plane[:, TC + c].reshape(TR, CH).astype(BF16)
        if n == 0:
            pl.semaphore_wait(barrier, 8 + 1 + CHUNKS - 1 + NZ - 1)
        for dy, dx in HALOS:

            @pl.when(there(dy, dx))
            def _(dy=dy, dx=dx):
                halo_copy(n, dy, dx).start()

    def halo_wait(n):
        for dy, dx in HALOS:

            @pl.when(there(-dy, -dx))
            def _(dy=dy, dx=dx):
                halo_copy(n, dy, dx).wait_recv()

            @pl.when(jnp.logical_not(there(-dy, -dx)))
            def _(dy=dy, dx=dx):
                if dy == 0:
                    crecv[n, 0 if dx > 0 else 1] = jnp.zeros((3, TR, CH), BF16)
                else:
                    rrecv[n, (1 if dy > 0 else 4) - dx] = jnp.zeros((3, TC, CH), BF16)

    def halo_done(n):
        for dy, dx in HALOS:

            @pl.when(there(dy, dx))
            def _(dy=dy, dx=dx):
                halo_copy(n, dy, dx).wait_send()

    def assemble(n, plane, q):
        for c in range(3):
            plane[:, c] = crecv[n, 0, c].astype(F32).reshape(NI, NS, CH)
            plane[:, TC + 3 + c] = crecv[n, 1, c].astype(F32).reshape(NI, NS, CH)
        for side in range(2):
            strips = jnp.concatenate([rrecv[n, 3 * side + k].reshape(3 * TC, CH) for k in range(3)], axis=0)
            tq[side] = nn(spread[side], strips).reshape(3, TC + 6, NS, CH)
        row = lax.broadcasted_iota(jnp.int32, (3, NS, LANES), 1)

        def fill(slot, mid, top, low):
            q[3:7, slot] = mid
            q[0:3, slot] = jnp.where(row == 0, top, pltpu.roll(mid[1:4], 1, 1))
            q[7:10, slot] = jnp.where(row == NS - 1, low, pltpu.roll(mid[0:3], NS - 1, 1))

        @pl.loop(0, TC + 6)
        def _(cc):
            fill(cc, plane[:, cc, :, :LANES], tq[0, :, cc, :, :LANES], tq[1, :, cc, :, :LANES])

        def pair(ref, *at):
            return jnp.concatenate([ref[(*at[:-1], at[-1], slice(None), slice(LANES, CH))],
                                    ref[(*at[:-1], at[-1] + 8, slice(None), slice(LANES, CH))]], axis=-1)

        @pl.loop(0, TC // 2 + 6)
        def _(k):
            fill(TC + 6 + k, pair(plane, slice(None), k), pair(tq, 0, slice(None), k), pair(tq, 1, slice(None), k))

    def convolve(q, l, flip):
        def columns(part, t, base):
            sums = [[None, None] for _ in range(NI)]
            for j2 in range(SPAN + 1):
                for r in range(NI + SPAN - 1):
                    x = q[r, base + j2]
                    for i in range(NI):
                        if not 0 <= r - i < SPAN:
                            continue
                        for o in range(2):
                            if not 0 <= j2 - o < SPAN:
                                continue
                            tap = (r - i) * SPAN + j2 - o
                            term = x * wexp[l, part, TAPS - 1 - tap if flip else tap]
                            sums[i][o] = term if sums[i][o] is None else sums[i][o] + term
            for i in range(NI):
                for o in range(2):
                    cbuf[i, t + o] = sums[i][o]

        @pl.loop(0, TC // 2)
        def _(k):
            columns(0, 2 * k, 2 * k)

        @pl.loop(0, TC // 4)
        def _(k):
            columns(1, TC + 2 * k, TC + 6 + 2 * k)

    def conv_rows(i):
        half = TC * NS // 2
        conv[:, :LANES] = cbuf[i, :TC].reshape(TC * NS, LANES)
        rest = cbuf[i, TC:].reshape(half, LANES)
        conv[:half, LANES:] = rest[:, :REST]
        conv[half:, LANES:] = rest[:, REST:]
        return conv[...]

    blk = TC * NS

    def rows_of(i):
        return pl.ds(pl.multiple_of(i * blk, blk), blk)

    def forward(l, plane, into, i):
        c = conv_rows(i) + cbias[l : l + 1]
        mid = c - jnp.mean(c, axis=1, keepdims=True)
        rstd = lax.rsqrt(jnp.mean(mid * mid, axis=1, keepdims=True) + EPSILON)
        u = mid * rstd
        rows = rows_of(i)
        unit[l, rows] = u
        inv[l, rows] = rstd
        nb = (u * gain[l : l + 1] + shift[l : l + 1]).astype(BF16)
        normed[l, rows] = nb
        pre = nn(nb, up[l]) + ubias[l : l + 1]
        cdf = 0.5 * (1.0 + lax.erf(pre * ROOT_HALF))
        slope[l, rows] = cdf + pre * INV_ROOT_TAU * jnp.exp(-0.5 * pre * pre)
        ab = (pre * cdf).astype(BF16)
        act[l, rows] = ab
        br = nt(ab, down[l]) + dbias[l : l + 1]
        branch[l, rows] = br
        before = plane[i, 3 : 3 + TC].reshape(blk, CH)
        new = (before + scale[l : l + 1] * br).astype(BF16)
        into(i, new)

    def backward(l, grad_rows, i, sums):
        rows = rows_of(i)
        g = grad_rows(i)
        s_gain, s_shift, s_dbias, s_scale, s_ubias, s_cbias = sums

        def fold(v):
            return jnp.sum(v.reshape(blk // 8, 8, v.shape[1]), axis=0)

        s_scale = s_scale + fold(g * branch[l, rows])
        gb = (g * scale[l : l + 1]).astype(BF16)
        gbr[rows] = gb
        s_dbias = s_dbias + fold(gb.astype(F32))
        gp = (nn(gb, down[l]) * slope[l, rows]).astype(BF16)
        gpre[rows] = gp
        s_ubias = s_ubias + fold(gp.astype(F32))
        gn = nt(gp, up[l])
        u = unit[l, rows]
        gnu = gn * u
        s_gain = s_gain + fold(gnu)
        s_shift = s_shift + fold(gn)
        q = gn * gain[l : l + 1]
        centred = q - jnp.mean(q, axis=1, keepdims=True) - u * jnp.mean(q * u, axis=1, keepdims=True)
        gc = (inv[l, rows] * centred).astype(BF16).astype(F32)
        s_cbias = s_cbias + fold(gc)
        gx[i, 3 : 3 + TC] = gc.reshape(TC, NS, CH)
        gcp[i, :TC] = gc[:, :LANES].reshape(TC, NS, LANES)
        half = blk // 2
        gcp[i, TC:, :, :REST] = gc[:half, LANES:].reshape(TC // 2, NS, REST)
        gcp[i, TC:, :, REST:] = gc[half:, LANES:].reshape(TC // 2, NS, REST)
        return s_gain, s_shift, s_dbias, s_scale, s_ubias, s_cbias

    def backward_all(l, grad_rows):
        zero = jnp.zeros((8, CH), F32)
        start = (zero, zero, zero, zero, jnp.zeros((8, HID), F32), zero)
        return lax.fori_loop(0, NI, lambda i, sums: backward(l, grad_rows, i, sums), start)

    def weight_grads(l):
        for m, (a, b) in enumerate(((normed.at[l], gpre), (gbr, act.at[l]))):
            for t in range(3):
                part = tn(a[...], b[:, 256 * t : 256 * t + 256])
                for v in range(2):
                    for r in range(8):
                        piece = m * 48 + (2 * t + v) * 8 + r
                        chunk, slot = divmod(piece, 3)
                        pay[l, chunk // CHUNKS, chunk % CHUNKS, 24 * slot : 24 * slot + 24] = part[
                            24 * r : 24 * r + 24, LANES * v : LANES * v + LANES
                        ]

    def tap_grads(l):
        for part, (cols, base, first) in enumerate(((TC, 0, 0), (TC // 2, TC + 6, TC))):

            @pl.loop(0, SPAN)
            def _(j):
                def body(c, sums):
                    sums = list(sums)
                    for o in range(2):
                        col = 2 * c + o
                        gcs = [gcp[i, first + col] for i in range(NI)]
                        for r in range(NI + SPAN - 1):
                            x = qa[l, r, base + col + j]
                            for i in range(NI):
                                if 0 <= r - i < SPAN:
                                    sums[r - i] = sums[r - i] + gcs[i] * x
                    return tuple(sums)

                zero = jnp.zeros((NS, LANES), F32)
                sums = lax.fori_loop(0, cols // 2, body, (zero,) * SPAN)
                for r in range(SPAN):
                    taps[part, r * SPAN + j] = sums[r]

    def small_grads(l, sums):
        s_gain, s_shift, s_dbias, s_scale, s_ubias, s_cbias = sums
        small[...] = jnp.zeros((LANES, LANES), F32)
        small[:TAPS] = jnp.sum(taps[0], axis=1)
        rest = jnp.sum(taps[1], axis=1)
        small[TAPS : 2 * TAPS, :REST] = rest[:, :REST] + rest[:, REST:]
        for at, v in ((ROW_CBIAS, s_cbias), (ROW_GAIN, s_gain), (ROW_SHIFT, s_shift),
                      (ROW_DBIAS, s_dbias), (ROW_SCALE, s_scale)):
            v = jnp.sum(v, axis=0, keepdims=True)
            small[at : at + 1] = v[:, :LANES]
            small[at + 1 : at + 2, :REST] = v[:, LANES:]
        v = jnp.sum(s_ubias, axis=0, keepdims=True)
        for t in range(6):
            small[ROW_UBIAS + t : ROW_UBIAS + t + 1] = v[:, LANES * t : LANES * t + LANES]
        upper = lax.broadcasted_iota(jnp.int32, (8, LANES), 0) < 4
        for k in range(2 * CHUNKS):
            v = small[8 * (k // 2) : 8 * (k // 2) + 8]
            if k % 2:
                v = pltpu.roll(v, 4, 0)
            pay[l, k // CHUNKS, k % CHUNKS, BIG:] = jnp.where(upper, v, 0.0)

    upper = lax.broadcasted_iota(jnp.int32, (8, LANES), 0) < 4

    def rounded(v, store):
        s = v[BIG:]
        s = s + pltpu.roll(s, 4, 0)
        high = s.astype(BF16).astype(F32)
        store(jnp.concatenate([v[:BIG], jnp.where(upper, high, s - high)], axis=0).astype(BF16))

    def core_copy(l):
        return pltpu.make_async_remote_copy(
            src_ref=pay.at[l, other], dst_ref=corebuf.at[l], send_sem=cs.at[l], recv_sem=cr.at[l],
            device_id=sibling, device_id_type=MESH,
        )

    def plane_copy(l, d):
        index, device = plane_peer(d)
        return pltpu.make_async_remote_copy(
            src_ref=sbuf.at[l, index], dst_ref=rbuf.at[l, d], send_sem=xs.at[l, d], recv_sem=xr.at[l, d],
            device_id=device, device_id_type=MESH,
        )

    def z_copy(l, d):
        return pltpu.make_async_remote_copy(
            src_ref=zbuf.at[l, z], dst_ref=zbuf.at[l, z], send_sem=zs.at[l, d], recv_sem=zr.at[l, z],
            device_id=z_peer(d)[1], device_id_type=MESH,
        )

    def z_arrival(l, d):
        pz, device = z_peer(d)
        return pltpu.make_async_remote_copy(
            src_ref=zbuf.at[l, pz], dst_ref=zbuf.at[l, pz], send_sem=zs.at[l, d], recv_sem=zr.at[l, pz],
            device_id=device, device_id_type=MESH,
        )

    def gather_copy(l, d):
        return pltpu.make_async_remote_copy(
            src_ref=result.at[l, core, me], dst_ref=result.at[l, core, me], send_sem=gs.at[l, d],
            recv_sem=gr.at[l, me], device_id=plane_peer(d)[1], device_id_type=MESH,
        )

    def gather_arrival(l, d):
        index, device = plane_peer(d)
        return pltpu.make_async_remote_copy(
            src_ref=result.at[l, core, index], dst_ref=result.at[l, core, index], send_sem=gs.at[l, d],
            recv_sem=gr.at[l, index], device_id=device, device_id_type=MESH,
        )

    def relay_copy(l, index):
        return pltpu.make_async_remote_copy(
            src_ref=result.at[l, core, index], dst_ref=result.at[l, core, index], send_sem=ls.at[l, index],
            recv_sem=lr.at[l, index], device_id=sibling, device_id_type=MESH,
        )

    def relay_arrival(l, index):
        return pltpu.make_async_remote_copy(
            src_ref=result.at[l, other, index], dst_ref=result.at[l, other, index], send_sem=ls.at[l, index],
            recv_sem=lr.at[l, index], device_id=sibling, device_id_type=MESH,
        )

    def to_plane(l):
        core_copy(l).wait_recv()

        @pl.loop(0, CHUNKS)
        def _(k):
            d = lax.rem(k + 1, CHUNKS)
            index, _ = plane_peer(d)
            v = pay[l, core, index] + corebuf[l, index]

            def store(r):
                sbuf[l, index] = r

            rounded(v, store)

            @pl.when(d > 0)
            def _():
                plane_copy(l, d).start()

    def to_z(l):
        @pl.loop(1, CHUNKS)
        def _(d):
            plane_copy(l, d).wait_recv()

        v = lax.fori_loop(1, CHUNKS, lambda d, v: v + rbuf[l, d].astype(F32), sbuf[l, me].astype(F32))

        def store(r):
            zbuf[l, z] = r

        rounded(v, store)

        @pl.loop(1, NZ)
        def _(d):
            z_copy(l, d).start()

    def to_all(l):
        @pl.loop(1, NZ)
        def _(d):
            z_arrival(l, d).wait_recv()

        v = zbuf[l, 0].astype(F32)
        for k in range(1, NZ):
            v = v + zbuf[l, k].astype(F32)

        def store(r):
            result[l, core, me] = r

        rounded(v * factor, store)

        @pl.loop(1, CHUNKS)
        def _(d):
            gather_copy(l, d).start()

        relay_copy(l, me).start()

    def to_sibling(l):
        @pl.loop(1, CHUNKS)
        def _(d):
            gather_arrival(l, d).wait_recv()
            relay_copy(l, plane_peer(d)[0]).start()

    def finish(l):
        @pl.loop(0, CHUNKS)
        def _(k):
            relay_arrival(l, k).wait_recv()
            relay_copy(l, k).wait_send()

        core_copy(l).wait_send()

        @pl.loop(1, CHUNKS)
        def _(d):
            plane_copy(l, d).wait_send()
            gather_copy(l, d).wait_send()

        @pl.loop(1, NZ)
        def _(d):
            z_copy(l, d).wait_send()

    def flat_rows(plane, i):
        return plane[i, 3 : 3 + TC].reshape(blk, CH)

    def cot_rows(i):
        return grad[rows_of(i)]

    def step_back(l):
        @pl.loop(0, NI)
        def _(i):
            rows = rows_of(i)
            grad[rows] = grad[rows] + conv_rows(i)

    xp[0, :, 3 : 3 + TC] = nn(place[...], feat[...]).reshape(NI, TC, NS, CH)
    halo_start(0, xp.at[0])
    grad[...] = nn(place[...], cot[...])

    @pl.loop(0, TAPS)
    def _(t):
        for l in range(2):
            tap = dw[t, l : l + 1]
            rest = tap[:, LANES:]
            wexp[l, 0, t] = jnp.broadcast_to(tap[:, :LANES], (NS, LANES))
            wexp[l, 1, t] = jnp.broadcast_to(jnp.concatenate([rest, rest], axis=1), (NS, LANES))

    halo_wait(0)
    assemble(0, xp.at[0], qa.at[0])
    convolve(qa.at[0], 0, False)

    def keep(i, new):
        xp[1, i, 3 : 3 + TC] = new.astype(F32).reshape(TC, NS, CH)

    @pl.loop(0, NI)
    def _(i):
        forward(0, xp.at[0], keep, i)

    halo_start(1, xp.at[1])
    halo_wait(1)
    assemble(1, xp.at[1], qa.at[1])
    convolve(qa.at[1], 1, False)

    def keep_out(i, new):
        outq[rows_of(i)] = new

    @pl.loop(0, NI)
    def _(i):
        forward(1, xp.at[1], keep_out, i)

    sums = backward_all(1, cot_rows)
    halo_start(2, gx)
    weight_grads(1)
    tap_grads(1)
    small_grads(1, sums)
    core_copy(1).start()
    out_ref[...] = tn(place[...], outq[...]).astype(BF16)
    halo_wait(2)
    assemble(2, gx, qg)
    convolve(qg, 1, True)
    step_back(1)
    to_plane(1)
    sums = backward_all(0, cot_rows)
    halo_start(3, gx)
    to_z(1)
    weight_grads(0)
    to_all(1)
    tap_grads(0)
    small_grads(0, sums)
    core_copy(0).start()
    to_sibling(1)
    halo_wait(3)
    assemble(3, gx, qg)
    to_plane(0)
    convolve(qg, 0, True)
    step_back(0)
    to_z(0)
    g = grad[...]
    high = g.astype(BF16)
    g = g - high.astype(F32)
    mid = g.astype(BF16)
    low = (g - mid.astype(F32)).astype(BF16)
    gfeat_ref[...] = tn(place[...], high) + (tn(place[...], mid) + tn(place[...], low))
    to_all(0)
    to_sibling(0)
    for n in range(4):
        halo_done(n)
    finish(1)
    finish(0)


def unpack(out_in, gfeat_in, result, out, gfeat, gtaps, gcbias, ggain, gshift, gup, gubias, gdown, gdbias, gscale, few):
    out[...] = out_in[...]
    gfeat[...] = gfeat_in[...]
    upper = lax.broadcasted_iota(jnp.int32, (8, LANES), 0) < 4
    for l in range(2):
        for piece in range(96):
            chunk, slot = divmod(piece, 3)
            m, piece = divmod(piece, 48)
            t, r = divmod(piece, 8)
            value = result[l, chunk // CHUNKS, chunk % CHUNKS, 24 * slot : 24 * slot + 24].astype(F32)
            (gup, gdown)[m][l, 24 * r : 24 * r + 24, LANES * t : LANES * t + LANES] = value
        for k in range(CHUNKS):
            pair = []
            for chunk in (2 * k, 2 * k + 1):
                v = result[l, chunk // CHUNKS, chunk % CHUNKS, BIG:].astype(F32)
                pair.append(v + pltpu.roll(v, 4, 0))
            few[8 * k : 8 * k + 8] = jnp.where(upper, pair[0], pair[1])
        for t in range(TAPS):
            gtaps[t, l : l + 1, :LANES] = few[t : t + 1]
            gtaps[t, l : l + 1, LANES:] = few[TAPS + t : TAPS + t + 1, :REST]
        for at, ref in ((ROW_CBIAS, gcbias), (ROW_GAIN, ggain), (ROW_SHIFT, gshift),
                        (ROW_DBIAS, gdbias), (ROW_SCALE, gscale)):
            ref[l : l + 1, :LANES] = few[at : at + 1]
            ref[l : l + 1, LANES:] = few[at + 1 : at + 2, :REST]
        for t in range(6):
            gubias[l : l + 1, LANES * t : LANES * t + LANES] = few[ROW_UBIAS + t : ROW_UBIAS + t + 1]


def on_device(features, cotangent, dw_kernel, conv_bias, ln_gain, ln_shift, up_weight, up_bias,
              down_weight, down_bias, layer_scale):
    depth = dw_kernel.shape[0]
    pixel_total = PX * lax.axis_size("slide") * lax.axis_size("ty") * lax.axis_size("tx")
    place, edges, spread = (jnp.asarray(v, BF16) for v in one_hots())
    taps = dw_kernel.reshape(depth, TAPS, CH).transpose(1, 0, 2)
    vmem = pl.BlockSpec(memory_space=pltpu.VMEM)
    dma = pltpu.SemaphoreType.DMA
    plane = (NI, TC + 6, NS, CH)
    wide = (NI + 6, WIDE, NS, LANES)
    out, gfeat, result = pl.pallas_call(
        functools.partial(kernel, 1.0 / math.sqrt(pixel_total)),
        out_shape=(
            jax.ShapeDtypeStruct((PX, CH), BF16),
            jax.ShapeDtypeStruct((PX, CH), F32),
            jax.ShapeDtypeStruct((depth, 2, CHUNKS, ROWS, LANES), BF16),
        ),
        in_specs=[vmem] * 14,
        out_specs=(vmem,) * 3,
        scratch_shapes=[
            pltpu.VMEM((2, *plane), F32),
            pltpu.VMEM(plane, F32),
            pltpu.VMEM((2, *wide), F32),
            pltpu.VMEM(wide, F32),
            pltpu.VMEM((NI, PACK, NS, LANES), F32),
            pltpu.VMEM((TC * NS, CH), F32),
            pltpu.VMEM((2, PX, CH), F32),
            pltpu.VMEM((2, PX, 1), F32),
            pltpu.VMEM((2, PX, CH), BF16),
            pltpu.VMEM((2, PX, HID), BF16),
            pltpu.VMEM((2, PX, HID), F32),
            pltpu.VMEM((2, PX, CH), F32),
            pltpu.VMEM((PX, CH), BF16),
            pltpu.VMEM((PX, HID), BF16),
            pltpu.VMEM((NI, PACK, NS, LANES), F32),
            pltpu.VMEM((2, 3, TC + 6, NS, CH), F32),
            pltpu.VMEM((2, TAPS, NS, LANES), F32),
            pltpu.VMEM((LANES, LANES), F32),
            pltpu.VMEM((PX, CH), F32),
            pltpu.VMEM((PX, CH), BF16),
            pltpu.VMEM((2, 2, TAPS, NS, LANES), F32),
            pltpu.VMEM((2, 2, CHUNKS, ROWS, LANES), F32),
            pltpu.VMEM((2, CHUNKS, ROWS, LANES), F32),
            pltpu.VMEM((2, CHUNKS, ROWS, LANES), BF16),
            pltpu.VMEM((2, CHUNKS, ROWS, LANES), BF16),
            pltpu.VMEM((2, NZ, ROWS, LANES), BF16),
            pltpu.VMEM((4, 2, 3, TR, CH), BF16),
            pltpu.VMEM((4, 2, 3, TC, CH), BF16),
            pltpu.VMEM((4, 2, 3, TR, CH), BF16),
            pltpu.VMEM((4, 6, 3, TC, CH), BF16),
            dma((4, 8)), dma((4, 8)),
            dma((2,)), dma((2,)),
            dma((2, CHUNKS)), dma((2, CHUNKS)),
            dma((2, NZ)), dma((2, NZ)),
            dma((2, CHUNKS)), dma((2, CHUNKS)),
            dma((2, CHUNKS)), dma((2, CHUNKS)),
        ],
        compiler_params=pltpu.CompilerParams(
            collective_id=0, has_side_effects=True, vmem_limit_bytes=56 * 2**20
        ),
    )(
        features.reshape(PX, CH), cotangent.reshape(PX, CH), taps, conv_bias, ln_gain, ln_shift,
        up_weight, up_bias, down_weight.transpose(0, 2, 1), down_bias, layer_scale, place, edges, spread,
    )
    vector = jax.ShapeDtypeStruct((depth, CH), F32)
    weight = jax.ShapeDtypeStruct((depth, CH, HID), F32)
    out, gfeat, gtaps, gcbias, ggain, gshift, gup, gubias, gdown, gdbias, gscale = pl.pallas_call(
        unpack,
        out_shape=(
            jax.ShapeDtypeStruct((PX, CH), BF16),
            jax.ShapeDtypeStruct((PX, CH), F32),
            jax.ShapeDtypeStruct((TAPS, depth, CH), F32),
            vector, vector, vector, weight, jax.ShapeDtypeStruct((depth, HID), F32), weight, vector, vector,
        ),
        in_specs=[vmem] * 3,
        out_specs=(vmem,) * 11,
        scratch_shapes=[pltpu.VMEM((LANES, LANES), F32)],
        compiler_params=pltpu.CompilerParams(vmem_limit_bytes=24 * 2**20),
    )(out, gfeat, result)
    return (
        out.reshape(1, TR, TC, CH),
        gfeat.reshape(1, TR, TC, CH),
        gtaps.transpose(1, 0, 2).reshape(depth, SPAN, SPAN, CH),
        gcbias,
        ggain,
        gshift,
        gup,
        gubias,
        gdown.transpose(0, 2, 1),
        gdbias,
        gscale,
    )


def solution(mesh):
    tiled = P("slide", "ty", "tx", None)
    return jax.shard_map(
        on_device,
        mesh=mesh,
        in_specs=(tiled, tiled) + (P(),) * 9,
        out_specs=(tiled, tiled) + (P(),) * 9,
        check_vma=False,
    )
```

```python
import functools
import math

import jax
import jax.numpy as jnp
import numpy as np
from jax import lax
from jax.experimental import pallas as pl
from jax.experimental.pallas import tpu as pltpu
from jax.sharding import PartitionSpec as P

MESH = pl.DeviceIdType.MESH
F32 = jnp.float32
BF16 = jnp.bfloat16
ROOT_HALF = 0.7071067811865476
INV_ROOT_TAU = 0.3989422804014327
EPSILON = 1e-06

TR, TC, CH, HID = 32, 16, 192, 768
PX = TR * TC
NI, NS = 4, 8
MARGIN = 3
SPAN = 7
TAPS = SPAN * SPAN
LANES = 128
REST = CH - LANES
PACK = TC + TC // 2
WIDE = (TC + 2 * MARGIN) + (TC // 2 + 2 * MARGIN)
PARTS = (32, 48)
DTILES = 128
SMALL_AT = 40
CHUNKS = 16
NZ = 8
HALOS = ((-1, -1), (-1, 0), (-1, 1), (1, -1), (1, 0), (1, 1), (0, -1), (0, 1))

ROW_CBIAS, ROW_GAIN, ROW_SHIFT, ROW_DBIAS, ROW_SCALE, ROW_UBIAS = 98, 100, 102, 104, 106, 108


def pixel_order():
    q = np.arange(PX)
    return (4 * (q % NS) + q // (TC * NS)) * TC + (q // NS) % TC


def one_hots():
    order = pixel_order()
    place = np.zeros((PX, PX), np.float32)
    place[np.arange(PX), order] = 1.0
    inverse = np.argsort(order)
    edge_rows = np.concatenate([np.arange(3 * TC), np.arange((TR - 3) * TC, TR * TC)])
    edges = np.zeros((6 * TC, PX), np.float32)
    edges[np.arange(6 * TC), inverse[edge_rows]] = 1.0
    spread = np.zeros((2, 3, TC + 6, NS, 3, 3, TC), np.float32)
    for cc in range(TC + 6):
        source, column = (0, TC - 3 + cc) if cc < 3 else (1, cc - 3) if cc < TC + 3 else (2, cc - TC - 3)
        for u in range(3):
            spread[0, u, cc, 0, source, u, column] = 1.0
            spread[1, u, cc, NS - 1, source, u, column] = 1.0
    spread = spread.reshape(2, 3 * (TC + 6) * NS, 9 * TC)
    return place, edges, spread


def tn(a, b):
    return lax.dot_general(a, b, (((0,), (0,)), ((), ())), preferred_element_type=F32)


def nt(a, b):
    return lax.dot_general(a, b, (((1,), (1,)), ((), ())), preferred_element_type=F32)


def nn(a, b):
    return jnp.dot(a, b, preferred_element_type=F32)


def kernel(
    factor,
    feat_in, cot_in, dw_in, cbias, gain, shift, up_in, ubias, down_in, dbias, scale, place_in, edges_in, spread_in,
    out_to, gfeat_to, result0_to, result1_to,
    feat, cot, dw, up, down, place, edges, spread, out_ref, gfeat_ref, result0, result1, ins, outs,
    xp, gx, qa, qg, cbuf, conv, unit, inv, normed, act, slope, branch, gbr, gpre, gcp, tq, taps, small,
    grad, outq, wexp,
    pay0, pay1, core0, core1, sbuf0, sbuf1, rbuf0, rbuf1, zbuf0, zbuf1,
    csend, rsend, crecv, rrecv,
    hs, hr, cs, cr, xs, xr, zs, zr, gs, gr, ls, lr,
):
    yh = lax.axis_index("slide")
    ty = lax.axis_index("ty")
    tx = lax.axis_index("tx")
    core = lax.rem(tx, 2)
    yl = lax.rem(lax.div(tx, 2), 2)
    z = lax.div(tx, 4)
    other = 1 - core
    me = ty * 4 + yh * 2 + yl
    sibling = (yh, ty, z * 4 + yl * 2 + other)

    def plane_peer(d):
        py = lax.rem(ty + lax.div(d, 4), 4)
        ph = lax.rem(yh + lax.rem(lax.div(d, 2), 2), 2)
        pl_ = lax.rem(yl + lax.rem(d, 2), 2)
        return py * 4 + ph * 2 + pl_, (ph, py, z * 4 + pl_ * 2 + core)

    def z_peer(d):
        pz = lax.rem(z + d, NZ)
        return pz, (yh, ty, pz * 4 + yl * 2 + core)

    barrier = pltpu.get_barrier_semaphore()

    def greet(device):
        pl.semaphore_signal(barrier, inc=1, device_id=device, device_id_type=MESH)

    for dy, dx in HALOS:
        greet((yh, lax.rem(ty + dy + 4, 4), lax.rem(tx + dx + 32, 32)))
    greet(sibling)

    @pl.loop(1, CHUNKS)
    def _(d):
        greet(plane_peer(d)[1])

    @pl.loop(1, NZ)
    def _(d):
        greet(z_peer(d)[1])

    arrivals = {}
    loads = ((feat_in, feat), (place_in, place), (edges_in, edges), (cot_in, cot), (dw_in, dw), (spread_in, spread),
             (up_in, up), (down_in, down))
    for k, (src, dst) in enumerate(loads):
        arrivals[id(dst)] = pltpu.make_async_copy(src, dst, ins.at[k])
        arrivals[id(dst)].start()

    def ready(*refs):
        for ref in refs:
            arrivals[id(ref)].wait()

    def leave(k, src, dst):
        return pltpu.make_async_copy(src, dst, outs.at[k])

    def there(dy, dx):
        flags = []
        if dy:
            flags.append(jnp.logical_and(ty + dy >= 0, ty + dy < 4))
        if dx:
            flags.append(jnp.logical_and(tx + dx >= 0, tx + dx < 32))
        return functools.reduce(jnp.logical_and, flags)

    def halo_copy(n, dy, dx):
        if dy == 0:
            slot = 6 if dx > 0 else 7
            src, dst = csend.at[n, 0 if dx < 0 else 1], crecv.at[n, slot - 6]
        else:
            slot = (1 if dy > 0 else 4) - dx
            src, dst = rsend.at[n, 0 if dy < 0 else 1], rrecv.at[n, slot]
        return pltpu.make_async_remote_copy(
            src_ref=src, dst_ref=dst, send_sem=hs.at[n, slot], recv_sem=hr.at[n, slot],
            device_id=(yh, ty + dy, tx + dx), device_id_type=MESH,
        )

    def halo_start(n, plane):
        flat = jnp.concatenate([plane[i, 3 : 3 + TC].reshape(TC * NS, CH) for i in range(NI)], axis=0)
        strips = nn(edges[...], flat.astype(BF16)).astype(BF16)
        rsend[n] = strips.reshape(2, 3, TC, CH)
        for c in range(3):
            csend[n, 0, c] = plane[:, 3 + c].reshape(TR, CH).astype(BF16)
            csend[n, 1, c] = plane[:, TC + c].reshape(TR, CH).astype(BF16)
        if n == 0:
            pl.semaphore_wait(barrier, 8 + 1 + CHUNKS - 1 + NZ - 1)
        for dy, dx in HALOS:

            @pl.when(there(dy, dx))
            def _(dy=dy, dx=dx):
                halo_copy(n, dy, dx).start()

    def halo_wait(n):
        for dy, dx in HALOS:

            @pl.when(there(-dy, -dx))
            def _(dy=dy, dx=dx):
                halo_copy(n, dy, dx).wait_recv()

            @pl.when(jnp.logical_not(there(-dy, -dx)))
            def _(dy=dy, dx=dx):
                if dy == 0:
                    crecv[n, 0 if dx > 0 else 1] = jnp.zeros((3, TR, CH), BF16)
                else:
                    rrecv[n, (1 if dy > 0 else 4) - dx] = jnp.zeros((3, TC, CH), BF16)

    def halo_done(n):
        for dy, dx in HALOS:

            @pl.when(there(dy, dx))
            def _(dy=dy, dx=dx):
                halo_copy(n, dy, dx).wait_send()

    def assemble(n, plane, q):
        for c in range(3):
            plane[:, c] = crecv[n, 0, c].astype(F32).reshape(NI, NS, CH)
            plane[:, TC + 3 + c] = crecv[n, 1, c].astype(F32).reshape(NI, NS, CH)
        for side in range(2):
            strips = jnp.concatenate([rrecv[n, 3 * side + k].reshape(3 * TC, CH) for k in range(3)], axis=0)
            tq[side] = nn(spread[side], strips).reshape(3, TC + 6, NS, CH)
        row = lax.broadcasted_iota(jnp.int32, (3, NS, LANES), 1)

        def fill(slot, mid, top, low):
            q[3:7, slot] = mid
            q[0:3, slot] = jnp.where(row == 0, top, pltpu.roll(mid[1:4], 1, 1))
            q[7:10, slot] = jnp.where(row == NS - 1, low, pltpu.roll(mid[0:3], NS - 1, 1))

        @pl.loop(0, TC + 6)
        def _(cc):
            fill(cc, plane[:, cc, :, :LANES], tq[0, :, cc, :, :LANES], tq[1, :, cc, :, :LANES])

        def pair(ref, *at):
            return jnp.concatenate([ref[(*at[:-1], at[-1], slice(None), slice(LANES, CH))],
                                    ref[(*at[:-1], at[-1] + 8, slice(None), slice(LANES, CH))]], axis=-1)

        @pl.loop(0, TC // 2 + 6)
        def _(k):
            fill(TC + 6 + k, pair(plane, slice(None), k), pair(tq, 0, slice(None), k), pair(tq, 1, slice(None), k))

    def convolve(q, l, flip):
        def columns(part, t, base):
            sums = [[None, None] for _ in range(NI)]
            for j2 in range(SPAN + 1):
                for r in range(NI + SPAN - 1):
                    x = q[r, base + j2]
                    for i in range(NI):
                        if not 0 <= r - i < SPAN:
                            continue
                        for o in range(2):
                            if not 0 <= j2 - o < SPAN:
                                continue
                            tap = (r - i) * SPAN + j2 - o
                            term = x * wexp[l, part, TAPS - 1 - tap if flip else tap]
                            sums[i][o] = term if sums[i][o] is None else sums[i][o] + term
            for i in range(NI):
                for o in range(2):
                    cbuf[i, t + o] = sums[i][o]

        @pl.loop(0, TC // 2)
        def _(k):
            columns(0, 2 * k, 2 * k)

        @pl.loop(0, TC // 4)
        def _(k):
            columns(1, TC + 2 * k, TC + 6 + 2 * k)

    def conv_rows(i):
        half = TC * NS // 2
        conv[:, :LANES] = cbuf[i, :TC].reshape(TC * NS, LANES)
        rest = cbuf[i, TC:].reshape(half, LANES)
        conv[:half, LANES:] = rest[:, :REST]
        conv[half:, LANES:] = rest[:, REST:]
        return conv[...]

    blk = TC * NS

    def rows_of(i):
        return pl.ds(pl.multiple_of(i * blk, blk), blk)

    def forward(l, plane, into, i):
        c = conv_rows(i) + cbias[l : l + 1]
        mid = c - jnp.mean(c, axis=1, keepdims=True)
        rstd = lax.rsqrt(jnp.mean(mid * mid, axis=1, keepdims=True) + EPSILON)
        u = mid * rstd
        rows = rows_of(i)
        unit[l, rows] = u
        inv[l, rows] = rstd
        nb = (u * gain[l : l + 1] + shift[l : l + 1]).astype(BF16)
        normed[l, rows] = nb
        pre = nn(nb, up[l]) + ubias[l : l + 1]
        cdf = 0.5 * (1.0 + lax.erf(pre * ROOT_HALF))
        slope[l, rows] = cdf + pre * INV_ROOT_TAU * jnp.exp(-0.5 * pre * pre)
        ab = (pre * cdf).astype(BF16)
        act[l, rows] = ab
        br = nt(ab, down[l]) + dbias[l : l + 1]
        branch[l, rows] = br
        before = plane[i, 3 : 3 + TC].reshape(blk, CH)
        new = (before + scale[l : l + 1] * br).astype(BF16)
        into(i, new)

    def fold(v):
        return jnp.sum(v.reshape(blk // 8, 8, v.shape[1]), axis=0)

    def branch_grads(l):
        def body(i, sums):
            rows = rows_of(i)
            g = grad[rows]
            gb = (g * scale[l : l + 1]).astype(BF16)
            gbr[rows] = gb
            return sums[0] + fold(gb.astype(F32)), sums[1] + fold(g * branch[l, rows])

        return lax.fori_loop(0, NI, body, (jnp.zeros((8, CH), F32),) * 2)

    def backward(l):
        def body(i, sums):
            rows = rows_of(i)
            s_gain, s_shift, s_ubias, s_cbias = sums
            gp = (nn(gbr[rows], down[l]) * slope[l, rows]).astype(BF16)
            gpre[rows] = gp
            s_ubias = s_ubias + fold(gp.astype(F32))
            gn = nt(gp, up[l])
            u = unit[l, rows]
            s_gain = s_gain + fold(gn * u)
            s_shift = s_shift + fold(gn)
            q = gn * gain[l : l + 1]
            centred = q - jnp.mean(q, axis=1, keepdims=True) - u * jnp.mean(q * u, axis=1, keepdims=True)
            gc = (inv[l, rows] * centred).astype(BF16).astype(F32)
            s_cbias = s_cbias + fold(gc)
            gx[i, 3 : 3 + TC] = gc.reshape(TC, NS, CH)
            gcp[i, :TC] = gc[:, :LANES].reshape(TC, NS, LANES)
            half = blk // 2
            gcp[i, TC:, :, :REST] = gc[:half, LANES:].reshape(TC // 2, NS, REST)
            gcp[i, TC:, :, REST:] = gc[half:, LANES:].reshape(TC // 2, NS, REST)
            return s_gain, s_shift, s_ubias, s_cbias

        zero = jnp.zeros((8, CH), F32)
        return lax.fori_loop(0, NI, body, (zero, zero, jnp.zeros((8, HID), F32), zero))

    def put(l, index, tile, tiles, pay):
        chunk, slot = divmod(index, tiles)
        pay[l, chunk // CHUNKS, chunk % CHUNKS, 8 * slot : 8 * slot + 8] = tile

    def weight_tiles(a, b, store):
        for t in range(3):
            part = tn(a[...], b[:, 256 * t : 256 * t + 256])
            for v in range(2):
                for r in range(CH // 8):
                    store((2 * t + v) * (CH // 8) + r, part[8 * r : 8 * r + 8, LANES * v : LANES * v + LANES])

    def down_grads(l):
        def store(index, tile):
            if index < DTILES:
                put(l, index, tile, 4, pay0)
            else:
                put(l, index + CH // 8 * 6 - DTILES, tile, 5, pay1)

        weight_tiles(gbr, act.at[l], store)

    def up_grads(l):
        weight_tiles(normed.at[l], gpre, lambda index, tile: put(l, index, tile, 5, pay1))

    def tap_grads(l):
        for part, (cols, base, first) in enumerate(((TC, 0, 0), (TC // 2, TC + 6, TC))):

            @pl.loop(0, SPAN)
            def _(j):
                def body(c, sums):
                    sums = list(sums)
                    for o in range(2):
                        col = 2 * c + o
                        gcs = [gcp[i, first + col] for i in range(NI)]
                        for r in range(NI + SPAN - 1):
                            x = qa[l, r, base + col + j]
                            for i in range(NI):
                                if 0 <= r - i < SPAN:
                                    sums[r - i] = sums[r - i] + gcs[i] * x
                    return tuple(sums)

                zero = jnp.zeros((NS, LANES), F32)
                sums = lax.fori_loop(0, cols // 2, body, (zero,) * SPAN)
                for r in range(SPAN):
                    taps[part, r * SPAN + j] = sums[r]

    def small_grads(l, early, sums):
        s_dbias, s_scale = early
        s_gain, s_shift, s_ubias, s_cbias = sums
        small[...] = jnp.zeros((LANES, LANES), F32)
        small[:TAPS] = jnp.sum(taps[0], axis=1)
        rest = jnp.sum(taps[1], axis=1)
        small[TAPS : 2 * TAPS, :REST] = rest[:, :REST] + rest[:, REST:]
        for at, v in ((ROW_CBIAS, s_cbias), (ROW_GAIN, s_gain), (ROW_SHIFT, s_shift),
                      (ROW_DBIAS, s_dbias), (ROW_SCALE, s_scale)):
            v = jnp.sum(v, axis=0, keepdims=True)
            small[at : at + 1] = v[:, :LANES]
            small[at + 1 : at + 2, :REST] = v[:, LANES:]
        v = jnp.sum(s_ubias, axis=0, keepdims=True)
        for t in range(6):
            small[ROW_UBIAS + t : ROW_UBIAS + t + 1] = v[:, LANES * t : LANES * t + LANES]
        upper = lax.broadcasted_iota(jnp.int32, (8, LANES), 0) < 4
        for k in range(2 * CHUNKS):
            v = small[8 * (k // 2) : 8 * (k // 2) + 8]
            if k % 2:
                v = pltpu.roll(v, 4, 0)
            pay1[l, k // CHUNKS, k % CHUNKS, SMALL_AT:] = jnp.where(upper, v, 0.0)

    upper = lax.broadcasted_iota(jnp.int32, (8, LANES), 0) < 4

    def rounded(v, part):
        if part == 0:
            return v.astype(BF16)
        s = v[SMALL_AT:]
        s = s + pltpu.roll(s, 4, 0)
        high = s.astype(BF16).astype(F32)
        return jnp.concatenate([v[:SMALL_AT], jnp.where(upper, high, s - high)], axis=0).astype(BF16)

    pays, cores, sbufs, rbufs, zbufs = (pay0, pay1), (core0, core1), (sbuf0, sbuf1), (rbuf0, rbuf1), (zbuf0, zbuf1)
    results = (result0, result1)

    def core_copy(l, p):
        return pltpu.make_async_remote_copy(
            src_ref=pays[p].at[l, other], dst_ref=cores[p].at[l], send_sem=cs.at[2 * l + p], recv_sem=cr.at[2 * l + p],
            device_id=sibling, device_id_type=MESH,
        )

    def plane_copy(l, p, d):
        index, device = plane_peer(d)
        return pltpu.make_async_remote_copy(
            src_ref=sbufs[p].at[l, index], dst_ref=rbufs[p].at[l, d], send_sem=xs.at[2 * l + p, d], recv_sem=xr.at[2 * l + p, d],
            device_id=device, device_id_type=MESH,
        )

    def z_copy(l, p, d):
        return pltpu.make_async_remote_copy(
            src_ref=zbufs[p].at[l, z], dst_ref=zbufs[p].at[l, z], send_sem=zs.at[2 * l + p, d], recv_sem=zr.at[2 * l + p, z],
            device_id=z_peer(d)[1], device_id_type=MESH,
        )

    def z_arrival(l, p, d):
        pz, device = z_peer(d)
        return pltpu.make_async_remote_copy(
            src_ref=zbufs[p].at[l, pz], dst_ref=zbufs[p].at[l, pz], send_sem=zs.at[2 * l + p, d], recv_sem=zr.at[2 * l + p, pz],
            device_id=device, device_id_type=MESH,
        )

    def gather_copy(l, p, d):
        return pltpu.make_async_remote_copy(
            src_ref=results[p].at[l, core, me], dst_ref=results[p].at[l, core, me], send_sem=gs.at[2 * l + p, d],
            recv_sem=gr.at[2 * l + p, me], device_id=plane_peer(d)[1], device_id_type=MESH,
        )

    def gather_arrival(l, p, d):
        index, device = plane_peer(d)
        return pltpu.make_async_remote_copy(
            src_ref=results[p].at[l, core, index], dst_ref=results[p].at[l, core, index], send_sem=gs.at[2 * l + p, d],
            recv_sem=gr.at[2 * l + p, index], device_id=device, device_id_type=MESH,
        )

    def relay_copy(l, p, index):
        return pltpu.make_async_remote_copy(
            src_ref=results[p].at[l, core, index], dst_ref=results[p].at[l, core, index], send_sem=ls.at[2 * l + p, index],
            recv_sem=lr.at[2 * l + p, index], device_id=sibling, device_id_type=MESH,
        )

    def relay_arrival(l, p, index):
        return pltpu.make_async_remote_copy(
            src_ref=results[p].at[l, other, index], dst_ref=results[p].at[l, other, index], send_sem=ls.at[2 * l + p, index],
            recv_sem=lr.at[2 * l + p, index], device_id=sibling, device_id_type=MESH,
        )

    def to_plane(l, p):
        core_copy(l, p).wait_recv()

        @pl.loop(0, CHUNKS)
        def _(k):
            d = lax.rem(k + 1, CHUNKS)
            index, _ = plane_peer(d)
            v = pays[p][l, core, index] + cores[p][l, index]
            sbufs[p][l, index] = rounded(v, p)

            @pl.when(d > 0)
            def _():
                plane_copy(l, p, d).start()

    def to_z(l, p):
        @pl.loop(1, CHUNKS)
        def _(d):
            plane_copy(l, p, d).wait_recv()

        v = lax.fori_loop(1, CHUNKS, lambda d, v: v + rbufs[p][l, d].astype(F32), sbufs[p][l, me].astype(F32))
        zbufs[p][l, z] = rounded(v, p)

        @pl.loop(1, NZ)
        def _(d):
            z_copy(l, p, d).start()

    def to_all(l, p):
        @pl.loop(1, NZ)
        def _(d):
            z_arrival(l, p, d).wait_recv()

        v = zbufs[p][l, 0].astype(F32)
        for k in range(1, NZ):
            v = v + zbufs[p][l, k].astype(F32)
        results[p][l, core, me] = rounded(v * factor, p)

        @pl.loop(1, CHUNKS)
        def _(d):
            gather_copy(l, p, d).start()

        relay_copy(l, p, me).start()

    def to_sibling(l, p):
        @pl.loop(1, CHUNKS)
        def _(d):
            gather_arrival(l, p, d).wait_recv()
            relay_copy(l, p, plane_peer(d)[0]).start()

    def finish(l, p):
        @pl.loop(0, CHUNKS)
        def _(k):
            relay_arrival(l, p, k).wait_recv()
            relay_copy(l, p, k).wait_send()

        core_copy(l, p).wait_send()

        @pl.loop(1, CHUNKS)
        def _(d):
            plane_copy(l, p, d).wait_send()
            gather_copy(l, p, d).wait_send()

        @pl.loop(1, NZ)
        def _(d):
            z_copy(l, p, d).wait_send()


    def flat_rows(plane, i):
        return plane[i, 3 : 3 + TC].reshape(blk, CH)

    def step_back(l):
        @pl.loop(0, NI)
        def _(i):
            rows = rows_of(i)
            grad[rows] = grad[rows] + conv_rows(i)

    ready(feat, place, edges)
    xp[0, :, 3 : 3 + TC] = nn(place[...], feat[...]).reshape(NI, TC, NS, CH)
    halo_start(0, xp.at[0])
    ready(cot, dw, spread)
    grad[...] = nn(place[...], cot[...])

    @pl.loop(0, TAPS)
    def _(t):
        for l in range(2):
            tap = dw[t, l : l + 1]
            rest = tap[:, LANES:]
            wexp[l, 0, t] = jnp.broadcast_to(tap[:, :LANES], (NS, LANES))
            wexp[l, 1, t] = jnp.broadcast_to(jnp.concatenate([rest, rest], axis=1), (NS, LANES))

    halo_wait(0)
    assemble(0, xp.at[0], qa.at[0])
    convolve(qa.at[0], 0, False)
    ready(up, down)

    def keep(i, new):
        xp[1, i, 3 : 3 + TC] = new.astype(F32).reshape(TC, NS, CH)

    @pl.loop(0, NI)
    def _(i):
        forward(0, xp.at[0], keep, i)

    halo_start(1, xp.at[1])
    halo_wait(1)
    assemble(1, xp.at[1], qa.at[1])
    convolve(qa.at[1], 1, False)

    def keep_out(i, new):
        outq[rows_of(i)] = new

    @pl.loop(0, NI)
    def _(i):
        forward(1, xp.at[1], keep_out, i)

    early = branch_grads(1)
    down_grads(1)
    core_copy(1, 0).start()
    sums = backward(1)
    halo_start(2, gx)
    to_plane(1, 0)
    up_grads(1)
    tap_grads(1)
    small_grads(1, early, sums)
    core_copy(1, 1).start()
    halo_wait(2)
    assemble(2, gx, qg)
    to_z(1, 0)
    to_plane(1, 1)
    convolve(qg, 1, True)
    step_back(1)
    early = branch_grads(0)
    down_grads(0)
    core_copy(0, 0).start()
    to_all(1, 0)
    to_z(1, 1)
    sums = backward(0)
    halo_start(3, gx)
    to_plane(0, 0)
    up_grads(0)
    to_sibling(1, 0)
    tap_grads(0)
    small_grads(0, early, sums)
    core_copy(0, 1).start()
    to_all(1, 1)
    halo_wait(3)
    assemble(3, gx, qg)
    to_z(0, 0)
    to_plane(0, 1)
    convolve(qg, 0, True)
    step_back(0)
    to_sibling(1, 1)
    to_all(0, 0)
    to_z(0, 1)
    out_ref[...] = tn(place[...], outq[...]).astype(BF16)
    leave(0, out_ref, out_to).start()
    g = grad[...]
    high = g.astype(BF16)
    g = g - high.astype(F32)
    mid = g.astype(BF16)
    low = (g - mid.astype(F32)).astype(BF16)
    gfeat_ref[...] = tn(place[...], high) + (tn(place[...], mid) + tn(place[...], low))
    leave(1, gfeat_ref, gfeat_to).start()
    to_sibling(0, 0)
    to_all(0, 1)
    finish(1, 0)
    leave(2, result0.at[1], result0_to.at[1]).start()
    finish(1, 1)
    leave(3, result1.at[1], result1_to.at[1]).start()
    for n in range(4):
        halo_done(n)
    to_sibling(0, 1)
    finish(0, 0)
    leave(4, result0.at[0], result0_to.at[0]).start()
    finish(0, 1)
    leave(5, result1.at[0], result1_to.at[0]).start()
    leave(0, out_ref, out_to).wait()
    leave(1, gfeat_ref, gfeat_to).wait()
    leave(2, result0.at[1], result0_to.at[1]).wait()
    leave(3, result1.at[1], result1_to.at[1]).wait()
    leave(4, result0.at[0], result0_to.at[0]).wait()
    leave(5, result1.at[0], result1_to.at[0]).wait()


def unpack(out_in, gfeat_in, result0_in, result1_in,
           out, gfeat, gtaps, gcbias, ggain, gshift, gup, gubias, gdown, gdbias, gscale,
           few, result0, result1, ins):
    copies = [
        pltpu.make_async_copy(src, dst, ins.at[k])
        for k, (src, dst) in enumerate(
            ((result0_in, result0), (result1_in, result1), (gfeat_in, gfeat), (out_in, out))
        )
    ]
    for copy in copies:
        copy.start()
    upper = lax.broadcasted_iota(jnp.int32, (8, LANES), 0) < 4

    def place_tile(l, ref, index, tile):
        t, r = divmod(index, CH // 8)
        ref[l, 8 * r : 8 * r + 8, LANES * t : LANES * t + LANES] = tile

    copies[0].wait()
    for l in range(2):
        for chunk in range(2 * CHUNKS):
            v = result0[l, chunk // CHUNKS, chunk % CHUNKS].astype(F32)
            for slot in range(4):
                place_tile(l, gdown, 4 * chunk + slot, v[8 * slot : 8 * slot + 8])
    copies[1].wait()
    for l in range(2):
        pair = []
        for chunk in range(2 * CHUNKS):
            v = result1[l, chunk // CHUNKS, chunk % CHUNKS].astype(F32)
            for slot in range(5):
                index = 5 * chunk + slot
                tile = v[8 * slot : 8 * slot + 8]
                if index < CH // 8 * 6:
                    place_tile(l, gup, index, tile)
                else:
                    place_tile(l, gdown, index - CH // 8 * 6 + DTILES, tile)
            v = v[SMALL_AT:]
            pair.append(v + pltpu.roll(v, 4, 0))
            if chunk % 2:
                few[4 * chunk - 4 : 4 * chunk + 4] = jnp.where(upper, pair[-2], pair[-1])
        for t in range(TAPS):
            gtaps[t, l : l + 1, :LANES] = few[t : t + 1]
            gtaps[t, l : l + 1, LANES:] = few[TAPS + t : TAPS + t + 1, :REST]
        for at, ref in ((ROW_CBIAS, gcbias), (ROW_GAIN, ggain), (ROW_SHIFT, gshift),
                        (ROW_DBIAS, gdbias), (ROW_SCALE, gscale)):
            ref[l : l + 1, :LANES] = few[at : at + 1]
            ref[l : l + 1, LANES:] = few[at + 1 : at + 2, :REST]
        for t in range(6):
            gubias[l : l + 1, LANES * t : LANES * t + LANES] = few[ROW_UBIAS + t : ROW_UBIAS + t + 1]
    copies[2].wait()
    copies[3].wait()


def on_device(features, cotangent, dw_kernel, conv_bias, ln_gain, ln_shift, up_weight, up_bias,
              down_weight, down_bias, layer_scale):
    depth = dw_kernel.shape[0]
    pixel_total = PX * lax.axis_size("slide") * lax.axis_size("ty") * lax.axis_size("tx")
    place, edges, spread = (jnp.asarray(v, BF16) for v in one_hots())
    taps = dw_kernel.reshape(depth, TAPS, CH).transpose(1, 0, 2)
    vmem = pl.BlockSpec(memory_space=pltpu.VMEM)
    dma = pltpu.SemaphoreType.DMA
    plane = (NI, TC + 6, NS, CH)
    wide = (NI + 6, WIDE, NS, LANES)
    hbm = pl.BlockSpec(memory_space=pltpu.HBM)
    results = tuple(jax.ShapeDtypeStruct((depth, 2, CHUNKS, rows, LANES), BF16) for rows in PARTS)
    out, gfeat, result0, result1 = pl.pallas_call(
        functools.partial(kernel, 1.0 / math.sqrt(pixel_total)),
        out_shape=(
            jax.ShapeDtypeStruct((PX, CH), BF16),
            jax.ShapeDtypeStruct((PX, CH), F32),
            *results,
        ),
        in_specs=[hbm] * 3 + [vmem] * 3 + [hbm, vmem, hbm] + [vmem] * 2 + [hbm] * 3,
        out_specs=(hbm,) * 4,
        scratch_shapes=[
            pltpu.VMEM((PX, CH), BF16),
            pltpu.VMEM((PX, CH), BF16),
            pltpu.VMEM((TAPS, depth, CH), F32),
            pltpu.VMEM((depth, CH, HID), BF16),
            pltpu.VMEM((depth, CH, HID), BF16),
            pltpu.VMEM(place.shape, BF16),
            pltpu.VMEM(edges.shape, BF16),
            pltpu.VMEM(spread.shape, BF16),
            pltpu.VMEM((PX, CH), BF16),
            pltpu.VMEM((PX, CH), F32),
            *(pltpu.VMEM(v.shape, v.dtype) for v in results),
            dma((8,)), dma((6,)),
            pltpu.VMEM((2, *plane), F32),
            pltpu.VMEM(plane, F32),
            pltpu.VMEM((2, *wide), F32),
            pltpu.VMEM(wide, F32),
            pltpu.VMEM((NI, PACK, NS, LANES), F32),
            pltpu.VMEM((TC * NS, CH), F32),
            pltpu.VMEM((2, PX, CH), F32),
            pltpu.VMEM((2, PX, 1), F32),
            pltpu.VMEM((2, PX, CH), BF16),
            pltpu.VMEM((2, PX, HID), BF16),
            pltpu.VMEM((2, PX, HID), F32),
            pltpu.VMEM((2, PX, CH), F32),
            pltpu.VMEM((PX, CH), BF16),
            pltpu.VMEM((PX, HID), BF16),
            pltpu.VMEM((NI, PACK, NS, LANES), F32),
            pltpu.VMEM((2, 3, TC + 6, NS, CH), F32),
            pltpu.VMEM((2, TAPS, NS, LANES), F32),
            pltpu.VMEM((LANES, LANES), F32),
            pltpu.VMEM((PX, CH), F32),
            pltpu.VMEM((PX, CH), BF16),
            pltpu.VMEM((2, 2, TAPS, NS, LANES), F32),
            *(pltpu.VMEM((2, 2, CHUNKS, rows, LANES), F32) for rows in PARTS),
            *(pltpu.VMEM((2, CHUNKS, rows, LANES), F32) for rows in PARTS),
            *(pltpu.VMEM((2, CHUNKS, rows, LANES), BF16) for rows in PARTS),
            *(pltpu.VMEM((2, CHUNKS, rows, LANES), BF16) for rows in PARTS),
            *(pltpu.VMEM((2, NZ, rows, LANES), BF16) for rows in PARTS),
            pltpu.VMEM((4, 2, 3, TR, CH), BF16),
            pltpu.VMEM((4, 2, 3, TC, CH), BF16),
            pltpu.VMEM((4, 2, 3, TR, CH), BF16),
            pltpu.VMEM((4, 6, 3, TC, CH), BF16),
            dma((4, 8)), dma((4, 8)),
            dma((4,)), dma((4,)),
            dma((4, CHUNKS)), dma((4, CHUNKS)),
            dma((4, NZ)), dma((4, NZ)),
            dma((4, CHUNKS)), dma((4, CHUNKS)),
            dma((4, CHUNKS)), dma((4, CHUNKS)),
        ],
        compiler_params=pltpu.CompilerParams(
            collective_id=0, has_side_effects=True, vmem_limit_bytes=56 * 2**20
        ),
    )(
        features.reshape(PX, CH), cotangent.reshape(PX, CH), taps, conv_bias, ln_gain, ln_shift,
        up_weight, up_bias, down_weight.transpose(0, 2, 1), down_bias, layer_scale, place, edges, spread,
    )
    vector = jax.ShapeDtypeStruct((depth, CH), F32)
    weight = jax.ShapeDtypeStruct((depth, CH, HID), F32)
    out, gfeat, gtaps, gcbias, ggain, gshift, gup, gubias, gdown, gdbias, gscale = pl.pallas_call(
        unpack,
        out_shape=(
            jax.ShapeDtypeStruct((PX, CH), BF16),
            jax.ShapeDtypeStruct((PX, CH), F32),
            jax.ShapeDtypeStruct((TAPS, depth, CH), F32),
            vector, vector, vector, weight, jax.ShapeDtypeStruct((depth, HID), F32), weight, vector, vector,
        ),
        in_specs=[hbm] * 4,
        out_specs=(vmem,) * 11,
        scratch_shapes=[
            pltpu.VMEM((LANES, LANES), F32),
            *(pltpu.VMEM(v.shape, v.dtype) for v in results),
            dma((4,)),
        ],
        compiler_params=pltpu.CompilerParams(vmem_limit_bytes=56 * 2**20),
    )(out, gfeat, result0, result1)
    return (
        out.reshape(1, TR, TC, CH),
        gfeat.reshape(1, TR, TC, CH),
        gtaps.transpose(1, 0, 2).reshape(depth, SPAN, SPAN, CH),
        gcbias,
        ggain,
        gshift,
        gup,
        gubias,
        gdown.transpose(0, 2, 1),
        gdbias,
        gscale,
    )


def solution(mesh):
    tiled = P("slide", "ty", "tx", None)
    return jax.shard_map(
        on_device,
        mesh=mesh,
        in_specs=(tiled, tiled) + (P(),) * 9,
        out_specs=(tiled, tiled) + (P(),) * 9,
        check_vma=False,
    )
```

```python
import functools
import math

import jax
import jax.numpy as jnp
import numpy as np
from jax import lax
from jax.experimental import pallas as pl
from jax.experimental.pallas import tpu as pltpu
from jax.sharding import PartitionSpec as P

MESH = pl.DeviceIdType.MESH
F32 = jnp.float32
BF16 = jnp.bfloat16
ROOT_HALF = 0.7071067811865476
INV_ROOT_TAU = 0.3989422804014327
EPSILON = 1e-06

TR, TC, CH, HID = 32, 16, 192, 768
PX = TR * TC
NI, NS = 4, 8
MARGIN = 3
SPAN = 7
TAPS = SPAN * SPAN
LANES = 128
REST = CH - LANES
PACK = TC + TC // 2
WIDE = (TC + 2 * MARGIN) + (TC // 2 + 2 * MARGIN)
PARTS = (32, 48)
DTILES = 128
USED = 40
CHUNKS = 16
NZ = 8
HALOS = ((-1, -1), (-1, 0), (-1, 1), (1, -1), (1, 0), (1, 1), (0, -1), (0, 1))

ROW_CBIAS, ROW_GAIN, ROW_SHIFT, ROW_DBIAS, ROW_SCALE, ROW_UBIAS = 98, 100, 102, 104, 106, 108


def pixel_order():
    q = np.arange(PX)
    return (4 * (q % NS) + q // (TC * NS)) * TC + (q // NS) % TC


def one_hots():
    order = pixel_order()
    place = np.zeros((PX, PX), np.float32)
    place[np.arange(PX), order] = 1.0
    inverse = np.argsort(order)
    edge_rows = np.concatenate([np.arange(3 * TC), np.arange((TR - 3) * TC, TR * TC)])
    edges = np.zeros((6 * TC, PX), np.float32)
    edges[np.arange(6 * TC), inverse[edge_rows]] = 1.0
    spread = np.zeros((2, 3, TC + 6, NS, 3, 3, TC), np.float32)
    for cc in range(TC + 6):
        source, column = (0, TC - 3 + cc) if cc < 3 else (1, cc - 3) if cc < TC + 3 else (2, cc - TC - 3)
        for u in range(3):
            spread[0, u, cc, 0, source, u, column] = 1.0
            spread[1, u, cc, NS - 1, source, u, column] = 1.0
    spread = spread.reshape(2, 3 * (TC + 6) * NS, 9 * TC)
    return place, edges, spread


def tn(a, b):
    return lax.dot_general(a, b, (((0,), (0,)), ((), ())), preferred_element_type=F32)


def nt(a, b):
    return lax.dot_general(a, b, (((1,), (1,)), ((), ())), preferred_element_type=F32)


def nn(a, b):
    return jnp.dot(a, b, preferred_element_type=F32)


def kernel(
    factor,
    feat_in, cot_in, dw_in, cbias, gain, shift, up_in, ubias, down_in, dbias, scale, place_in, edges_in, spread_in,
    out_to, gfeat_to, result0_to, result1_to, result2_to,
    feat, cot, dw, up, down, place, edges, spread, out_ref, gfeat_ref, result0, result1, result2, ins, outs,
    xp, gx, qa, qg, cbuf, conv, unit, inv, normed, act, slope, branch, gbr, gpre, gcp, tq, taps, small,
    grad, outq, wexp,
    pay0, pay1, core0, core1, sbuf0, sbuf1, rbuf0, rbuf1, zbuf0, zbuf1,
    few, fewr, fewz, csend, rsend, crecv, rrecv,
    hs, hr, cs, cr, xs, xr, zs, zr, gs, gr, ls, lr, fs, fr,
):
    yh = lax.axis_index("slide")
    ty = lax.axis_index("ty")
    tx = lax.axis_index("tx")
    core = lax.rem(tx, 2)
    yl = lax.rem(lax.div(tx, 2), 2)
    z = lax.div(tx, 4)
    other = 1 - core
    me = ty * 4 + yh * 2 + yl
    sibling = (yh, ty, z * 4 + yl * 2 + other)

    def plane_peer(d):
        py = lax.rem(ty + lax.div(d, 4), 4)
        ph = lax.rem(yh + lax.rem(lax.div(d, 2), 2), 2)
        pl_ = lax.rem(yl + lax.rem(d, 2), 2)
        return py * 4 + ph * 2 + pl_, (ph, py, z * 4 + pl_ * 2 + core)

    def column_peer(e):
        pz = lax.rem(z + lax.div(e, 2), NZ)
        pc = lax.rem(core + lax.rem(e, 2), 2)
        return pz * 2 + pc, (yh, ty, pz * 4 + yl * 2 + pc)

    def z_peer(d):
        pz = lax.rem(z + d, NZ)
        return pz, (yh, ty, pz * 4 + yl * 2 + core)

    barrier = pltpu.get_barrier_semaphore()

    def greet(device):
        pl.semaphore_signal(barrier, inc=1, device_id=device, device_id_type=MESH)

    for dy, dx in HALOS:
        greet((yh, lax.rem(ty + dy + 4, 4), lax.rem(tx + dx + 32, 32)))
    @pl.loop(1, CHUNKS)
    def _(d):
        greet(plane_peer(d)[1])

    @pl.loop(1, 2 * NZ)
    def _(e):
        greet(column_peer(e)[1])

    arrivals = {}
    loads = ((feat_in, feat), (place_in, place), (edges_in, edges), (cot_in, cot), (dw_in, dw), (spread_in, spread),
             (up_in, up), (down_in, down))
    for k, (src, dst) in enumerate(loads):
        arrivals[id(dst)] = pltpu.make_async_copy(src, dst, ins.at[k])
        arrivals[id(dst)].start()

    def ready(*refs):
        for ref in refs:
            arrivals[id(ref)].wait()

    def leave(k, src, dst):
        return pltpu.make_async_copy(src, dst, outs.at[k])

    def there(dy, dx):
        flags = []
        if dy:
            flags.append(jnp.logical_and(ty + dy >= 0, ty + dy < 4))
        if dx:
            flags.append(jnp.logical_and(tx + dx >= 0, tx + dx < 32))
        return functools.reduce(jnp.logical_and, flags)

    def halo_copy(n, dy, dx):
        if dy == 0:
            slot = 6 if dx > 0 else 7
            src, dst = csend.at[n, 0 if dx < 0 else 1], crecv.at[n, slot - 6]
        else:
            slot = (1 if dy > 0 else 4) - dx
            src, dst = rsend.at[n, 0 if dy < 0 else 1], rrecv.at[n, slot]
        return pltpu.make_async_remote_copy(
            src_ref=src, dst_ref=dst, send_sem=hs.at[n, slot], recv_sem=hr.at[n, slot],
            device_id=(yh, ty + dy, tx + dx), device_id_type=MESH,
        )

    def halo_start(n, plane):
        flat = jnp.concatenate([plane[i, 3 : 3 + TC].reshape(TC * NS, CH) for i in range(NI)], axis=0)
        strips = nn(edges[...], flat.astype(BF16)).astype(BF16)
        rsend[n] = strips.reshape(2, 3, TC, CH)
        for c in range(3):
            csend[n, 0, c] = plane[:, 3 + c].reshape(TR, CH).astype(BF16)
            csend[n, 1, c] = plane[:, TC + c].reshape(TR, CH).astype(BF16)
        if n == 0:
            pl.semaphore_wait(barrier, 8 + CHUNKS - 1 + 2 * NZ - 1)
        for dy, dx in HALOS:

            @pl.when(there(dy, dx))
            def _(dy=dy, dx=dx):
                halo_copy(n, dy, dx).start()

    def halo_wait(n):
        for dy, dx in HALOS:

            @pl.when(there(-dy, -dx))
            def _(dy=dy, dx=dx):
                halo_copy(n, dy, dx).wait_recv()

            @pl.when(jnp.logical_not(there(-dy, -dx)))
            def _(dy=dy, dx=dx):
                if dy == 0:
                    crecv[n, 0 if dx > 0 else 1] = jnp.zeros((3, TR, CH), BF16)
                else:
                    rrecv[n, (1 if dy > 0 else 4) - dx] = jnp.zeros((3, TC, CH), BF16)

    def halo_done(n):
        for dy, dx in HALOS:

            @pl.when(there(dy, dx))
            def _(dy=dy, dx=dx):
                halo_copy(n, dy, dx).wait_send()

    def assemble(n, plane, q):
        for c in range(3):
            plane[:, c] = crecv[n, 0, c].astype(F32).reshape(NI, NS, CH)
            plane[:, TC + 3 + c] = crecv[n, 1, c].astype(F32).reshape(NI, NS, CH)
        for side in range(2):
            strips = jnp.concatenate([rrecv[n, 3 * side + k].reshape(3 * TC, CH) for k in range(3)], axis=0)
            tq[side] = nn(spread[side], strips).reshape(3, TC + 6, NS, CH)
        row = lax.broadcasted_iota(jnp.int32, (3, NS, LANES), 1)

        def fill(slot, mid, top, low):
            q[3:7, slot] = mid
            q[0:3, slot] = jnp.where(row == 0, top, pltpu.roll(mid[1:4], 1, 1))
            q[7:10, slot] = jnp.where(row == NS - 1, low, pltpu.roll(mid[0:3], NS - 1, 1))

        @pl.loop(0, TC + 6)
        def _(cc):
            fill(cc, plane[:, cc, :, :LANES], tq[0, :, cc, :, :LANES], tq[1, :, cc, :, :LANES])

        def pair(ref, *at):
            return jnp.concatenate([ref[(*at[:-1], at[-1], slice(None), slice(LANES, CH))],
                                    ref[(*at[:-1], at[-1] + 8, slice(None), slice(LANES, CH))]], axis=-1)

        @pl.loop(0, TC // 2 + 6)
        def _(k):
            fill(TC + 6 + k, pair(plane, slice(None), k), pair(tq, 0, slice(None), k), pair(tq, 1, slice(None), k))

    def convolve(q, l, flip):
        def columns(part, t, base):
            sums = [[None, None] for _ in range(NI)]
            for j2 in range(SPAN + 1):
                for r in range(NI + SPAN - 1):
                    x = q[r, base + j2]
                    for i in range(NI):
                        if not 0 <= r - i < SPAN:
                            continue
                        for o in range(2):
                            if not 0 <= j2 - o < SPAN:
                                continue
                            tap = (r - i) * SPAN + j2 - o
                            term = x * wexp[l, part, TAPS - 1 - tap if flip else tap]
                            sums[i][o] = term if sums[i][o] is None else sums[i][o] + term
            for i in range(NI):
                for o in range(2):
                    cbuf[i, t + o] = sums[i][o]

        @pl.loop(0, TC // 2)
        def _(k):
            columns(0, 2 * k, 2 * k)

        @pl.loop(0, TC // 4)
        def _(k):
            columns(1, TC + 2 * k, TC + 6 + 2 * k)

    def conv_rows(i):
        half = TC * NS // 2
        conv[:, :LANES] = cbuf[i, :TC].reshape(TC * NS, LANES)
        rest = cbuf[i, TC:].reshape(half, LANES)
        conv[:half, LANES:] = rest[:, :REST]
        conv[half:, LANES:] = rest[:, REST:]
        return conv[...]

    blk = TC * NS

    def rows_of(i):
        return pl.ds(pl.multiple_of(i * blk, blk), blk)

    def forward(l, plane, into, i):
        c = conv_rows(i) + cbias[l : l + 1]
        mid = c - jnp.mean(c, axis=1, keepdims=True)
        rstd = lax.rsqrt(jnp.mean(mid * mid, axis=1, keepdims=True) + EPSILON)
        u = mid * rstd
        rows = rows_of(i)
        unit[l, rows] = u
        inv[l, rows] = rstd
        nb = (u * gain[l : l + 1] + shift[l : l + 1]).astype(BF16)
        normed[l, rows] = nb
        pre = nn(nb, up[l]) + ubias[l : l + 1]
        cdf = 0.5 * (1.0 + lax.erf(pre * ROOT_HALF))
        slope[l, rows] = cdf + pre * INV_ROOT_TAU * jnp.exp(-0.5 * pre * pre)
        ab = (pre * cdf).astype(BF16)
        act[l, rows] = ab
        br = nt(ab, down[l]) + dbias[l : l + 1]
        branch[l, rows] = br
        before = plane[i, 3 : 3 + TC].reshape(blk, CH)
        new = (before + scale[l : l + 1] * br).astype(BF16)
        into(i, new)

    def fold(v):
        return jnp.sum(v.reshape(blk // 8, 8, v.shape[1]), axis=0)

    def branch_grads(l):
        def body(i, sums):
            rows = rows_of(i)
            g = grad[rows]
            gb = (g * scale[l : l + 1]).astype(BF16)
            gbr[rows] = gb
            return sums[0] + fold(gb.astype(F32)), sums[1] + fold(g * branch[l, rows])

        return lax.fori_loop(0, NI, body, (jnp.zeros((8, CH), F32),) * 2)

    def pre_grads(l):
        def body(i, total):
            rows = rows_of(i)
            gp = (nn(gbr[rows], down[l]) * slope[l, rows]).astype(BF16)
            gpre[rows] = gp
            return total + fold(gp.astype(F32))

        return lax.fori_loop(0, NI, body, jnp.zeros((8, HID), F32))

    def backward(l):
        def body(i, sums):
            rows = rows_of(i)
            s_gain, s_shift, s_cbias = sums
            gn = nt(gpre[rows], up[l])
            u = unit[l, rows]
            s_gain = s_gain + fold(gn * u)
            s_shift = s_shift + fold(gn)
            q = gn * gain[l : l + 1]
            centred = q - jnp.mean(q, axis=1, keepdims=True) - u * jnp.mean(q * u, axis=1, keepdims=True)
            gc = (inv[l, rows] * centred).astype(BF16).astype(F32)
            s_cbias = s_cbias + fold(gc)
            gx[i, 3 : 3 + TC] = gc.reshape(TC, NS, CH)
            gcp[i, :TC] = gc[:, :LANES].reshape(TC, NS, LANES)
            half = blk // 2
            gcp[i, TC:, :, :REST] = gc[:half, LANES:].reshape(TC // 2, NS, REST)
            gcp[i, TC:, :, REST:] = gc[half:, LANES:].reshape(TC // 2, NS, REST)
            return s_gain, s_shift, s_cbias

        zero = jnp.zeros((8, CH), F32)
        return lax.fori_loop(0, NI, body, (zero, zero, zero))

    def put(l, index, tile, tiles, pay):
        chunk, slot = divmod(index, tiles)
        pay[l, chunk // CHUNKS, chunk % CHUNKS, 8 * slot : 8 * slot + 8] = tile

    def weight_tiles(a, b, store):
        for t in range(3):
            part = tn(a[...], b[:, 256 * t : 256 * t + 256])
            for v in range(2):
                for r in range(CH // 8):
                    store((2 * t + v) * (CH // 8) + r, part[8 * r : 8 * r + 8, LANES * v : LANES * v + LANES])

    def down_grads(l):
        def store(index, tile):
            if index < DTILES:
                put(l, index, tile, 4, pay0)
            else:
                put(l, index + CH // 8 * 6 - DTILES, tile, 5, pay1)

        weight_tiles(gbr, act.at[l], store)

    def up_grads(l):
        weight_tiles(normed.at[l], gpre, lambda index, tile: put(l, index, tile, 5, pay1))

    def tap_grads(l):
        for part, (cols, base, first) in enumerate(((TC, 0, 0), (TC // 2, TC + 6, TC))):

            @pl.loop(0, SPAN)
            def _(j):
                def body(c, sums):
                    sums = list(sums)
                    for o in range(2):
                        col = 2 * c + o
                        gcs = [gcp[i, first + col] for i in range(NI)]
                        for r in range(NI + SPAN - 1):
                            x = qa[l, r, base + col + j]
                            for i in range(NI):
                                if 0 <= r - i < SPAN:
                                    sums[r - i] = sums[r - i] + gcs[i] * x
                    return tuple(sums)

                zero = jnp.zeros((NS, LANES), F32)
                sums = lax.fori_loop(0, cols // 2, body, (zero,) * SPAN)
                for r in range(SPAN):
                    taps[part, r * SPAN + j] = sums[r]

    def small_grads(l, early, s_ubias, sums):
        s_dbias, s_scale = early
        s_gain, s_shift, s_cbias = sums
        small[...] = jnp.zeros((LANES, LANES), F32)
        small[:TAPS] = jnp.sum(taps[0], axis=1)
        rest = jnp.sum(taps[1], axis=1)
        small[TAPS : 2 * TAPS, :REST] = rest[:, :REST] + rest[:, REST:]
        for at, v in ((ROW_CBIAS, s_cbias), (ROW_GAIN, s_gain), (ROW_SHIFT, s_shift),
                      (ROW_DBIAS, s_dbias), (ROW_SCALE, s_scale)):
            v = jnp.sum(v, axis=0, keepdims=True)
            small[at : at + 1] = v[:, :LANES]
            small[at + 1 : at + 2, :REST] = v[:, LANES:]
        v = jnp.sum(s_ubias, axis=0, keepdims=True)
        for t in range(6):
            small[ROW_UBIAS + t : ROW_UBIAS + t + 1] = v[:, LANES * t : LANES * t + LANES]
        few[l] = small[...].reshape(CHUNKS, 8, LANES)

    pays, cores, sbufs, rbufs, zbufs = (pay0, pay1), (core0, core1), (sbuf0, sbuf1), (rbuf0, rbuf1), (zbuf0, zbuf1)
    results = (result0, result1)

    def core_copy(l, p):
        return pltpu.make_async_remote_copy(
            src_ref=pays[p].at[l, other], dst_ref=cores[p].at[l], send_sem=cs.at[2 * l + p], recv_sem=cr.at[2 * l + p],
            device_id=sibling, device_id_type=MESH,
        )

    def plane_copy(l, p, d):
        index, device = plane_peer(d)
        return pltpu.make_async_remote_copy(
            src_ref=sbufs[p].at[l, index], dst_ref=rbufs[p].at[l, d], send_sem=xs.at[2 * l + p, d], recv_sem=xr.at[2 * l + p, d],
            device_id=device, device_id_type=MESH,
        )

    def z_copy(l, p, d):
        return pltpu.make_async_remote_copy(
            src_ref=zbufs[p].at[l, z], dst_ref=zbufs[p].at[l, z], send_sem=zs.at[2 * l + p, d], recv_sem=zr.at[2 * l + p, z],
            device_id=z_peer(d)[1], device_id_type=MESH,
        )

    def z_arrival(l, p, d):
        pz, device = z_peer(d)
        return pltpu.make_async_remote_copy(
            src_ref=zbufs[p].at[l, pz], dst_ref=zbufs[p].at[l, pz], send_sem=zs.at[2 * l + p, d], recv_sem=zr.at[2 * l + p, pz],
            device_id=device, device_id_type=MESH,
        )

    def gather_copy(l, p, d):
        return pltpu.make_async_remote_copy(
            src_ref=results[p].at[l, core, me], dst_ref=results[p].at[l, core, me], send_sem=gs.at[2 * l + p, d],
            recv_sem=gr.at[2 * l + p, me], device_id=plane_peer(d)[1], device_id_type=MESH,
        )

    def gather_arrival(l, p, d):
        index, device = plane_peer(d)
        return pltpu.make_async_remote_copy(
            src_ref=results[p].at[l, core, index], dst_ref=results[p].at[l, core, index], send_sem=gs.at[2 * l + p, d],
            recv_sem=gr.at[2 * l + p, index], device_id=device, device_id_type=MESH,
        )

    def relay_copy(l, p, index):
        return pltpu.make_async_remote_copy(
            src_ref=results[p].at[l, core, index], dst_ref=results[p].at[l, core, index], send_sem=ls.at[2 * l + p, index],
            recv_sem=lr.at[2 * l + p, index], device_id=sibling, device_id_type=MESH,
        )

    def relay_arrival(l, p, index):
        return pltpu.make_async_remote_copy(
            src_ref=results[p].at[l, other, index], dst_ref=results[p].at[l, other, index], send_sem=ls.at[2 * l + p, index],
            recv_sem=lr.at[2 * l + p, index], device_id=sibling, device_id_type=MESH,
        )

    def to_plane(l, p):
        core_copy(l, p).wait_recv()

        @pl.loop(0, CHUNKS)
        def _(k):
            d = lax.rem(k + 1, CHUNKS)
            index, _ = plane_peer(d)
            v = pays[p][l, core, index] + cores[p][l, index]
            sbufs[p][l, index] = v.astype(BF16)

            @pl.when(d > 0)
            def _():
                plane_copy(l, p, d).start()

    def to_z(l, p):
        @pl.loop(1, CHUNKS)
        def _(d):
            plane_copy(l, p, d).wait_recv()

        v = lax.fori_loop(1, CHUNKS, lambda d, v: v + rbufs[p][l, d].astype(F32), sbufs[p][l, me].astype(F32))
        zbufs[p][l, z] = v.astype(BF16)

        @pl.loop(1, NZ)
        def _(d):
            z_copy(l, p, d).start()

    def to_all(l, p):
        @pl.loop(1, NZ)
        def _(d):
            z_arrival(l, p, d).wait_recv()

        v = zbufs[p][l, 0].astype(F32)
        for k in range(1, NZ):
            v = v + zbufs[p][l, k].astype(F32)
        results[p][l, core, me] = (v * factor).astype(BF16)

        @pl.loop(1, CHUNKS)
        def _(d):
            gather_copy(l, p, d).start()

        relay_copy(l, p, me).start()

    def to_sibling(l, p):
        @pl.loop(1, CHUNKS)
        def _(d):
            gather_arrival(l, p, d).wait_recv()
            relay_copy(l, p, plane_peer(d)[0]).start()

    def finish(l, p):
        @pl.loop(0, CHUNKS)
        def _(k):
            relay_arrival(l, p, k).wait_recv()
            relay_copy(l, p, k).wait_send()

        core_copy(l, p).wait_send()

        @pl.loop(1, CHUNKS)
        def _(d):
            plane_copy(l, p, d).wait_send()
            gather_copy(l, p, d).wait_send()

        @pl.loop(1, NZ)
        def _(d):
            z_copy(l, p, d).wait_send()


    def few_copy(l, stage, d):
        if stage == 0:
            index, device = plane_peer(d)
            src, dst, slot = few.at[l, index], fewr.at[l, d], d
        elif stage == 1:
            device = column_peer(d)[1]
            slot = z * 2 + core
            src = dst = fewz.at[l, slot]
        else:
            device, slot = plane_peer(d)[1], me
            src = dst = result2.at[l, slot]
        return pltpu.make_async_remote_copy(
            src_ref=src, dst_ref=dst, send_sem=fs.at[3 * l + stage, d], recv_sem=fr.at[3 * l + stage, slot],
            device_id=device, device_id_type=MESH,
        )

    def few_arrival(l, stage, d):
        if stage == 0:
            return few_copy(l, 0, d)
        if stage == 1:
            slot, device = column_peer(d)
            ref = fewz.at[l, slot]
        else:
            slot, device = plane_peer(d)
            ref = result2.at[l, slot]
        return pltpu.make_async_remote_copy(
            src_ref=ref, dst_ref=ref, send_sem=fs.at[3 * l + stage, d], recv_sem=fr.at[3 * l + stage, slot],
            device_id=device, device_id_type=MESH,
        )

    def few_send(l, stage):
        @pl.loop(1, CHUNKS)
        def _(d):
            few_copy(l, stage, d).start()

    def few_wait(l, stage):
        @pl.loop(1, CHUNKS)
        def _(d):
            few_arrival(l, stage, d).wait_recv()

    def few_column(l):
        few_wait(l, 0)
        v = few[l, me]
        for d in range(1, CHUNKS):
            v = v + fewr[l, d]
        fewz[l, z * 2 + core] = v
        few_send(l, 1)

    def few_plane(l):
        few_wait(l, 1)
        v = fewz[l, 0]
        for k in range(1, 2 * NZ):
            v = v + fewz[l, k]
        result2[l, me] = v * factor
        few_send(l, 2)

    def few_finish(l):
        few_wait(l, 2)

        @pl.loop(1, CHUNKS)
        def _(d):
            for stage in range(3):
                few_copy(l, stage, d).wait_send()

    def flat_rows(plane, i):
        return plane[i, 3 : 3 + TC].reshape(blk, CH)

    def step_back(l):
        @pl.loop(0, NI)
        def _(i):
            rows = rows_of(i)
            grad[rows] = grad[rows] + conv_rows(i)

    ready(feat, place, edges)
    xp[0, :, 3 : 3 + TC] = nn(place[...], feat[...]).reshape(NI, TC, NS, CH)
    halo_start(0, xp.at[0])
    for l in range(2):
        for k in range(2 * CHUNKS):
            pay1[l, k // CHUNKS, k % CHUNKS, USED:] = jnp.zeros((8, LANES), F32)
    ready(cot, dw, spread)
    grad[...] = nn(place[...], cot[...])

    @pl.loop(0, TAPS)
    def _(t):
        for l in range(2):
            tap = dw[t, l : l + 1]
            rest = tap[:, LANES:]
            wexp[l, 0, t] = jnp.broadcast_to(tap[:, :LANES], (NS, LANES))
            wexp[l, 1, t] = jnp.broadcast_to(jnp.concatenate([rest, rest], axis=1), (NS, LANES))

    halo_wait(0)
    assemble(0, xp.at[0], qa.at[0])
    convolve(qa.at[0], 0, False)
    ready(up, down)

    def keep(i, new):
        xp[1, i, 3 : 3 + TC] = new.astype(F32).reshape(TC, NS, CH)

    @pl.loop(0, NI)
    def _(i):
        forward(0, xp.at[0], keep, i)

    halo_start(1, xp.at[1])
    halo_wait(1)
    assemble(1, xp.at[1], qa.at[1])
    convolve(qa.at[1], 1, False)

    def keep_out(i, new):
        outq[rows_of(i)] = new

    @pl.loop(0, NI)
    def _(i):
        forward(1, xp.at[1], keep_out, i)

    def leave_all(l):
        return [leave(3 * l + k, v.at[l], to.at[l]) for k, (v, to) in enumerate(
            ((result0, result0_to), (result1, result1_to), (result2, result2_to)))]

    early = branch_grads(1)
    down_grads(1)
    core_copy(1, 0).start()
    s_ubias = pre_grads(1)
    up_grads(1)
    core_copy(1, 1).start()
    sums = backward(1)
    halo_start(2, gx)
    to_plane(1, 0)
    tap_grads(1)
    to_plane(1, 1)
    small_grads(1, early, s_ubias, sums)
    few_send(1, 0)
    halo_wait(2)
    assemble(2, gx, qg)
    to_z(1, 0)
    convolve(qg, 1, True)
    step_back(1)
    early = branch_grads(0)
    down_grads(0)
    core_copy(0, 0).start()
    to_z(1, 1)
    s_ubias = pre_grads(0)
    up_grads(0)
    core_copy(0, 1).start()
    few_column(1)
    to_plane(0, 0)
    sums = backward(0)
    halo_start(3, gx)
    to_plane(0, 1)
    to_all(1, 0)
    tap_grads(0)
    small_grads(0, early, s_ubias, sums)
    few_send(0, 0)
    few_plane(1)
    halo_wait(3)
    assemble(3, gx, qg)
    to_z(0, 0)
    to_all(1, 1)
    convolve(qg, 0, True)
    step_back(0)
    to_z(0, 1)
    few_column(0)
    to_sibling(1, 0)
    g = grad[...]
    high = g.astype(BF16)
    g = g - high.astype(F32)
    mid = g.astype(BF16)
    low = (g - mid.astype(F32)).astype(BF16)
    gfeat_ref[...] = tn(place[...], high) + (tn(place[...], mid) + tn(place[...], low))
    leave(6, gfeat_ref, gfeat_to).start()
    to_all(0, 0)
    few_plane(0)
    to_sibling(1, 1)
    out_ref[...] = tn(place[...], outq[...]).astype(BF16)
    leave(7, out_ref, out_to).start()
    to_all(0, 1)
    for n in range(4):
        halo_done(n)
    to_sibling(0, 0)
    for p in range(2):
        finish(1, p)
    few_finish(1)
    for copy in leave_all(1):
        copy.start()
    few_finish(0)
    to_sibling(0, 1)
    for p in range(2):
        finish(0, p)
    for copy in leave_all(0):
        copy.start()
    for copy in leave_all(0) + leave_all(1):
        copy.wait()
    leave(6, gfeat_ref, gfeat_to).wait()
    leave(7, out_ref, out_to).wait()


def unpack(out_in, gfeat_in, result0_in, result1_in, result2_in,
           out, gfeat, gtaps, gcbias, ggain, gshift, gup, gubias, gdown, gdbias, gscale,
           result0, result1, result2, ins):
    copies = [
        pltpu.make_async_copy(src, dst, ins.at[k])
        for k, (src, dst) in enumerate(
            ((result0_in, result0), (result1_in, result1), (result2_in, result2), (gfeat_in, gfeat), (out_in, out))
        )
    ]
    for copy in copies:
        copy.start()

    def place_tile(l, ref, index, tile):
        t, r = divmod(index, CH // 8)
        ref[l, 8 * r : 8 * r + 8, LANES * t : LANES * t + LANES] = tile

    copies[0].wait()
    for l in range(2):
        for chunk in range(2 * CHUNKS):
            v = result0[l, chunk // CHUNKS, chunk % CHUNKS].astype(F32)
            for slot in range(4):
                place_tile(l, gdown, 4 * chunk + slot, v[8 * slot : 8 * slot + 8])
    copies[1].wait()
    for l in range(2):
        for chunk in range(2 * CHUNKS):
            v = result1[l, chunk // CHUNKS, chunk % CHUNKS].astype(F32)
            for slot in range(5):
                index = 5 * chunk + slot
                tile = v[8 * slot : 8 * slot + 8]
                if index < CH // 8 * 6:
                    place_tile(l, gup, index, tile)
                else:
                    place_tile(l, gdown, index - CH // 8 * 6 + DTILES, tile)
    copies[2].wait()
    for l in range(2):
        few = result2[l].reshape(LANES, LANES)
        for t in range(TAPS):
            gtaps[t, l : l + 1, :LANES] = few[t : t + 1]
            gtaps[t, l : l + 1, LANES:] = few[TAPS + t : TAPS + t + 1, :REST]
        for at, ref in ((ROW_CBIAS, gcbias), (ROW_GAIN, ggain), (ROW_SHIFT, gshift),
                        (ROW_DBIAS, gdbias), (ROW_SCALE, gscale)):
            ref[l : l + 1, :LANES] = few[at : at + 1]
            ref[l : l + 1, LANES:] = few[at + 1 : at + 2, :REST]
        for t in range(6):
            gubias[l : l + 1, LANES * t : LANES * t + LANES] = few[ROW_UBIAS + t : ROW_UBIAS + t + 1]
    copies[3].wait()
    copies[4].wait()


def on_device(features, cotangent, dw_kernel, conv_bias, ln_gain, ln_shift, up_weight, up_bias,
              down_weight, down_bias, layer_scale):
    depth = dw_kernel.shape[0]
    pixel_total = PX * lax.axis_size("slide") * lax.axis_size("ty") * lax.axis_size("tx")
    place, edges, spread = (jnp.asarray(v, BF16) for v in one_hots())
    taps = dw_kernel.reshape(depth, TAPS, CH).transpose(1, 0, 2)
    vmem = pl.BlockSpec(memory_space=pltpu.VMEM)
    dma = pltpu.SemaphoreType.DMA
    plane = (NI, TC + 6, NS, CH)
    wide = (NI + 6, WIDE, NS, LANES)
    hbm = pl.BlockSpec(memory_space=pltpu.HBM)
    results = tuple(jax.ShapeDtypeStruct((depth, 2, CHUNKS, rows, LANES), BF16) for rows in PARTS) + (
        jax.ShapeDtypeStruct((depth, CHUNKS, 8, LANES), F32),
    )
    out, gfeat, result0, result1, result2 = pl.pallas_call(
        functools.partial(kernel, 1.0 / math.sqrt(pixel_total)),
        out_shape=(
            jax.ShapeDtypeStruct((PX, CH), BF16),
            jax.ShapeDtypeStruct((PX, CH), F32),
            *results,
        ),
        in_specs=[hbm] * 3 + [vmem] * 3 + [hbm, vmem, hbm] + [vmem] * 2 + [hbm] * 3,
        out_specs=(hbm,) * 5,
        scratch_shapes=[
            pltpu.VMEM((PX, CH), BF16),
            pltpu.VMEM((PX, CH), BF16),
            pltpu.VMEM((TAPS, depth, CH), F32),
            pltpu.VMEM((depth, CH, HID), BF16),
            pltpu.VMEM((depth, CH, HID), BF16),
            pltpu.VMEM(place.shape, BF16),
            pltpu.VMEM(edges.shape, BF16),
            pltpu.VMEM(spread.shape, BF16),
            pltpu.VMEM((PX, CH), BF16),
            pltpu.VMEM((PX, CH), F32),
            *(pltpu.VMEM(v.shape, v.dtype) for v in results),
            dma((8,)), dma((8,)),
            pltpu.VMEM((2, *plane), F32),
            pltpu.VMEM(plane, F32),
            pltpu.VMEM((2, *wide), F32),
            pltpu.VMEM(wide, F32),
            pltpu.VMEM((NI, PACK, NS, LANES), F32),
            pltpu.VMEM((TC * NS, CH), F32),
            pltpu.VMEM((2, PX, CH), F32),
            pltpu.VMEM((2, PX, 1), F32),
            pltpu.VMEM((2, PX, CH), BF16),
            pltpu.VMEM((2, PX, HID), BF16),
            pltpu.VMEM((2, PX, HID), F32),
            pltpu.VMEM((2, PX, CH), F32),
            pltpu.VMEM((PX, CH), BF16),
            pltpu.VMEM((PX, HID), BF16),
            pltpu.VMEM((NI, PACK, NS, LANES), F32),
            pltpu.VMEM((2, 3, TC + 6, NS, CH), F32),
            pltpu.VMEM((2, TAPS, NS, LANES), F32),
            pltpu.VMEM((LANES, LANES), F32),
            pltpu.VMEM((PX, CH), F32),
            pltpu.VMEM((PX, CH), BF16),
            pltpu.VMEM((2, 2, TAPS, NS, LANES), F32),
            *(pltpu.VMEM((2, 2, CHUNKS, rows, LANES), F32) for rows in PARTS),
            *(pltpu.VMEM((2, CHUNKS, rows, LANES), F32) for rows in PARTS),
            *(pltpu.VMEM((2, CHUNKS, rows, LANES), BF16) for rows in PARTS),
            *(pltpu.VMEM((2, CHUNKS, rows, LANES), BF16) for rows in PARTS),
            *(pltpu.VMEM((2, NZ, rows, LANES), BF16) for rows in PARTS),
            pltpu.VMEM((2, CHUNKS, 8, LANES), F32),
            pltpu.VMEM((2, CHUNKS, 8, LANES), F32),
            pltpu.VMEM((2, 2 * NZ, 8, LANES), F32),
            pltpu.VMEM((4, 2, 3, TR, CH), BF16),
            pltpu.VMEM((4, 2, 3, TC, CH), BF16),
            pltpu.VMEM((4, 2, 3, TR, CH), BF16),
            pltpu.VMEM((4, 6, 3, TC, CH), BF16),
            dma((4, 8)), dma((4, 8)),
            dma((4,)), dma((4,)),
            dma((4, CHUNKS)), dma((4, CHUNKS)),
            dma((4, NZ)), dma((4, NZ)),
            dma((4, CHUNKS)), dma((4, CHUNKS)),
            dma((4, CHUNKS)), dma((4, CHUNKS)),
            dma((6, CHUNKS)), dma((6, CHUNKS)),
        ],
        compiler_params=pltpu.CompilerParams(
            collective_id=0, has_side_effects=True, vmem_limit_bytes=56 * 2**20
        ),
    )(
        features.reshape(PX, CH), cotangent.reshape(PX, CH), taps, conv_bias, ln_gain, ln_shift,
        up_weight, up_bias, down_weight.transpose(0, 2, 1), down_bias, layer_scale, place, edges, spread,
    )
    vector = jax.ShapeDtypeStruct((depth, CH), F32)
    weight = jax.ShapeDtypeStruct((depth, CH, HID), F32)
    out, gfeat, gtaps, gcbias, ggain, gshift, gup, gubias, gdown, gdbias, gscale = pl.pallas_call(
        unpack,
        out_shape=(
            jax.ShapeDtypeStruct((PX, CH), BF16),
            jax.ShapeDtypeStruct((PX, CH), F32),
            jax.ShapeDtypeStruct((TAPS, depth, CH), F32),
            vector, vector, vector, weight, jax.ShapeDtypeStruct((depth, HID), F32), weight, vector, vector,
        ),
        in_specs=[hbm] * 5,
        out_specs=(vmem,) * 11,
        scratch_shapes=[
            *(pltpu.VMEM(v.shape, v.dtype) for v in results),
            dma((5,)),
        ],
        compiler_params=pltpu.CompilerParams(vmem_limit_bytes=56 * 2**20),
    )(out, gfeat, result0, result1, result2)
    return (
        out.reshape(1, TR, TC, CH),
        gfeat.reshape(1, TR, TC, CH),
        gtaps.transpose(1, 0, 2).reshape(depth, SPAN, SPAN, CH),
        gcbias,
        ggain,
        gshift,
        gup,
        gubias,
        gdown.transpose(0, 2, 1),
        gdbias,
        gscale,
    )


def solution(mesh):
    tiled = P("slide", "ty", "tx", None)
    return jax.shard_map(
        on_device,
        mesh=mesh,
        in_specs=(tiled, tiled) + (P(),) * 9,
        out_specs=(tiled, tiled) + (P(),) * 9,
        check_vma=False,
    )
```

```python
import functools
import math

import jax
import jax.numpy as jnp
import numpy as np
from jax import lax
from jax.experimental import pallas as pl
from jax.experimental.pallas import tpu as pltpu
from jax.sharding import PartitionSpec as P

MESH = pl.DeviceIdType.MESH
F32 = jnp.float32
BF16 = jnp.bfloat16
ROOT_HALF = 0.7071067811865476
INV_ROOT_TAU = 0.3989422804014327
EPSILON = 1e-06

TR, TC, CH, HID = 32, 16, 192, 768
PX = TR * TC
NI, NS = 4, 8
MARGIN = 3
SPAN = 7
TAPS = SPAN * SPAN
LANES = 128
REST = CH - LANES
PACK = TC + TC // 2
WIDE = (TC + 2 * MARGIN) + (TC // 2 + 2 * MARGIN)
PARTS = (64, 16)
TILES = CH // 8 * (HID // LANES)
SMALL_AT = 8
CHUNKS = 16
NZ = 8
HALOS = ((-1, -1), (-1, 0), (-1, 1), (1, -1), (1, 0), (1, 1), (0, -1), (0, 1))

ROW_CBIAS, ROW_GAIN, ROW_SHIFT, ROW_DBIAS, ROW_SCALE, ROW_UBIAS = 98, 100, 102, 104, 106, 108


def pixel_order():
    q = np.arange(PX)
    return (4 * (q % NS) + q // (TC * NS)) * TC + (q // NS) % TC


def one_hots():
    order = pixel_order()
    place = np.zeros((PX, PX), np.float32)
    place[np.arange(PX), order] = 1.0
    inverse = np.argsort(order)
    edge_rows = np.concatenate([np.arange(3 * TC), np.arange((TR - 3) * TC, TR * TC)])
    edges = np.zeros((6 * TC, PX), np.float32)
    edges[np.arange(6 * TC), inverse[edge_rows]] = 1.0
    spread = np.zeros((2, 3, TC + 6, NS, 3, 3, TC), np.float32)
    for cc in range(TC + 6):
        source, column = (0, TC - 3 + cc) if cc < 3 else (1, cc - 3) if cc < TC + 3 else (2, cc - TC - 3)
        for u in range(3):
            spread[0, u, cc, 0, source, u, column] = 1.0
            spread[1, u, cc, NS - 1, source, u, column] = 1.0
    spread = spread.reshape(2, 3 * (TC + 6) * NS, 9 * TC)
    return place, edges, spread


def tn(a, b):
    return lax.dot_general(a, b, (((0,), (0,)), ((), ())), preferred_element_type=F32)


def nt(a, b):
    return lax.dot_general(a, b, (((1,), (1,)), ((), ())), preferred_element_type=F32)


def nn(a, b):
    return jnp.dot(a, b, preferred_element_type=F32)


def kernel(
    factor,
    feat_in, cot_in, dw_in, cbias, gain, shift, up_in, ubias, down_in, dbias, scale, place_in, edges_in, spread_in,
    out_to, gfeat_to, result0_to, result1_to,
    feat, cot, dw, up, down, place, edges, spread, out_ref, gfeat_ref, result0, result1, ins, outs,
    xp, gx, qa, qg, cbuf, convs, unit, inv, normed, act, slope, branch, gbr, gpre, gcp, tq, taps, small,
    grad, outq, wexp,
    pay0, pay1, core0, core1, sbuf0, sbuf1, rbuf0, rbuf1, zbuf0, zbuf1,
    csend, rsend, crecv, rrecv,
    hs, hr, cs, cr, xs, xr, zs, zr, gs, gr, ls, lr,
):
    yh = lax.axis_index("slide")
    ty = lax.axis_index("ty")
    tx = lax.axis_index("tx")
    core = lax.rem(tx, 2)
    yl = lax.rem(lax.div(tx, 2), 2)
    z = lax.div(tx, 4)
    other = 1 - core
    me = ty * 4 + yh * 2 + yl
    sibling = (yh, ty, z * 4 + yl * 2 + other)

    def plane_peer(d):
        py = lax.rem(ty + lax.div(d, 4), 4)
        ph = lax.rem(yh + lax.rem(lax.div(d, 2), 2), 2)
        pl_ = lax.rem(yl + lax.rem(d, 2), 2)
        return py * 4 + ph * 2 + pl_, (ph, py, z * 4 + pl_ * 2 + core)

    def z_peer(d):
        pz = lax.rem(z + d, NZ)
        return pz, (yh, ty, pz * 4 + yl * 2 + core)

    barrier = pltpu.get_barrier_semaphore()

    def greet(device):
        pl.semaphore_signal(barrier, inc=1, device_id=device, device_id_type=MESH)

    for dy, dx in HALOS:
        greet((yh, lax.rem(ty + dy + 4, 4), lax.rem(tx + dx + 32, 32)))
    greet(sibling)

    @pl.loop(1, CHUNKS)
    def _(d):
        greet(plane_peer(d)[1])

    @pl.loop(1, NZ)
    def _(d):
        greet(z_peer(d)[1])

    arrivals = {}
    loads = ((feat_in, feat), (place_in, place), (edges_in, edges), (cot_in, cot), (dw_in, dw), (spread_in, spread),
             (up_in, up), (down_in, down))
    for k, (src, dst) in enumerate(loads):
        arrivals[id(dst)] = pltpu.make_async_copy(src, dst, ins.at[k])
        arrivals[id(dst)].start()

    def ready(*refs):
        for ref in refs:
            arrivals[id(ref)].wait()

    def leave(k, src, dst):
        return pltpu.make_async_copy(src, dst, outs.at[k])

    def there(dy, dx):
        flags = []
        if dy:
            flags.append(jnp.logical_and(ty + dy >= 0, ty + dy < 4))
        if dx:
            flags.append(jnp.logical_and(tx + dx >= 0, tx + dx < 32))
        return functools.reduce(jnp.logical_and, flags)

    def halo_copy(n, dy, dx):
        if dy == 0:
            slot = 6 if dx > 0 else 7
            src, dst = csend.at[n, 0 if dx < 0 else 1], crecv.at[n, slot - 6]
        else:
            slot = (1 if dy > 0 else 4) - dx
            src, dst = rsend.at[n, 0 if dy < 0 else 1], rrecv.at[n, slot]
        return pltpu.make_async_remote_copy(
            src_ref=src, dst_ref=dst, send_sem=hs.at[n, slot], recv_sem=hr.at[n, slot],
            device_id=(yh, ty + dy, tx + dx), device_id_type=MESH,
        )

    def halo_start(n, plane):
        flat = jnp.concatenate([plane[i, 3 : 3 + TC].reshape(TC * NS, CH) for i in range(NI)], axis=0)
        strips = nn(edges[...], flat.astype(BF16)).astype(BF16)
        rsend[n] = strips.reshape(2, 3, TC, CH)
        for c in range(3):
            csend[n, 0, c] = plane[:, 3 + c].reshape(TR, CH).astype(BF16)
            csend[n, 1, c] = plane[:, TC + c].reshape(TR, CH).astype(BF16)
        if n == 0:
            pl.semaphore_wait(barrier, 8 + 1 + CHUNKS - 1 + NZ - 1)
        for dy, dx in HALOS:

            @pl.when(there(dy, dx))
            def _(dy=dy, dx=dx):
                halo_copy(n, dy, dx).start()

    def halo_wait(n):
        for dy, dx in HALOS:

            @pl.when(there(-dy, -dx))
            def _(dy=dy, dx=dx):
                halo_copy(n, dy, dx).wait_recv()

            @pl.when(jnp.logical_not(there(-dy, -dx)))
            def _(dy=dy, dx=dx):
                if dy == 0:
                    crecv[n, 0 if dx > 0 else 1] = jnp.zeros((3, TR, CH), BF16)
                else:
                    rrecv[n, (1 if dy > 0 else 4) - dx] = jnp.zeros((3, TC, CH), BF16)

    def halo_done(n):
        for dy, dx in HALOS:

            @pl.when(there(dy, dx))
            def _(dy=dy, dx=dx):
                halo_copy(n, dy, dx).wait_send()

    def assemble(n, plane, q):
        for c in range(3):
            plane[:, c] = crecv[n, 0, c].astype(F32).reshape(NI, NS, CH)
            plane[:, TC + 3 + c] = crecv[n, 1, c].astype(F32).reshape(NI, NS, CH)
        for side in range(2):
            strips = jnp.concatenate([rrecv[n, 3 * side + k].reshape(3 * TC, CH) for k in range(3)], axis=0)
            tq[side] = nn(spread[side], strips).reshape(3, TC + 6, NS, CH)
        row = lax.broadcasted_iota(jnp.int32, (3, NS, LANES), 1)

        def fill(slot, mid, top, low):
            q[3:7, slot] = mid
            q[0:3, slot] = jnp.where(row == 0, top, pltpu.roll(mid[1:4], 1, 1))
            q[7:10, slot] = jnp.where(row == NS - 1, low, pltpu.roll(mid[0:3], NS - 1, 1))

        @pl.loop(0, TC + 6)
        def _(cc):
            fill(cc, plane[:, cc, :, :LANES], tq[0, :, cc, :, :LANES], tq[1, :, cc, :, :LANES])

        def pair(ref, *at):
            return jnp.concatenate([ref[(*at[:-1], at[-1], slice(None), slice(LANES, CH))],
                                    ref[(*at[:-1], at[-1] + 8, slice(None), slice(LANES, CH))]], axis=-1)

        @pl.loop(0, TC // 2 + 6)
        def _(k):
            fill(TC + 6 + k, pair(plane, slice(None), k), pair(tq, 0, slice(None), k), pair(tq, 1, slice(None), k))

    def convolve(q, l, flip):
        def columns(part, t, base):
            sums = [[None, None] for _ in range(NI)]
            for j2 in range(SPAN + 1):
                for r in range(NI + SPAN - 1):
                    x = q[r, base + j2]
                    for i in range(NI):
                        if not 0 <= r - i < SPAN:
                            continue
                        for o in range(2):
                            if not 0 <= j2 - o < SPAN:
                                continue
                            tap = (r - i) * SPAN + j2 - o
                            term = x * wexp[l, part, TAPS - 1 - tap if flip else tap]
                            sums[i][o] = term if sums[i][o] is None else sums[i][o] + term
            for i in range(NI):
                for o in range(2):
                    cbuf[i, t + o] = sums[i][o]

        @pl.loop(0, TC // 2)
        def _(k):
            columns(0, 2 * k, 2 * k)

        @pl.loop(0, TC // 4)
        def _(k):
            columns(1, TC + 2 * k, TC + 6 + 2 * k)

    def conv_rows(i):
        half = TC * NS // 2
        conv = convs.at[i]
        conv[:, :LANES] = cbuf[i, :TC].reshape(TC * NS, LANES)
        rest = cbuf[i, TC:].reshape(half, LANES)
        conv[:half, LANES:] = rest[:, :REST]
        conv[half:, LANES:] = rest[:, REST:]
        return conv[...]

    blk = TC * NS

    def rows_of(i):
        return pl.ds(pl.multiple_of(i * blk, blk), blk)

    def forward(l, plane, into, i):
        c = conv_rows(i) + cbias[l : l + 1]
        mid = c - jnp.mean(c, axis=1, keepdims=True)
        rstd = lax.rsqrt(jnp.mean(mid * mid, axis=1, keepdims=True) + EPSILON)
        u = mid * rstd
        rows = rows_of(i)
        unit[l, rows] = u
        inv[l, rows] = rstd
        nb = (u * gain[l : l + 1] + shift[l : l + 1]).astype(BF16)
        normed[l, rows] = nb
        pre = nn(nb, up[l]) + ubias[l : l + 1]
        cdf = 0.5 * (1.0 + lax.erf(pre * ROOT_HALF))
        slope[l, rows] = cdf + pre * INV_ROOT_TAU * jnp.exp(-0.5 * pre * pre)
        ab = (pre * cdf).astype(BF16)
        act[l, rows] = ab
        br = nt(ab, down[l]) + dbias[l : l + 1]
        branch[l, rows] = br
        before = plane[i, 3 : 3 + TC].reshape(blk, CH)
        new = (before + scale[l : l + 1] * br).astype(BF16)
        into(i, new)

    def fold(v):
        return jnp.sum(v.reshape(blk // 8, 8, v.shape[1]), axis=0)

    def branch_grads(l):
        def body(i, sums):
            rows = rows_of(i)
            g = grad[rows]
            gb = (g * scale[l : l + 1]).astype(BF16)
            gbr[rows] = gb
            return sums[0] + fold(gb.astype(F32)), sums[1] + fold(g * branch[l, rows])

        return lax.fori_loop(0, NI, body, (jnp.zeros((8, CH), F32),) * 2, unroll=True)

    def pre_grads(l):
        def body(i, total):
            rows = rows_of(i)
            gp = (nn(gbr[rows], down[l]) * slope[l, rows]).astype(BF16)
            gpre[rows] = gp
            return total + fold(gp.astype(F32))

        return lax.fori_loop(0, NI, body, jnp.zeros((8, HID), F32), unroll=True)

    def backward(l):
        def body(i, sums):
            rows = rows_of(i)
            s_gain, s_shift, s_cbias = sums
            gn = nt(gpre[rows], up[l])
            u = unit[l, rows]
            s_gain = s_gain + fold(gn * u)
            s_shift = s_shift + fold(gn)
            q = gn * gain[l : l + 1]
            centred = q - jnp.mean(q, axis=1, keepdims=True) - u * jnp.mean(q * u, axis=1, keepdims=True)
            gc = (inv[l, rows] * centred).astype(BF16).astype(F32)
            s_cbias = s_cbias + fold(gc)
            gx[i, 3 : 3 + TC] = gc.reshape(TC, NS, CH)
            gcp[i, :TC] = gc[:, :LANES].reshape(TC, NS, LANES)
            half = blk // 2
            gcp[i, TC:, :, :REST] = gc[:half, LANES:].reshape(TC // 2, NS, REST)
            gcp[i, TC:, :, REST:] = gc[half:, LANES:].reshape(TC // 2, NS, REST)
            return s_gain, s_shift, s_cbias

        zero = jnp.zeros((8, CH), F32)
        return lax.fori_loop(0, NI, body, (zero, zero, zero), unroll=True)

    def put(l, index, tile):
        if index < 256:
            chunk, slot = divmod(index, 8)
            pay0[l, chunk // CHUNKS, chunk % CHUNKS, 8 * slot : 8 * slot + 8] = tile
        else:
            chunk = index - 256
            pay1[l, chunk // CHUNKS, chunk % CHUNKS, :8] = tile

    def weight_tiles(a, b, store):
        for t in range(3):
            part = tn(a[...], b[:, 256 * t : 256 * t + 256])
            for v in range(2):
                for r in range(CH // 8):
                    store((2 * t + v) * (CH // 8) + r, part[8 * r : 8 * r + 8, LANES * v : LANES * v + LANES])

    def down_grads(l):
        weight_tiles(gbr, act.at[l], lambda index, tile: put(l, index, tile))

    def up_grads(l):
        weight_tiles(normed.at[l], gpre, lambda index, tile: put(l, TILES + index, tile))

    def tap_grads(l):
        for part, (cols, base, first) in enumerate(((TC, 0, 0), (TC // 2, TC + 6, TC))):

            @pl.loop(0, SPAN)
            def _(j):
                def body(c, sums):
                    sums = list(sums)
                    for o in range(2):
                        col = 2 * c + o
                        gcs = [gcp[i, first + col] for i in range(NI)]
                        for r in range(NI + SPAN - 1):
                            x = qa[l, r, base + col + j]
                            for i in range(NI):
                                if 0 <= r - i < SPAN:
                                    sums[r - i] = sums[r - i] + gcs[i] * x
                    return tuple(sums)

                zero = jnp.zeros((NS, LANES), F32)
                sums = lax.fori_loop(0, cols // 2, body, (zero,) * SPAN)
                for r in range(SPAN):
                    taps[part, r * SPAN + j] = sums[r]

    def small_grads(l, early, s_ubias, sums):
        s_dbias, s_scale = early
        s_gain, s_shift, s_cbias = sums
        small[...] = jnp.zeros((LANES, LANES), F32)
        small[:TAPS] = jnp.sum(taps[0], axis=1)
        rest = jnp.sum(taps[1], axis=1)
        small[TAPS : 2 * TAPS, :REST] = rest[:, :REST] + rest[:, REST:]
        for at, v in ((ROW_CBIAS, s_cbias), (ROW_GAIN, s_gain), (ROW_SHIFT, s_shift),
                      (ROW_DBIAS, s_dbias), (ROW_SCALE, s_scale)):
            v = jnp.sum(v, axis=0, keepdims=True)
            small[at : at + 1] = v[:, :LANES]
            small[at + 1 : at + 2, :REST] = v[:, LANES:]
        v = jnp.sum(s_ubias, axis=0, keepdims=True)
        for t in range(6):
            small[ROW_UBIAS + t : ROW_UBIAS + t + 1] = v[:, LANES * t : LANES * t + LANES]
        upper = lax.broadcasted_iota(jnp.int32, (8, LANES), 0) < 4
        for k in range(2 * CHUNKS):
            v = small[8 * (k // 2) : 8 * (k // 2) + 8]
            if k % 2:
                v = pltpu.roll(v, 4, 0)
            pay1[l, k // CHUNKS, k % CHUNKS, SMALL_AT:] = jnp.where(upper, v, 0.0)

    upper = lax.broadcasted_iota(jnp.int32, (8, LANES), 0) < 4

    def rounded(v, part):
        if part == 0:
            return v.astype(BF16)
        s = v[SMALL_AT:]
        s = s + pltpu.roll(s, 4, 0)
        high = s.astype(BF16).astype(F32)
        return jnp.concatenate([v[:SMALL_AT], jnp.where(upper, high, s - high)], axis=0).astype(BF16)

    pays, cores, sbufs, rbufs, zbufs = (pay0, pay1), (core0, core1), (sbuf0, sbuf1), (rbuf0, rbuf1), (zbuf0, zbuf1)
    results = (result0, result1)

    def core_copy(l, p):
        return pltpu.make_async_remote_copy(
            src_ref=pays[p].at[l, other], dst_ref=cores[p].at[l], send_sem=cs.at[2 * l + p], recv_sem=cr.at[2 * l + p],
            device_id=sibling, device_id_type=MESH,
        )

    def plane_copy(l, p, d):
        index, device = plane_peer(d)
        return pltpu.make_async_remote_copy(
            src_ref=sbufs[p].at[l, index], dst_ref=rbufs[p].at[l, d], send_sem=xs.at[2 * l + p, d], recv_sem=xr.at[2 * l + p, d],
            device_id=device, device_id_type=MESH,
        )

    def z_copy(l, p, d):
        return pltpu.make_async_remote_copy(
            src_ref=zbufs[p].at[l, z], dst_ref=zbufs[p].at[l, z], send_sem=zs.at[2 * l + p, d], recv_sem=zr.at[2 * l + p, z],
            device_id=z_peer(d)[1], device_id_type=MESH,
        )

    def z_arrival(l, p, d):
        pz, device = z_peer(d)
        return pltpu.make_async_remote_copy(
            src_ref=zbufs[p].at[l, pz], dst_ref=zbufs[p].at[l, pz], send_sem=zs.at[2 * l + p, d], recv_sem=zr.at[2 * l + p, pz],
            device_id=device, device_id_type=MESH,
        )

    def gather_copy(l, p, d):
        return pltpu.make_async_remote_copy(
            src_ref=results[p].at[l, core, me], dst_ref=results[p].at[l, core, me], send_sem=gs.at[2 * l + p, d],
            recv_sem=gr.at[2 * l + p, me], device_id=plane_peer(d)[1], device_id_type=MESH,
        )

    def gather_arrival(l, p, d):
        index, device = plane_peer(d)
        return pltpu.make_async_remote_copy(
            src_ref=results[p].at[l, core, index], dst_ref=results[p].at[l, core, index], send_sem=gs.at[2 * l + p, d],
            recv_sem=gr.at[2 * l + p, index], device_id=device, device_id_type=MESH,
        )

    def relay_copy(l, p, index):
        return pltpu.make_async_remote_copy(
            src_ref=results[p].at[l, core, index], dst_ref=results[p].at[l, core, index], send_sem=ls.at[2 * l + p, index],
            recv_sem=lr.at[2 * l + p, index], device_id=sibling, device_id_type=MESH,
        )

    def relay_arrival(l, p, index):
        return pltpu.make_async_remote_copy(
            src_ref=results[p].at[l, other, index], dst_ref=results[p].at[l, other, index], send_sem=ls.at[2 * l + p, index],
            recv_sem=lr.at[2 * l + p, index], device_id=sibling, device_id_type=MESH,
        )

    def to_plane(l, p):
        core_copy(l, p).wait_recv()

        @pl.loop(0, CHUNKS)
        def _(k):
            d = lax.rem(k + 1, CHUNKS)
            index, _ = plane_peer(d)
            v = pays[p][l, core, index] + cores[p][l, index]
            sbufs[p][l, index] = rounded(v, p)

            @pl.when(d > 0)
            def _():
                plane_copy(l, p, d).start()

    def to_z(l, p):
        @pl.loop(1, CHUNKS)
        def _(d):
            plane_copy(l, p, d).wait_recv()

        v = lax.fori_loop(1, CHUNKS, lambda d, v: v + rbufs[p][l, d].astype(F32), sbufs[p][l, me].astype(F32))
        zbufs[p][l, z] = rounded(v, p)

        @pl.loop(1, NZ)
        def _(d):
            z_copy(l, p, d).start()

    def to_all(l, p):
        @pl.loop(1, NZ)
        def _(d):
            z_arrival(l, p, d).wait_recv()

        v = zbufs[p][l, 0].astype(F32)
        for k in range(1, NZ):
            v = v + zbufs[p][l, k].astype(F32)
        results[p][l, core, me] = rounded(v * factor, p)

        @pl.loop(1, CHUNKS)
        def _(d):
            gather_copy(l, p, d).start()

        relay_copy(l, p, me).start()

    def to_sibling(l, p):
        @pl.loop(1, CHUNKS)
        def _(d):
            gather_arrival(l, p, d).wait_recv()
            relay_copy(l, p, plane_peer(d)[0]).start()

    def finish(l, p):
        @pl.loop(0, CHUNKS)
        def _(k):
            relay_arrival(l, p, k).wait_recv()
            relay_copy(l, p, k).wait_send()

        core_copy(l, p).wait_send()

        @pl.loop(1, CHUNKS)
        def _(d):
            plane_copy(l, p, d).wait_send()
            gather_copy(l, p, d).wait_send()

        @pl.loop(1, NZ)
        def _(d):
            z_copy(l, p, d).wait_send()


    def flat_rows(plane, i):
        return plane[i, 3 : 3 + TC].reshape(blk, CH)

    def step_back(l):
        @pl.loop(0, NI)
        def _(i):
            rows = rows_of(i)
            grad[rows] = grad[rows] + conv_rows(i)

    ready(feat, place, edges)
    xp[0, :, 3 : 3 + TC] = nn(place[...], feat[...]).reshape(NI, TC, NS, CH)
    halo_start(0, xp.at[0])
    ready(cot, dw, spread)
    grad[...] = nn(place[...], cot[...])

    @pl.loop(0, TAPS)
    def _(t):
        for l in range(2):
            tap = dw[t, l : l + 1]
            rest = tap[:, LANES:]
            wexp[l, 0, t] = jnp.broadcast_to(tap[:, :LANES], (NS, LANES))
            wexp[l, 1, t] = jnp.broadcast_to(jnp.concatenate([rest, rest], axis=1), (NS, LANES))

    halo_wait(0)
    assemble(0, xp.at[0], qa.at[0])
    convolve(qa.at[0], 0, False)
    ready(up, down)

    def keep(i, new):
        xp[1, i, 3 : 3 + TC] = new.astype(F32).reshape(TC, NS, CH)

    @pl.loop(0, NI, unroll=2)
    def _(i):
        forward(0, xp.at[0], keep, i)

    halo_start(1, xp.at[1])
    halo_wait(1)
    assemble(1, xp.at[1], qa.at[1])
    convolve(qa.at[1], 1, False)

    def keep_out(i, new):
        outq[rows_of(i)] = new

    @pl.loop(0, NI, unroll=2)
    def _(i):
        forward(1, xp.at[1], keep_out, i)

    def leave_all(l):
        return [leave(2 * l + k, v.at[l], to.at[l]) for k, (v, to) in enumerate(
            ((result0, result0_to), (result1, result1_to)))]

    early = branch_grads(1)
    s_ubias = pre_grads(1)
    down_grads(1)
    up_grads(1)
    core_copy(1, 0).start()
    sums = backward(1)
    halo_start(2, gx)
    to_plane(1, 0)
    tap_grads(1)
    small_grads(1, early, s_ubias, sums)
    core_copy(1, 1).start()
    halo_wait(2)
    assemble(2, gx, qg)
    to_plane(1, 1)
    convolve(qg, 1, True)
    to_z(1, 0)
    step_back(1)
    early = branch_grads(0)
    s_ubias = pre_grads(0)
    down_grads(0)
    up_grads(0)
    core_copy(0, 0).start()
    to_z(1, 1)
    sums = backward(0)
    halo_start(3, gx)
    to_plane(0, 0)
    to_all(1, 0)
    tap_grads(0)
    small_grads(0, early, s_ubias, sums)
    core_copy(0, 1).start()
    to_all(1, 1)
    halo_wait(3)
    assemble(3, gx, qg)
    to_z(0, 0)
    to_plane(0, 1)
    convolve(qg, 0, True)
    step_back(0)
    to_sibling(1, 0)
    to_all(0, 0)
    to_z(0, 1)
    g = grad[...]
    high = g.astype(BF16)
    g = g - high.astype(F32)
    mid = g.astype(BF16)
    low = (g - mid.astype(F32)).astype(BF16)
    gfeat_ref[...] = tn(place[...], high) + (tn(place[...], mid) + tn(place[...], low))
    leave(4, gfeat_ref, gfeat_to).start()
    to_sibling(1, 1)
    out_ref[...] = tn(place[...], outq[...]).astype(BF16)
    leave(5, out_ref, out_to).start()
    to_all(0, 1)
    to_sibling(0, 0)
    for p in range(2):
        finish(1, p)
    for copy in leave_all(1):
        copy.start()
    for n in range(4):
        halo_done(n)
    to_sibling(0, 1)
    for p in range(2):
        finish(0, p)
    for copy in leave_all(0):
        copy.start()
    for copy in leave_all(0) + leave_all(1):
        copy.wait()
    leave(4, gfeat_ref, gfeat_to).wait()
    leave(5, out_ref, out_to).wait()


def unpack(out_in, gfeat_in, result0_in, result1_in,
           out, gfeat, gtaps, gcbias, ggain, gshift, gup, gubias, gdown, gdbias, gscale,
           few, result0, result1, ins):
    copies = [
        pltpu.make_async_copy(src, dst, ins.at[k])
        for k, (src, dst) in enumerate(
            ((result0_in, result0), (result1_in, result1), (gfeat_in, gfeat), (out_in, out))
        )
    ]
    for copy in copies:
        copy.start()
    upper = lax.broadcasted_iota(jnp.int32, (8, LANES), 0) < 4

    def place_tile(l, ref, index, tile):
        t, r = divmod(index, CH // 8)
        ref[l, 8 * r : 8 * r + 8, LANES * t : LANES * t + LANES] = tile

    def place_any(l, index, tile):
        if index < TILES:
            place_tile(l, gdown, index, tile)
        else:
            place_tile(l, gup, index - TILES, tile)

    copies[0].wait()
    for l in range(2):
        for chunk in range(2 * CHUNKS):
            v = result0[l, chunk // CHUNKS, chunk % CHUNKS].astype(F32)
            for slot in range(8):
                place_any(l, 8 * chunk + slot, v[8 * slot : 8 * slot + 8])
    copies[1].wait()
    for l in range(2):
        pair = []
        for chunk in range(2 * CHUNKS):
            v = result1[l, chunk // CHUNKS, chunk % CHUNKS].astype(F32)
            place_any(l, 256 + chunk, v[:8])
            v = v[SMALL_AT:]
            pair.append(v + pltpu.roll(v, 4, 0))
            if chunk % 2:
                few[4 * chunk - 4 : 4 * chunk + 4] = jnp.where(upper, pair[-2], pair[-1])
        for t in range(TAPS):
            gtaps[t, l : l + 1, :LANES] = few[t : t + 1]
            gtaps[t, l : l + 1, LANES:] = few[TAPS + t : TAPS + t + 1, :REST]
        for at, ref in ((ROW_CBIAS, gcbias), (ROW_GAIN, ggain), (ROW_SHIFT, gshift),
                        (ROW_DBIAS, gdbias), (ROW_SCALE, gscale)):
            ref[l : l + 1, :LANES] = few[at : at + 1]
            ref[l : l + 1, LANES:] = few[at + 1 : at + 2, :REST]
        for t in range(6):
            gubias[l : l + 1, LANES * t : LANES * t + LANES] = few[ROW_UBIAS + t : ROW_UBIAS + t + 1]
    copies[2].wait()
    copies[3].wait()


def on_device(features, cotangent, dw_kernel, conv_bias, ln_gain, ln_shift, up_weight, up_bias,
              down_weight, down_bias, layer_scale):
    depth = dw_kernel.shape[0]
    pixel_total = PX * lax.axis_size("slide") * lax.axis_size("ty") * lax.axis_size("tx")
    place, edges, spread = (jnp.asarray(v, BF16) for v in one_hots())
    taps = dw_kernel.reshape(depth, TAPS, CH).transpose(1, 0, 2)
    vmem = pl.BlockSpec(memory_space=pltpu.VMEM)
    dma = pltpu.SemaphoreType.DMA
    plane = (NI, TC + 6, NS, CH)
    wide = (NI + 6, WIDE, NS, LANES)
    hbm = pl.BlockSpec(memory_space=pltpu.HBM)
    results = tuple(jax.ShapeDtypeStruct((depth, 2, CHUNKS, rows, LANES), BF16) for rows in PARTS)
    out, gfeat, result0, result1 = pl.pallas_call(
        functools.partial(kernel, 1.0 / math.sqrt(pixel_total)),
        out_shape=(
            jax.ShapeDtypeStruct((PX, CH), BF16),
            jax.ShapeDtypeStruct((PX, CH), F32),
            *results,
        ),
        in_specs=[hbm] * 3 + [vmem] * 3 + [hbm, vmem, hbm] + [vmem] * 2 + [hbm] * 3,
        out_specs=(hbm,) * 4,
        scratch_shapes=[
            pltpu.VMEM((PX, CH), BF16),
            pltpu.VMEM((PX, CH), BF16),
            pltpu.VMEM((TAPS, depth, CH), F32),
            pltpu.VMEM((depth, CH, HID), BF16),
            pltpu.VMEM((depth, CH, HID), BF16),
            pltpu.VMEM(place.shape, BF16),
            pltpu.VMEM(edges.shape, BF16),
            pltpu.VMEM(spread.shape, BF16),
            pltpu.VMEM((PX, CH), BF16),
            pltpu.VMEM((PX, CH), F32),
            *(pltpu.VMEM(v.shape, v.dtype) for v in results),
            dma((8,)), dma((6,)),
            pltpu.VMEM((2, *plane), F32),
            pltpu.VMEM(plane, F32),
            pltpu.VMEM((2, *wide), F32),
            pltpu.VMEM(wide, F32),
            pltpu.VMEM((NI, PACK, NS, LANES), F32),
            pltpu.VMEM((NI, TC * NS, CH), F32),
            pltpu.VMEM((2, PX, CH), F32),
            pltpu.VMEM((2, PX, 1), F32),
            pltpu.VMEM((2, PX, CH), BF16),
            pltpu.VMEM((2, PX, HID), BF16),
            pltpu.VMEM((2, PX, HID), F32),
            pltpu.VMEM((2, PX, CH), F32),
            pltpu.VMEM((PX, CH), BF16),
            pltpu.VMEM((PX, HID), BF16),
            pltpu.VMEM((NI, PACK, NS, LANES), F32),
            pltpu.VMEM((2, 3, TC + 6, NS, CH), F32),
            pltpu.VMEM((2, TAPS, NS, LANES), F32),
            pltpu.VMEM((LANES, LANES), F32),
            pltpu.VMEM((PX, CH), F32),
            pltpu.VMEM((PX, CH), BF16),
            pltpu.VMEM((2, 2, TAPS, NS, LANES), F32),
            *(pltpu.VMEM((2, 2, CHUNKS, rows, LANES), F32) for rows in PARTS),
            *(pltpu.VMEM((2, CHUNKS, rows, LANES), F32) for rows in PARTS),
            *(pltpu.VMEM((2, CHUNKS, rows, LANES), BF16) for rows in PARTS),
            *(pltpu.VMEM((2, CHUNKS, rows, LANES), BF16) for rows in PARTS),
            *(pltpu.VMEM((2, NZ, rows, LANES), BF16) for rows in PARTS),
            pltpu.VMEM((4, 2, 3, TR, CH), BF16),
            pltpu.VMEM((4, 2, 3, TC, CH), BF16),
            pltpu.VMEM((4, 2, 3, TR, CH), BF16),
            pltpu.VMEM((4, 6, 3, TC, CH), BF16),
            dma((4, 8)), dma((4, 8)),
            dma((4,)), dma((4,)),
            dma((4, CHUNKS)), dma((4, CHUNKS)),
            dma((4, NZ)), dma((4, NZ)),
            dma((4, CHUNKS)), dma((4, CHUNKS)),
            dma((4, CHUNKS)), dma((4, CHUNKS)),
        ],
        compiler_params=pltpu.CompilerParams(
            collective_id=0, has_side_effects=True, vmem_limit_bytes=56 * 2**20
        ),
    )(
        features.reshape(PX, CH), cotangent.reshape(PX, CH), taps, conv_bias, ln_gain, ln_shift,
        up_weight, up_bias, down_weight.transpose(0, 2, 1), down_bias, layer_scale, place, edges, spread,
    )
    vector = jax.ShapeDtypeStruct((depth, CH), F32)
    weight = jax.ShapeDtypeStruct((depth, CH, HID), F32)
    out, gfeat, gtaps, gcbias, ggain, gshift, gup, gubias, gdown, gdbias, gscale = pl.pallas_call(
        unpack,
        out_shape=(
            jax.ShapeDtypeStruct((PX, CH), BF16),
            jax.ShapeDtypeStruct((PX, CH), F32),
            jax.ShapeDtypeStruct((TAPS, depth, CH), F32),
            vector, vector, vector, weight, jax.ShapeDtypeStruct((depth, HID), F32), weight, vector, vector,
        ),
        in_specs=[hbm] * 4,
        out_specs=(vmem,) * 11,
        scratch_shapes=[
            pltpu.VMEM((LANES, LANES), F32),
            *(pltpu.VMEM(v.shape, v.dtype) for v in results),
            dma((4,)),
        ],
        compiler_params=pltpu.CompilerParams(vmem_limit_bytes=56 * 2**20),
    )(out, gfeat, result0, result1)
    return (
        out.reshape(1, TR, TC, CH),
        gfeat.reshape(1, TR, TC, CH),
        gtaps.transpose(1, 0, 2).reshape(depth, SPAN, SPAN, CH),
        gcbias,
        ggain,
        gshift,
        gup,
        gubias,
        gdown.transpose(0, 2, 1),
        gdbias,
        gscale,
    )


def solution(mesh):
    tiled = P("slide", "ty", "tx", None)
    return jax.shard_map(
        on_device,
        mesh=mesh,
        in_specs=(tiled, tiled) + (P(),) * 9,
        out_specs=(tiled, tiled) + (P(),) * 9,
        check_vma=False,
    )
```

```python
import functools
import math

import jax
import jax.numpy as jnp
import numpy as np
from jax import lax
from jax.experimental import pallas as pl
from jax.experimental.pallas import tpu as pltpu
from jax.sharding import PartitionSpec as P

MESH = pl.DeviceIdType.MESH
F32 = jnp.float32
BF16 = jnp.bfloat16
ROOT_HALF = 0.7071067811865476
INV_ROOT_TAU = 0.3989422804014327
EPSILON = 1e-06

TR, TC, CH, HID = 32, 16, 192, 768
PX = TR * TC
NI, NS = 4, 8
MARGIN = 3
SPAN = 7
TAPS = SPAN * SPAN
LANES = 128
REST = CH - LANES
PACK = TC + TC // 2
WIDE = (TC + 2 * MARGIN) + (TC // 2 + 2 * MARGIN)
PARTS = (64, 16)
TILES = CH // 8 * (HID // LANES)
SMALL_AT = 8
CHUNKS = 16
NZ = 8
HALOS = ((-1, -1), (-1, 0), (-1, 1), (1, -1), (1, 0), (1, 1), (0, -1), (0, 1))

ROW_CBIAS, ROW_GAIN, ROW_SHIFT, ROW_DBIAS, ROW_SCALE, ROW_UBIAS = 98, 100, 102, 104, 106, 108


def pixel_order():
    q = np.arange(PX)
    return (4 * (q % NS) + q // (TC * NS)) * TC + (q // NS) % TC


def one_hots():
    order = pixel_order()
    place = np.zeros((PX, PX), np.float32)
    place[np.arange(PX), order] = 1.0
    inverse = np.argsort(order)
    edge_rows = np.concatenate([np.arange(3 * TC), np.arange((TR - 3) * TC, TR * TC)])
    edges = np.zeros((6 * TC, PX), np.float32)
    edges[np.arange(6 * TC), inverse[edge_rows]] = 1.0
    spread = np.zeros((2, 3, TC + 6, NS, 3, 3, TC), np.float32)
    for cc in range(TC + 6):
        source, column = (0, TC - 3 + cc) if cc < 3 else (1, cc - 3) if cc < TC + 3 else (2, cc - TC - 3)
        for u in range(3):
            spread[0, u, cc, 0, source, u, column] = 1.0
            spread[1, u, cc, NS - 1, source, u, column] = 1.0
    spread = spread.reshape(2, 3 * (TC + 6) * NS, 9 * TC)
    return place, edges, spread


def tn(a, b):
    return lax.dot_general(a, b, (((0,), (0,)), ((), ())), preferred_element_type=F32)


def nt(a, b):
    return lax.dot_general(a, b, (((1,), (1,)), ((), ())), preferred_element_type=F32)


def nn(a, b):
    return jnp.dot(a, b, preferred_element_type=F32)


def kernel(
    factor,
    feat_in, cot_in, dw_in, cbias, gain, shift, up_in, ubias, down_in, dbias, scale, place_in, edges_in, spread_in,
    out_to, gfeat_to, result0_to, result1_to,
    feat, cot, dw, up, down, place, edges, spread, out_ref, gfeat_ref, result0, result1, ins, outs,
    xp, gx, qa, qg, cbuf, convs, unit, inv, normed, act, slope, branch, gbr, gpre, gcp, tq, taps, small,
    grad, outq, wexp,
    pay0, pay1, core0, core1, sbuf0, sbuf1, rbuf0, rbuf1, zbuf0, zbuf1,
    csend, rsend, crecv, rrecv,
    hs, hr, cs, cr, xs, xr, zs, zr, gs, gr, ls, lr,
):
    yh = lax.axis_index("slide")
    ty = lax.axis_index("ty")
    tx = lax.axis_index("tx")
    core = lax.rem(tx, 2)
    yl = lax.rem(lax.div(tx, 2), 2)
    z = lax.div(tx, 4)
    other = 1 - core
    me = ty * 4 + yh * 2 + yl
    sibling = (yh, ty, z * 4 + yl * 2 + other)

    def plane_peer(d):
        py = lax.rem(ty + lax.div(d, 4), 4)
        ph = lax.rem(yh + lax.rem(lax.div(d, 2), 2), 2)
        pl_ = lax.rem(yl + lax.rem(d, 2), 2)
        return py * 4 + ph * 2 + pl_, (ph, py, z * 4 + pl_ * 2 + core)

    def z_peer(d):
        pz = lax.rem(z + d, NZ)
        return pz, (yh, ty, pz * 4 + yl * 2 + core)

    arrivals = {}
    loads = ((feat_in, feat), (place_in, place), (edges_in, edges), (cot_in, cot), (dw_in, dw), (spread_in, spread),
             (up_in, up), (down_in, down))
    for k, (src, dst) in enumerate(loads):
        arrivals[id(dst)] = pltpu.make_async_copy(src, dst, ins.at[k])
        arrivals[id(dst)].start()

    barrier = pltpu.get_barrier_semaphore()

    def greet(device):
        pl.semaphore_signal(barrier, inc=1, device_id=device, device_id_type=MESH)

    for dy, dx in HALOS:
        greet((yh, lax.rem(ty + dy + 4, 4), lax.rem(tx + dx + 32, 32)))
    greet(sibling)

    @pl.loop(1, CHUNKS)
    def _(d):
        greet(plane_peer(d)[1])

    @pl.loop(1, NZ)
    def _(d):
        greet(z_peer(d)[1])

    def ready(*refs):
        for ref in refs:
            arrivals[id(ref)].wait()

    def leave(k, src, dst):
        return pltpu.make_async_copy(src, dst, outs.at[k])

    def there(dy, dx):
        flags = []
        if dy:
            flags.append(jnp.logical_and(ty + dy >= 0, ty + dy < 4))
        if dx:
            flags.append(jnp.logical_and(tx + dx >= 0, tx + dx < 32))
        return functools.reduce(jnp.logical_and, flags)

    def halo_copy(n, dy, dx):
        if dy == 0:
            slot = 6 if dx > 0 else 7
            src, dst = csend.at[n, 0 if dx < 0 else 1], crecv.at[n, slot - 6]
        else:
            slot = (1 if dy > 0 else 4) - dx
            src, dst = rsend.at[n, 0 if dy < 0 else 1], rrecv.at[n, slot]
        return pltpu.make_async_remote_copy(
            src_ref=src, dst_ref=dst, send_sem=hs.at[n, slot], recv_sem=hr.at[n, slot],
            device_id=(yh, ty + dy, tx + dx), device_id_type=MESH,
        )

    def halo_start(n, plane):
        flat = jnp.concatenate([plane[i, 3 : 3 + TC].reshape(TC * NS, CH) for i in range(NI)], axis=0)
        strips = nn(edges[...], flat.astype(BF16)).astype(BF16)
        rsend[n] = strips.reshape(2, 3, TC, CH)
        for c in range(3):
            csend[n, 0, c] = plane[:, 3 + c].reshape(TR, CH).astype(BF16)
            csend[n, 1, c] = plane[:, TC + c].reshape(TR, CH).astype(BF16)
        if n == 0:
            pl.semaphore_wait(barrier, 8 + 1 + CHUNKS - 1 + NZ - 1)
        for dy, dx in HALOS:

            @pl.when(there(dy, dx))
            def _(dy=dy, dx=dx):
                halo_copy(n, dy, dx).start()

    def halo_wait(n):
        for dy, dx in HALOS:

            @pl.when(there(-dy, -dx))
            def _(dy=dy, dx=dx):
                halo_copy(n, dy, dx).wait_recv()

            @pl.when(jnp.logical_not(there(-dy, -dx)))
            def _(dy=dy, dx=dx):
                if dy == 0:
                    crecv[n, 0 if dx > 0 else 1] = jnp.zeros((3, TR, CH), BF16)
                else:
                    rrecv[n, (1 if dy > 0 else 4) - dx] = jnp.zeros((3, TC, CH), BF16)

    def halo_done(n):
        for dy, dx in HALOS:

            @pl.when(there(dy, dx))
            def _(dy=dy, dx=dx):
                halo_copy(n, dy, dx).wait_send()

    def assemble(n, plane, q):
        for c in range(3):
            plane[:, c] = crecv[n, 0, c].astype(F32).reshape(NI, NS, CH)
            plane[:, TC + 3 + c] = crecv[n, 1, c].astype(F32).reshape(NI, NS, CH)
        for side in range(2):
            strips = jnp.concatenate([rrecv[n, 3 * side + k].reshape(3 * TC, CH) for k in range(3)], axis=0)
            tq[side] = nn(spread[side], strips).reshape(3, TC + 6, NS, CH)
        row = lax.broadcasted_iota(jnp.int32, (3, NS, LANES), 1)

        def fill(slot, mid, top, low):
            q[3:7, slot] = mid
            q[0:3, slot] = jnp.where(row == 0, top, pltpu.roll(mid[1:4], 1, 1))
            q[7:10, slot] = jnp.where(row == NS - 1, low, pltpu.roll(mid[0:3], NS - 1, 1))

        @pl.loop(0, TC + 6)
        def _(cc):
            fill(cc, plane[:, cc, :, :LANES], tq[0, :, cc, :, :LANES], tq[1, :, cc, :, :LANES])

        def pair(ref, *at):
            return jnp.concatenate([ref[(*at[:-1], at[-1], slice(None), slice(LANES, CH))],
                                    ref[(*at[:-1], at[-1] + 8, slice(None), slice(LANES, CH))]], axis=-1)

        @pl.loop(0, TC // 2 + 6)
        def _(k):
            fill(TC + 6 + k, pair(plane, slice(None), k), pair(tq, 0, slice(None), k), pair(tq, 1, slice(None), k))

    def convolve(q, l, flip):
        def columns(part, t, base):
            sums = [[None, None] for _ in range(NI)]
            for j2 in range(SPAN + 1):
                for r in range(NI + SPAN - 1):
                    x = q[r, base + j2]
                    for i in range(NI):
                        if not 0 <= r - i < SPAN:
                            continue
                        for o in range(2):
                            if not 0 <= j2 - o < SPAN:
                                continue
                            tap = (r - i) * SPAN + j2 - o
                            term = x * wexp[l, part, TAPS - 1 - tap if flip else tap]
                            sums[i][o] = term if sums[i][o] is None else sums[i][o] + term
            for i in range(NI):
                for o in range(2):
                    cbuf[i, t + o] = sums[i][o]

        @pl.loop(0, TC // 2)
        def _(k):
            columns(0, 2 * k, 2 * k)

        @pl.loop(0, TC // 4)
        def _(k):
            columns(1, TC + 2 * k, TC + 6 + 2 * k)

    def conv_rows(i):
        half = TC * NS // 2
        conv = convs.at[i]
        conv[:, :LANES] = cbuf[i, :TC].reshape(TC * NS, LANES)
        rest = cbuf[i, TC:].reshape(half, LANES)
        conv[:half, LANES:] = rest[:, :REST]
        conv[half:, LANES:] = rest[:, REST:]
        return conv[...]

    blk = TC * NS

    def rows_of(i):
        return pl.ds(pl.multiple_of(i * blk, blk), blk)

    def forward(l, plane, into, i):
        c = conv_rows(i) + cbias[l : l + 1]
        mid = c - jnp.mean(c, axis=1, keepdims=True)
        rstd = lax.rsqrt(jnp.mean(mid * mid, axis=1, keepdims=True) + EPSILON)
        u = mid * rstd
        rows = rows_of(i)
        unit[l, rows] = u
        inv[l, rows] = rstd
        nb = (u * gain[l : l + 1] + shift[l : l + 1]).astype(BF16)
        normed[l, rows] = nb
        pre = nn(nb, up[l]) + ubias[l : l + 1]
        cdf = 0.5 * (1.0 + lax.erf(pre * ROOT_HALF))
        slope[l, rows] = cdf + pre * INV_ROOT_TAU * jnp.exp(-0.5 * pre * pre)
        ab = (pre * cdf).astype(BF16)
        act[l, rows] = ab
        br = nt(ab, down[l]) + dbias[l : l + 1]
        branch[l, rows] = br
        before = plane[i, 3 : 3 + TC].reshape(blk, CH)
        new = (before + scale[l : l + 1] * br).astype(BF16)
        into(i, new)

    def fold(v):
        return jnp.sum(v.reshape(blk // 8, 8, v.shape[1]), axis=0)

    def branch_grads(l):
        def body(i, sums):
            rows = rows_of(i)
            g = grad[rows]
            gb = (g * scale[l : l + 1]).astype(BF16)
            gbr[rows] = gb
            return sums[0] + fold(gb.astype(F32)), sums[1] + fold(g * branch[l, rows])

        return lax.fori_loop(0, NI, body, (jnp.zeros((8, CH), F32),) * 2, unroll=True)

    def pre_grads(l):
        def body(i, total):
            rows = rows_of(i)
            gp = (nn(gbr[rows], down[l]) * slope[l, rows]).astype(BF16)
            gpre[rows] = gp
            return total + fold(gp.astype(F32))

        return lax.fori_loop(0, NI, body, jnp.zeros((8, HID), F32), unroll=True)

    def backward(l):
        def body(i, sums):
            rows = rows_of(i)
            s_gain, s_shift, s_cbias = sums
            gn = nt(gpre[rows], up[l])
            u = unit[l, rows]
            s_gain = s_gain + fold(gn * u)
            s_shift = s_shift + fold(gn)
            q = gn * gain[l : l + 1]
            centred = q - jnp.mean(q, axis=1, keepdims=True) - u * jnp.mean(q * u, axis=1, keepdims=True)
            gc = (inv[l, rows] * centred).astype(BF16).astype(F32)
            s_cbias = s_cbias + fold(gc)
            gx[i, 3 : 3 + TC] = gc.reshape(TC, NS, CH)
            gcp[i, :TC] = gc[:, :LANES].reshape(TC, NS, LANES)
            half = blk // 2
            gcp[i, TC:, :, :REST] = gc[:half, LANES:].reshape(TC // 2, NS, REST)
            gcp[i, TC:, :, REST:] = gc[half:, LANES:].reshape(TC // 2, NS, REST)
            return s_gain, s_shift, s_cbias

        zero = jnp.zeros((8, CH), F32)
        return lax.fori_loop(0, NI, body, (zero, zero, zero), unroll=True)

    def put(l, index, tile):
        if index < 256:
            chunk, slot = divmod(index, 8)
            pay0[l, chunk // CHUNKS, chunk % CHUNKS, 8 * slot : 8 * slot + 8] = tile
        else:
            chunk = index - 256
            pay1[l, chunk // CHUNKS, chunk % CHUNKS, :8] = tile

    def weight_tiles(a, b, store):
        for t in range(3):
            part = tn(a[...], b[:, 256 * t : 256 * t + 256])
            for v in range(2):
                for r in range(CH // 8):
                    store((2 * t + v) * (CH // 8) + r, part[8 * r : 8 * r + 8, LANES * v : LANES * v + LANES])

    def down_grads(l):
        weight_tiles(gbr, act.at[l], lambda index, tile: put(l, index, tile))

    def up_grads(l):
        weight_tiles(normed.at[l], gpre, lambda index, tile: put(l, TILES + index, tile))

    def tap_grads(l, *parts):
        for part in parts:
            cols, base, first = ((TC, 0, 0), (TC // 2, TC + 6, TC))[part]

            @pl.loop(0, SPAN)
            def _(j):
                def body(c, sums):
                    sums = list(sums)
                    for o in range(2):
                        col = 2 * c + o
                        gcs = [gcp[i, first + col] for i in range(NI)]
                        for r in range(NI + SPAN - 1):
                            x = qa[l, r, base + col + j]
                            for i in range(NI):
                                if 0 <= r - i < SPAN:
                                    sums[r - i] = sums[r - i] + gcs[i] * x
                    return tuple(sums)

                zero = jnp.zeros((NS, LANES), F32)
                sums = lax.fori_loop(0, cols // 2, body, (zero,) * SPAN)
                for r in range(SPAN):
                    taps[part, r * SPAN + j] = sums[r]

    def small_grads(l, early, s_ubias, sums):
        s_dbias, s_scale = early
        s_gain, s_shift, s_cbias = sums
        small[...] = jnp.zeros((LANES, LANES), F32)
        small[:TAPS] = jnp.sum(taps[0], axis=1)
        rest = jnp.sum(taps[1], axis=1)
        small[TAPS : 2 * TAPS, :REST] = rest[:, :REST] + rest[:, REST:]
        for at, v in ((ROW_CBIAS, s_cbias), (ROW_GAIN, s_gain), (ROW_SHIFT, s_shift),
                      (ROW_DBIAS, s_dbias), (ROW_SCALE, s_scale)):
            v = jnp.sum(v, axis=0, keepdims=True)
            small[at : at + 1] = v[:, :LANES]
            small[at + 1 : at + 2, :REST] = v[:, LANES:]
        v = jnp.sum(s_ubias, axis=0, keepdims=True)
        for t in range(6):
            small[ROW_UBIAS + t : ROW_UBIAS + t + 1] = v[:, LANES * t : LANES * t + LANES]
        upper = lax.broadcasted_iota(jnp.int32, (8, LANES), 0) < 4
        for k in range(2 * CHUNKS):
            v = small[8 * (k // 2) : 8 * (k // 2) + 8]
            if k % 2:
                v = pltpu.roll(v, 4, 0)
            pay1[l, k // CHUNKS, k % CHUNKS, SMALL_AT:] = jnp.where(upper, v, 0.0)

    upper = lax.broadcasted_iota(jnp.int32, (8, LANES), 0) < 4

    def rounded(v, part):
        if part == 0:
            return v.astype(BF16)
        s = v[SMALL_AT:]
        s = s + pltpu.roll(s, 4, 0)
        high = s.astype(BF16).astype(F32)
        return jnp.concatenate([v[:SMALL_AT], jnp.where(upper, high, s - high)], axis=0).astype(BF16)

    pays, cores, sbufs, rbufs, zbufs = (pay0, pay1), (core0, core1), (sbuf0, sbuf1), (rbuf0, rbuf1), (zbuf0, zbuf1)
    results = (result0, result1)

    def core_copy(l, p):
        return pltpu.make_async_remote_copy(
            src_ref=pays[p].at[l, other], dst_ref=cores[p].at[l], send_sem=cs.at[2 * l + p], recv_sem=cr.at[2 * l + p],
            device_id=sibling, device_id_type=MESH,
        )

    def plane_copy(l, p, d):
        index, device = plane_peer(d)
        return pltpu.make_async_remote_copy(
            src_ref=sbufs[p].at[l, index], dst_ref=rbufs[p].at[l, d], send_sem=xs.at[2 * l + p, d], recv_sem=xr.at[2 * l + p, d],
            device_id=device, device_id_type=MESH,
        )

    def z_copy(l, p, d):
        return pltpu.make_async_remote_copy(
            src_ref=zbufs[p].at[l, z], dst_ref=zbufs[p].at[l, z], send_sem=zs.at[2 * l + p, d], recv_sem=zr.at[2 * l + p, z],
            device_id=z_peer(d)[1], device_id_type=MESH,
        )

    def z_arrival(l, p, d):
        pz, device = z_peer(d)
        return pltpu.make_async_remote_copy(
            src_ref=zbufs[p].at[l, pz], dst_ref=zbufs[p].at[l, pz], send_sem=zs.at[2 * l + p, d], recv_sem=zr.at[2 * l + p, pz],
            device_id=device, device_id_type=MESH,
        )

    def gather_copy(l, p, d):
        return pltpu.make_async_remote_copy(
            src_ref=results[p].at[l, core, me], dst_ref=results[p].at[l, core, me], send_sem=gs.at[2 * l + p, d],
            recv_sem=gr.at[2 * l + p, me], device_id=plane_peer(d)[1], device_id_type=MESH,
        )

    def gather_arrival(l, p, d):
        index, device = plane_peer(d)
        return pltpu.make_async_remote_copy(
            src_ref=results[p].at[l, core, index], dst_ref=results[p].at[l, core, index], send_sem=gs.at[2 * l + p, d],
            recv_sem=gr.at[2 * l + p, index], device_id=device, device_id_type=MESH,
        )

    def relay_copy(l, p, index):
        return pltpu.make_async_remote_copy(
            src_ref=results[p].at[l, core, index], dst_ref=results[p].at[l, core, index], send_sem=ls.at[2 * l + p, index],
            recv_sem=lr.at[2 * l + p, index], device_id=sibling, device_id_type=MESH,
        )

    def relay_arrival(l, p, index):
        return pltpu.make_async_remote_copy(
            src_ref=results[p].at[l, other, index], dst_ref=results[p].at[l, other, index], send_sem=ls.at[2 * l + p, index],
            recv_sem=lr.at[2 * l + p, index], device_id=sibling, device_id_type=MESH,
        )

    def to_plane(l, p):
        core_copy(l, p).wait_recv()

        @pl.loop(0, CHUNKS)
        def _(k):
            d = lax.rem(k + 1, CHUNKS)
            index, _ = plane_peer(d)
            v = pays[p][l, core, index] + cores[p][l, index]
            sbufs[p][l, index] = rounded(v, p)

            @pl.when(d > 0)
            def _():
                plane_copy(l, p, d).start()

    def to_z(l, p):
        @pl.loop(1, CHUNKS)
        def _(d):
            plane_copy(l, p, d).wait_recv()

        v = lax.fori_loop(1, CHUNKS, lambda d, v: v + rbufs[p][l, d].astype(F32), sbufs[p][l, me].astype(F32))
        zbufs[p][l, z] = rounded(v, p)

        @pl.loop(1, NZ)
        def _(d):
            z_copy(l, p, d).start()

    def to_all(l, p):
        @pl.loop(1, NZ)
        def _(d):
            z_arrival(l, p, d).wait_recv()

        v = zbufs[p][l, 0].astype(F32)
        for k in range(1, NZ):
            v = v + zbufs[p][l, k].astype(F32)
        results[p][l, core, me] = rounded(v * factor, p)

        @pl.loop(1, CHUNKS)
        def _(d):
            gather_copy(l, p, d).start()

        relay_copy(l, p, me).start()

    def to_sibling(l, p):
        @pl.loop(1, CHUNKS)
        def _(d):
            gather_arrival(l, p, d).wait_recv()
            relay_copy(l, p, plane_peer(d)[0]).start()

    def finish(l, p):
        @pl.loop(0, CHUNKS)
        def _(k):
            relay_arrival(l, p, k).wait_recv()
            relay_copy(l, p, k).wait_send()

        core_copy(l, p).wait_send()

        @pl.loop(1, CHUNKS)
        def _(d):
            plane_copy(l, p, d).wait_send()
            gather_copy(l, p, d).wait_send()

        @pl.loop(1, NZ)
        def _(d):
            z_copy(l, p, d).wait_send()


    def flat_rows(plane, i):
        return plane[i, 3 : 3 + TC].reshape(blk, CH)

    def step_back(l):
        @pl.loop(0, NI)
        def _(i):
            rows = rows_of(i)
            grad[rows] = grad[rows] + conv_rows(i)

    ready(feat, place, edges)
    xp[0, :, 3 : 3 + TC] = nn(place[...], feat[...]).reshape(NI, TC, NS, CH)
    halo_start(0, xp.at[0])
    ready(cot, dw, spread)
    grad[...] = nn(place[...], cot[...])

    @pl.loop(0, TAPS)
    def _(t):
        for l in range(2):
            tap = dw[t, l : l + 1]
            rest = tap[:, LANES:]
            wexp[l, 0, t] = jnp.broadcast_to(tap[:, :LANES], (NS, LANES))
            wexp[l, 1, t] = jnp.broadcast_to(jnp.concatenate([rest, rest], axis=1), (NS, LANES))

    halo_wait(0)
    assemble(0, xp.at[0], qa.at[0])
    convolve(qa.at[0], 0, False)
    ready(up, down)

    def keep(i, new):
        xp[1, i, 3 : 3 + TC] = new.astype(F32).reshape(TC, NS, CH)

    @pl.loop(0, NI, unroll=2)
    def _(i):
        forward(0, xp.at[0], keep, i)

    halo_start(1, xp.at[1])
    halo_wait(1)
    assemble(1, xp.at[1], qa.at[1])
    convolve(qa.at[1], 1, False)

    def keep_out(i, new):
        outq[rows_of(i)] = new

    @pl.loop(0, NI, unroll=2)
    def _(i):
        forward(1, xp.at[1], keep_out, i)

    def leave_all(l):
        return [leave(2 * l + k, v.at[l], to.at[l]) for k, (v, to) in enumerate(
            ((result0, result0_to), (result1, result1_to)))]

    early = branch_grads(1)
    s_ubias = pre_grads(1)
    down_grads(1)
    up_grads(1)
    core_copy(1, 0).start()
    sums = backward(1)
    halo_start(2, gx)
    tap_grads(1, 1)
    to_plane(1, 0)
    tap_grads(1, 0)
    small_grads(1, early, s_ubias, sums)
    core_copy(1, 1).start()
    halo_wait(2)
    assemble(2, gx, qg)
    to_plane(1, 1)
    convolve(qg, 1, True)
    step_back(1)
    early = branch_grads(0)
    s_ubias = pre_grads(0)
    down_grads(0)
    up_grads(0)
    core_copy(0, 0).start()
    to_z(1, 0)
    to_z(1, 1)
    sums = backward(0)
    halo_start(3, gx)
    tap_grads(0, 1)
    to_plane(0, 0)
    tap_grads(0, 0)
    small_grads(0, early, s_ubias, sums)
    core_copy(0, 1).start()
    halo_wait(3)
    assemble(3, gx, qg)
    to_plane(0, 1)
    to_all(1, 0)
    to_all(1, 1)
    convolve(qg, 0, True)
    step_back(0)
    to_z(0, 0)
    to_z(0, 1)
    g = grad[...]
    high = g.astype(BF16)
    g = g - high.astype(F32)
    mid = g.astype(BF16)
    low = (g - mid.astype(F32)).astype(BF16)
    gfeat_ref[...] = tn(place[...], high) + (tn(place[...], mid) + tn(place[...], low))
    leave(4, gfeat_ref, gfeat_to).start()
    out_ref[...] = tn(place[...], outq[...]).astype(BF16)
    leave(5, out_ref, out_to).start()
    to_sibling(1, 0)
    to_sibling(1, 1)
    to_all(0, 0)
    to_all(0, 1)
    for p in range(2):
        finish(1, p)
    for copy in leave_all(1):
        copy.start()
    to_sibling(0, 0)
    for n in range(4):
        halo_done(n)
    to_sibling(0, 1)
    for p in range(2):
        finish(0, p)
    for copy in leave_all(0):
        copy.start()
    for copy in leave_all(0) + leave_all(1):
        copy.wait()
    leave(4, gfeat_ref, gfeat_to).wait()
    leave(5, out_ref, out_to).wait()


def unpack(out_in, gfeat_in, result0_in, result1_in,
           out_to, gfeat_to, gtaps, gcbias, ggain, gshift, gup_to, gubias, gdown_to, gdbias, gscale,
           few, result0, result1, gup, gdown, ins, outs):
    copies = [
        pltpu.make_async_copy(src, dst, ins.at[k])
        for k, (src, dst) in enumerate(
            ((result0_in, result0), (result1_in, result1), (gfeat_in, gfeat_to), (out_in, out_to))
        )
    ]
    for copy in copies:
        copy.start()
    leaving = [pltpu.make_async_copy(gdown, gdown_to, outs.at[0]), pltpu.make_async_copy(gup, gup_to, outs.at[1])]
    upper = lax.broadcasted_iota(jnp.int32, (8, LANES), 0) < 4

    def place_tile(l, ref, index, tile):
        t, r = divmod(index, CH // 8)
        ref[l, 8 * r : 8 * r + 8, LANES * t : LANES * t + LANES] = tile

    def place_any(l, index, tile):
        if index < TILES:
            place_tile(l, gdown, index, tile)
        else:
            place_tile(l, gup, index - TILES, tile)

    copies[0].wait()
    for l in range(2):
        for chunk in range(2 * CHUNKS):
            v = result0[l, chunk // CHUNKS, chunk % CHUNKS].astype(F32)
            for slot in range(8):
                place_any(l, 8 * chunk + slot, v[8 * slot : 8 * slot + 8])
    leaving[0].start()
    copies[1].wait()
    for l in range(2):
        for chunk in range(2 * CHUNKS):
            place_any(l, 256 + chunk, result1[l, chunk // CHUNKS, chunk % CHUNKS].astype(F32)[:8])
    leaving[1].start()
    for l in range(2):
        pair = []
        for chunk in range(2 * CHUNKS):
            v = result1[l, chunk // CHUNKS, chunk % CHUNKS].astype(F32)[SMALL_AT:]
            pair.append(v + pltpu.roll(v, 4, 0))
            if chunk % 2:
                few[4 * chunk - 4 : 4 * chunk + 4] = jnp.where(upper, pair[-2], pair[-1])
        for t in range(TAPS):
            gtaps[t, l : l + 1, :LANES] = few[t : t + 1]
            gtaps[t, l : l + 1, LANES:] = few[TAPS + t : TAPS + t + 1, :REST]
        for at, ref in ((ROW_CBIAS, gcbias), (ROW_GAIN, ggain), (ROW_SHIFT, gshift),
                        (ROW_DBIAS, gdbias), (ROW_SCALE, gscale)):
            ref[l : l + 1, :LANES] = few[at : at + 1]
            ref[l : l + 1, LANES:] = few[at + 1 : at + 2, :REST]
        for t in range(6):
            gubias[l : l + 1, LANES * t : LANES * t + LANES] = few[ROW_UBIAS + t : ROW_UBIAS + t + 1]
    for copy in copies[2:] + leaving:
        copy.wait()


def on_device(features, cotangent, dw_kernel, conv_bias, ln_gain, ln_shift, up_weight, up_bias,
              down_weight, down_bias, layer_scale):
    depth = dw_kernel.shape[0]
    pixel_total = PX * lax.axis_size("slide") * lax.axis_size("ty") * lax.axis_size("tx")
    place, edges, spread = (jnp.asarray(v, BF16) for v in one_hots())
    taps = dw_kernel.reshape(depth, TAPS, CH).transpose(1, 0, 2)
    vmem = pl.BlockSpec(memory_space=pltpu.VMEM)
    dma = pltpu.SemaphoreType.DMA
    plane = (NI, TC + 6, NS, CH)
    wide = (NI + 6, WIDE, NS, LANES)
    hbm = pl.BlockSpec(memory_space=pltpu.HBM)
    results = tuple(jax.ShapeDtypeStruct((depth, 2, CHUNKS, rows, LANES), BF16) for rows in PARTS)
    out, gfeat, result0, result1 = pl.pallas_call(
        functools.partial(kernel, 1.0 / math.sqrt(pixel_total)),
        out_shape=(
            jax.ShapeDtypeStruct((PX, CH), BF16),
            jax.ShapeDtypeStruct((PX, CH), F32),
            *results,
        ),
        in_specs=[hbm] * 3 + [vmem] * 3 + [hbm, vmem, hbm] + [vmem] * 2 + [hbm] * 3,
        out_specs=(hbm,) * 4,
        scratch_shapes=[
            pltpu.VMEM((PX, CH), BF16),
            pltpu.VMEM((PX, CH), BF16),
            pltpu.VMEM((TAPS, depth, CH), F32),
            pltpu.VMEM((depth, CH, HID), BF16),
            pltpu.VMEM((depth, CH, HID), BF16),
            pltpu.VMEM(place.shape, BF16),
            pltpu.VMEM(edges.shape, BF16),
            pltpu.VMEM(spread.shape, BF16),
            pltpu.VMEM((PX, CH), BF16),
            pltpu.VMEM((PX, CH), F32),
            *(pltpu.VMEM(v.shape, v.dtype) for v in results),
            dma((8,)), dma((6,)),
            pltpu.VMEM((2, *plane), F32),
            pltpu.VMEM(plane, F32),
            pltpu.VMEM((2, *wide), F32),
            pltpu.VMEM(wide, F32),
            pltpu.VMEM((NI, PACK, NS, LANES), F32),
            pltpu.VMEM((NI, TC * NS, CH), F32),
            pltpu.VMEM((2, PX, CH), F32),
            pltpu.VMEM((2, PX, 1), F32),
            pltpu.VMEM((2, PX, CH), BF16),
            pltpu.VMEM((2, PX, HID), BF16),
            pltpu.VMEM((2, PX, HID), F32),
            pltpu.VMEM((2, PX, CH), F32),
            pltpu.VMEM((PX, CH), BF16),
            pltpu.VMEM((PX, HID), BF16),
            pltpu.VMEM((NI, PACK, NS, LANES), F32),
            pltpu.VMEM((2, 3, TC + 6, NS, CH), F32),
            pltpu.VMEM((2, TAPS, NS, LANES), F32),
            pltpu.VMEM((LANES, LANES), F32),
            pltpu.VMEM((PX, CH), F32),
            pltpu.VMEM((PX, CH), BF16),
            pltpu.VMEM((2, 2, TAPS, NS, LANES), F32),
            *(pltpu.VMEM((2, 2, CHUNKS, rows, LANES), F32) for rows in PARTS),
            *(pltpu.VMEM((2, CHUNKS, rows, LANES), F32) for rows in PARTS),
            *(pltpu.VMEM((2, CHUNKS, rows, LANES), BF16) for rows in PARTS),
            *(pltpu.VMEM((2, CHUNKS, rows, LANES), BF16) for rows in PARTS),
            *(pltpu.VMEM((2, NZ, rows, LANES), BF16) for rows in PARTS),
            pltpu.VMEM((4, 2, 3, TR, CH), BF16),
            pltpu.VMEM((4, 2, 3, TC, CH), BF16),
            pltpu.VMEM((4, 2, 3, TR, CH), BF16),
            pltpu.VMEM((4, 6, 3, TC, CH), BF16),
            dma((4, 8)), dma((4, 8)),
            dma((4,)), dma((4,)),
            dma((4, CHUNKS)), dma((4, CHUNKS)),
            dma((4, NZ)), dma((4, NZ)),
            dma((4, CHUNKS)), dma((4, CHUNKS)),
            dma((4, CHUNKS)), dma((4, CHUNKS)),
        ],
        compiler_params=pltpu.CompilerParams(
            collective_id=0, has_side_effects=True, vmem_limit_bytes=56 * 2**20
        ),
    )(
        features.reshape(PX, CH), cotangent.reshape(PX, CH), taps, conv_bias, ln_gain, ln_shift,
        up_weight, up_bias, down_weight.transpose(0, 2, 1), down_bias, layer_scale, place, edges, spread,
    )
    vector = jax.ShapeDtypeStruct((depth, CH), F32)
    weight = jax.ShapeDtypeStruct((depth, CH, HID), F32)
    out, gfeat, gtaps, gcbias, ggain, gshift, gup, gubias, gdown, gdbias, gscale = pl.pallas_call(
        unpack,
        out_shape=(
            jax.ShapeDtypeStruct((PX, CH), BF16),
            jax.ShapeDtypeStruct((PX, CH), F32),
            jax.ShapeDtypeStruct((TAPS, depth, CH), F32),
            vector, vector, vector, weight, jax.ShapeDtypeStruct((depth, HID), F32), weight, vector, vector,
        ),
        in_specs=[hbm] * 4,
        out_specs=(hbm,) * 2 + (vmem,) * 4 + (hbm, vmem, hbm) + (vmem,) * 2,
        scratch_shapes=[
            pltpu.VMEM((LANES, LANES), F32),
            *(pltpu.VMEM(v.shape, v.dtype) for v in results),
            pltpu.VMEM((depth, CH, HID), F32),
            pltpu.VMEM((depth, CH, HID), F32),
            dma((4,)),
            dma((2,)),
        ],
        compiler_params=pltpu.CompilerParams(vmem_limit_bytes=56 * 2**20),
    )(out, gfeat, result0, result1)
    return (
        out.reshape(1, TR, TC, CH),
        gfeat.reshape(1, TR, TC, CH),
        gtaps.transpose(1, 0, 2).reshape(depth, SPAN, SPAN, CH),
        gcbias,
        ggain,
        gshift,
        gup,
        gubias,
        gdown.transpose(0, 2, 1),
        gdbias,
        gscale,
    )


def solution(mesh):
    tiled = P("slide", "ty", "tx", None)
    return jax.shard_map(
        on_device,
        mesh=mesh,
        in_specs=(tiled, tiled) + (P(),) * 9,
        out_specs=(tiled, tiled) + (P(),) * 9,
        check_vma=False,
    )
```

```python
import functools
import math

import jax
import jax.numpy as jnp
import numpy as np
from jax import lax
from jax.experimental import pallas as pl
from jax.experimental.pallas import tpu as pltpu
from jax.sharding import PartitionSpec as P

MESH = pl.DeviceIdType.MESH
F32 = jnp.float32
BF16 = jnp.bfloat16
ROOT_HALF = 0.7071067811865476
INV_ROOT_TAU = 0.3989422804014327
EPSILON = 1e-06

TR, TC, CH, HID = 32, 16, 192, 768
PX = TR * TC
NI, NS = 4, 8
MARGIN = 3
SPAN = 7
TAPS = SPAN * SPAN
LANES = 128
REST = CH - LANES
PACK = TC + TC // 2
WIDE = (TC + 2 * MARGIN) + (TC // 2 + 2 * MARGIN)
PARTS = (64, 16)
TILES = CH // 8 * (HID // LANES)
SMALL_AT = 8
CHUNKS = 16
NZ = 8
HALOS = ((-1, -1), (-1, 0), (-1, 1), (1, -1), (1, 0), (1, 1), (0, -1), (0, 1))

ROW_CBIAS, ROW_GAIN, ROW_SHIFT, ROW_DBIAS, ROW_SCALE, ROW_UBIAS = 98, 100, 102, 104, 106, 108


def pixel_order():
    q = np.arange(PX)
    return (4 * (q % NS) + q // (TC * NS)) * TC + (q // NS) % TC


def one_hots():
    order = pixel_order()
    place = np.zeros((PX, PX), np.float32)
    place[np.arange(PX), order] = 1.0
    inverse = np.argsort(order)
    edge_rows = np.concatenate([np.arange(3 * TC), np.arange((TR - 3) * TC, TR * TC)])
    edges = np.zeros((6 * TC, PX), np.float32)
    edges[np.arange(6 * TC), inverse[edge_rows]] = 1.0
    spread = np.zeros((2, 3, TC + 6, NS, 3, 3, TC), np.float32)
    for cc in range(TC + 6):
        source, column = (0, TC - 3 + cc) if cc < 3 else (1, cc - 3) if cc < TC + 3 else (2, cc - TC - 3)
        for u in range(3):
            spread[0, u, cc, 0, source, u, column] = 1.0
            spread[1, u, cc, NS - 1, source, u, column] = 1.0
    spread = spread.reshape(2, 3 * (TC + 6) * NS, 9 * TC)
    return place, edges, spread


def tn(a, b):
    return lax.dot_general(a, b, (((0,), (0,)), ((), ())), preferred_element_type=F32)


def nt(a, b):
    return lax.dot_general(a, b, (((1,), (1,)), ((), ())), preferred_element_type=F32)


def nn(a, b):
    return jnp.dot(a, b, preferred_element_type=F32)


def kernel(
    factor,
    feat_in, cot_in, dw_in, cbias, gain, shift, up_in, ubias, down_in, dbias, scale, place_in, edges_in, spread_in,
    out_to, gfeat_to, result0_to, result1_to,
    feat, cot, dw, up, down, place, edges, spread, out_ref, gfeat_ref, result0, result1, ins, outs,
    xp, gx, qa, qg, cbuf, convs, unit, inv, normed, act, slope, branch, gbr, gpre, gcp, tq, taps, small,
    grad, outq, wexp,
    pay0, pay1, core0, core1, sbuf0, sbuf1, rbuf0, rbuf1, zbuf0, zbuf1,
    csend, rsend, crecv, rrecv,
    hs, hr, cs, cr, xs, xr, zs, zr, gs, gr, ls, lr,
):
    yh = lax.axis_index("slide")
    ty = lax.axis_index("ty")
    tx = lax.axis_index("tx")
    core = lax.rem(tx, 2)
    yl = lax.rem(lax.div(tx, 2), 2)
    z = lax.div(tx, 4)
    other = 1 - core
    me = ty * 4 + yh * 2 + yl
    sibling = (yh, ty, z * 4 + yl * 2 + other)

    def plane_peer(d):
        py = lax.rem(ty + lax.div(d, 4), 4)
        ph = lax.rem(yh + lax.rem(lax.div(d, 2), 2), 2)
        pl_ = lax.rem(yl + lax.rem(d, 2), 2)
        return py * 4 + ph * 2 + pl_, (ph, py, z * 4 + pl_ * 2 + core)

    def z_peer(d):
        pz = lax.rem(z + d, NZ)
        return pz, (yh, ty, pz * 4 + yl * 2 + core)

    arrivals = {}
    loads = ((feat_in, feat), (place_in, place), (edges_in, edges), (cot_in, cot), (dw_in, dw), (spread_in, spread),
             (up_in, up), (down_in, down))
    for k, (src, dst) in enumerate(loads):
        arrivals[id(dst)] = pltpu.make_async_copy(src, dst, ins.at[k])
        arrivals[id(dst)].start()

    barrier = pltpu.get_barrier_semaphore()

    def greet(device):
        pl.semaphore_signal(barrier, inc=1, device_id=device, device_id_type=MESH)

    for dy, dx in HALOS:
        greet((yh, lax.rem(ty + dy + 4, 4), lax.rem(tx + dx + 32, 32)))
    greet(sibling)

    @pl.loop(1, CHUNKS)
    def _(d):
        greet(plane_peer(d)[1])

    @pl.loop(1, NZ)
    def _(d):
        greet(z_peer(d)[1])

    def ready(*refs):
        for ref in refs:
            arrivals[id(ref)].wait()

    def leave(k, src, dst):
        return pltpu.make_async_copy(src, dst, outs.at[k])

    def there(dy, dx):
        flags = []
        if dy:
            flags.append(jnp.logical_and(ty + dy >= 0, ty + dy < 4))
        if dx:
            flags.append(jnp.logical_and(tx + dx >= 0, tx + dx < 32))
        return functools.reduce(jnp.logical_and, flags)

    def halo_copy(n, dy, dx):
        if dy == 0:
            slot = 6 if dx > 0 else 7
            src, dst = csend.at[n, 0 if dx < 0 else 1], crecv.at[n, slot - 6]
        else:
            slot = (1 if dy > 0 else 4) - dx
            src, dst = rsend.at[n, 0 if dy < 0 else 1], rrecv.at[n, slot]
        return pltpu.make_async_remote_copy(
            src_ref=src, dst_ref=dst, send_sem=hs.at[n, slot], recv_sem=hr.at[n, slot],
            device_id=(yh, ty + dy, tx + dx), device_id_type=MESH,
        )

    def halo_start(n, plane):
        flat = jnp.concatenate([plane[i, 3 : 3 + TC].reshape(TC * NS, CH) for i in range(NI)], axis=0)
        strips = nn(edges[...], flat.astype(BF16)).astype(BF16)
        rsend[n] = strips.reshape(2, 3, TC, CH)
        for c in range(3):
            csend[n, 0, c] = plane[:, 3 + c].reshape(TR, CH).astype(BF16)
            csend[n, 1, c] = plane[:, TC + c].reshape(TR, CH).astype(BF16)
        if n == 0:
            pl.semaphore_wait(barrier, 8 + 1 + CHUNKS - 1 + NZ - 1)
        for dy, dx in HALOS:

            @pl.when(there(dy, dx))
            def _(dy=dy, dx=dx):
                halo_copy(n, dy, dx).start()

    def halo_wait(n):
        for dy, dx in HALOS:

            @pl.when(there(-dy, -dx))
            def _(dy=dy, dx=dx):
                halo_copy(n, dy, dx).wait_recv()

            @pl.when(jnp.logical_not(there(-dy, -dx)))
            def _(dy=dy, dx=dx):
                if dy == 0:
                    crecv[n, 0 if dx > 0 else 1] = jnp.zeros((3, TR, CH), BF16)
                else:
                    rrecv[n, (1 if dy > 0 else 4) - dx] = jnp.zeros((3, TC, CH), BF16)

    def halo_done(n):
        for dy, dx in HALOS:

            @pl.when(there(dy, dx))
            def _(dy=dy, dx=dx):
                halo_copy(n, dy, dx).wait_send()

    def assemble(n, plane, q):
        for c in range(3):
            plane[:, c] = crecv[n, 0, c].astype(F32).reshape(NI, NS, CH)
            plane[:, TC + 3 + c] = crecv[n, 1, c].astype(F32).reshape(NI, NS, CH)
        for side in range(2):
            strips = jnp.concatenate([rrecv[n, 3 * side + k].reshape(3 * TC, CH) for k in range(3)], axis=0)
            tq[side] = nn(spread[side], strips).reshape(3, TC + 6, NS, CH)
        row = lax.broadcasted_iota(jnp.int32, (3, NS, LANES), 1)

        def fill(slot, mid, top, low):
            q[3:7, slot] = mid
            q[0:3, slot] = jnp.where(row == 0, top, pltpu.roll(mid[1:4], 1, 1))
            q[7:10, slot] = jnp.where(row == NS - 1, low, pltpu.roll(mid[0:3], NS - 1, 1))

        @pl.loop(0, TC + 6, unroll=2)
        def _(cc):
            fill(cc, plane[:, cc, :, :LANES], tq[0, :, cc, :, :LANES], tq[1, :, cc, :, :LANES])

        def pair(ref, *at):
            return jnp.concatenate([ref[(*at[:-1], at[-1], slice(None), slice(LANES, CH))],
                                    ref[(*at[:-1], at[-1] + 8, slice(None), slice(LANES, CH))]], axis=-1)

        @pl.loop(0, TC // 2 + 6, unroll=2)
        def _(k):
            fill(TC + 6 + k, pair(plane, slice(None), k), pair(tq, 0, slice(None), k), pair(tq, 1, slice(None), k))

    def convolve(q, l, flip):
        def columns(part, t, base):
            sums = [[None, None] for _ in range(NI)]
            for j2 in range(SPAN + 1):
                for r in range(NI + SPAN - 1):
                    x = q[r, base + j2]
                    for i in range(NI):
                        if not 0 <= r - i < SPAN:
                            continue
                        for o in range(2):
                            if not 0 <= j2 - o < SPAN:
                                continue
                            tap = (r - i) * SPAN + j2 - o
                            term = x * wexp[l, part, TAPS - 1 - tap if flip else tap]
                            sums[i][o] = term if sums[i][o] is None else sums[i][o] + term
            for i in range(NI):
                for o in range(2):
                    cbuf[i, t + o] = sums[i][o]

        @pl.loop(0, TC // 2)
        def _(k):
            columns(0, 2 * k, 2 * k)

        @pl.loop(0, TC // 4)
        def _(k):
            columns(1, TC + 2 * k, TC + 6 + 2 * k)

    def conv_rows(i):
        half = TC * NS // 2
        conv = convs.at[i]
        conv[:, :LANES] = cbuf[i, :TC].reshape(TC * NS, LANES)
        rest = cbuf[i, TC:].reshape(half, LANES)
        conv[:half, LANES:] = rest[:, :REST]
        conv[half:, LANES:] = rest[:, REST:]
        return conv[...]

    blk = TC * NS

    def rows_of(i):
        return pl.ds(pl.multiple_of(i * blk, blk), blk)

    def forward(l, plane, into, i):
        c = conv_rows(i) + cbias[l : l + 1]
        mid = c - jnp.mean(c, axis=1, keepdims=True)
        rstd = lax.rsqrt(jnp.mean(mid * mid, axis=1, keepdims=True) + EPSILON)
        u = mid * rstd
        rows = rows_of(i)
        unit[l, rows] = u
        inv[l, rows] = rstd
        nb = (u * gain[l : l + 1] + shift[l : l + 1]).astype(BF16)
        normed[l, rows] = nb
        pre = nn(nb, up[l]) + ubias[l : l + 1]
        cdf = 0.5 * (1.0 + lax.erf(pre * ROOT_HALF))
        slope[l, rows] = cdf + pre * INV_ROOT_TAU * jnp.exp(-0.5 * pre * pre)
        ab = (pre * cdf).astype(BF16)
        act[l, rows] = ab
        br = nt(ab, down[l]) + dbias[l : l + 1]
        branch[l, rows] = br
        before = plane[i, 3 : 3 + TC].reshape(blk, CH)
        new = (before + scale[l : l + 1] * br).astype(BF16)
        into(i, new)

    def fold(v):
        return jnp.sum(v.reshape(blk // 8, 8, v.shape[1]), axis=0)

    def branch_grads(l):
        def body(i, sums):
            rows = rows_of(i)
            g = grad[rows]
            gb = (g * scale[l : l + 1]).astype(BF16)
            gbr[rows] = gb
            return sums[0] + fold(gb.astype(F32)), sums[1] + fold(g * branch[l, rows])

        return lax.fori_loop(0, NI, body, (jnp.zeros((8, CH), F32),) * 2, unroll=True)

    def pre_grads(l):
        def body(i, total):
            rows = rows_of(i)
            gp = (nn(gbr[rows], down[l]) * slope[l, rows]).astype(BF16)
            gpre[rows] = gp
            return total + fold(gp.astype(F32))

        return lax.fori_loop(0, NI, body, jnp.zeros((8, HID), F32), unroll=True)

    def backward(l):
        def body(i, sums):
            rows = rows_of(i)
            s_gain, s_shift, s_cbias = sums
            gn = nt(gpre[rows], up[l])
            u = unit[l, rows]
            s_gain = s_gain + fold(gn * u)
            s_shift = s_shift + fold(gn)
            q = gn * gain[l : l + 1]
            centred = q - jnp.mean(q, axis=1, keepdims=True) - u * jnp.mean(q * u, axis=1, keepdims=True)
            gc = (inv[l, rows] * centred).astype(BF16).astype(F32)
            s_cbias = s_cbias + fold(gc)
            gx[i, 3 : 3 + TC] = gc.reshape(TC, NS, CH)
            gcp[i, :TC] = gc[:, :LANES].reshape(TC, NS, LANES)
            half = blk // 2
            gcp[i, TC:, :, :REST] = gc[:half, LANES:].reshape(TC // 2, NS, REST)
            gcp[i, TC:, :, REST:] = gc[half:, LANES:].reshape(TC // 2, NS, REST)
            return s_gain, s_shift, s_cbias

        zero = jnp.zeros((8, CH), F32)
        return lax.fori_loop(0, NI, body, (zero, zero, zero), unroll=True)

    def put(l, index, tile):
        if index < 256:
            chunk, slot = divmod(index, 8)
            pay0[l, chunk // CHUNKS, chunk % CHUNKS, 8 * slot : 8 * slot + 8] = tile
        else:
            chunk = index - 256
            pay1[l, chunk // CHUNKS, chunk % CHUNKS, :8] = tile

    def weight_tiles(a, b, store):
        for t in range(3):
            part = tn(a[...], b[:, 256 * t : 256 * t + 256])
            for v in range(2):
                for r in range(CH // 8):
                    store((2 * t + v) * (CH // 8) + r, part[8 * r : 8 * r + 8, LANES * v : LANES * v + LANES])

    def down_grads(l):
        weight_tiles(gbr, act.at[l], lambda index, tile: put(l, index, tile))

    def up_grads(l):
        weight_tiles(normed.at[l], gpre, lambda index, tile: put(l, TILES + index, tile))

    def tap_grads(l, *parts):
        for part in parts:
            cols, base, first = ((TC, 0, 0), (TC // 2, TC + 6, TC))[part]

            @pl.loop(0, SPAN)
            def _(j):
                def body(c, sums):
                    sums = list(sums)
                    for o in range(2):
                        col = 2 * c + o
                        gcs = [gcp[i, first + col] for i in range(NI)]
                        for r in range(NI + SPAN - 1):
                            x = qa[l, r, base + col + j]
                            for i in range(NI):
                                if 0 <= r - i < SPAN:
                                    sums[r - i] = sums[r - i] + gcs[i] * x
                    return tuple(sums)

                zero = jnp.zeros((NS, LANES), F32)
                sums = lax.fori_loop(0, cols // 2, body, (zero,) * SPAN)
                for r in range(SPAN):
                    taps[part, r * SPAN + j] = sums[r]

    def small_grads(l, early, s_ubias, sums):
        s_dbias, s_scale = early
        s_gain, s_shift, s_cbias = sums
        small[...] = jnp.zeros((LANES, LANES), F32)
        small[:TAPS] = jnp.sum(taps[0], axis=1)
        rest = jnp.sum(taps[1], axis=1)
        small[TAPS : 2 * TAPS, :REST] = rest[:, :REST] + rest[:, REST:]
        for at, v in ((ROW_CBIAS, s_cbias), (ROW_GAIN, s_gain), (ROW_SHIFT, s_shift),
                      (ROW_DBIAS, s_dbias), (ROW_SCALE, s_scale)):
            v = jnp.sum(v, axis=0, keepdims=True)
            small[at : at + 1] = v[:, :LANES]
            small[at + 1 : at + 2, :REST] = v[:, LANES:]
        v = jnp.sum(s_ubias, axis=0, keepdims=True)
        for t in range(6):
            small[ROW_UBIAS + t : ROW_UBIAS + t + 1] = v[:, LANES * t : LANES * t + LANES]
        upper = lax.broadcasted_iota(jnp.int32, (8, LANES), 0) < 4
        for k in range(2 * CHUNKS):
            v = small[8 * (k // 2) : 8 * (k // 2) + 8]
            if k % 2:
                v = pltpu.roll(v, 4, 0)
            pay1[l, k // CHUNKS, k % CHUNKS, SMALL_AT:] = jnp.where(upper, v, 0.0)

    upper = lax.broadcasted_iota(jnp.int32, (8, LANES), 0) < 4

    def rounded(v, part):
        if part == 0:
            return v.astype(BF16)
        s = v[SMALL_AT:]
        s = s + pltpu.roll(s, 4, 0)
        high = s.astype(BF16).astype(F32)
        return jnp.concatenate([v[:SMALL_AT], jnp.where(upper, high, s - high)], axis=0).astype(BF16)

    pays, cores, sbufs, rbufs, zbufs = (pay0, pay1), (core0, core1), (sbuf0, sbuf1), (rbuf0, rbuf1), (zbuf0, zbuf1)
    results = (result0, result1)

    def core_copy(l, p):
        return pltpu.make_async_remote_copy(
            src_ref=pays[p].at[l, other], dst_ref=cores[p].at[l], send_sem=cs.at[2 * l + p], recv_sem=cr.at[2 * l + p],
            device_id=sibling, device_id_type=MESH,
        )

    def plane_copy(l, p, d):
        index, device = plane_peer(d)
        return pltpu.make_async_remote_copy(
            src_ref=sbufs[p].at[l, index], dst_ref=rbufs[p].at[l, d], send_sem=xs.at[2 * l + p, d], recv_sem=xr.at[2 * l + p, d],
            device_id=device, device_id_type=MESH,
        )

    def z_copy(l, p, d):
        return pltpu.make_async_remote_copy(
            src_ref=zbufs[p].at[l, z], dst_ref=zbufs[p].at[l, z], send_sem=zs.at[2 * l + p, d], recv_sem=zr.at[2 * l + p, z],
            device_id=z_peer(d)[1], device_id_type=MESH,
        )

    def z_arrival(l, p, d):
        pz, device = z_peer(d)
        return pltpu.make_async_remote_copy(
            src_ref=zbufs[p].at[l, pz], dst_ref=zbufs[p].at[l, pz], send_sem=zs.at[2 * l + p, d], recv_sem=zr.at[2 * l + p, pz],
            device_id=device, device_id_type=MESH,
        )

    def gather_copy(l, p, d):
        return pltpu.make_async_remote_copy(
            src_ref=results[p].at[l, core, me], dst_ref=results[p].at[l, core, me], send_sem=gs.at[2 * l + p, d],
            recv_sem=gr.at[2 * l + p, me], device_id=plane_peer(d)[1], device_id_type=MESH,
        )

    def gather_arrival(l, p, d):
        index, device = plane_peer(d)
        return pltpu.make_async_remote_copy(
            src_ref=results[p].at[l, core, index], dst_ref=results[p].at[l, core, index], send_sem=gs.at[2 * l + p, d],
            recv_sem=gr.at[2 * l + p, index], device_id=device, device_id_type=MESH,
        )

    def relay_copy(l, p, index):
        return pltpu.make_async_remote_copy(
            src_ref=results[p].at[l, core, index], dst_ref=results[p].at[l, core, index], send_sem=ls.at[2 * l + p, index],
            recv_sem=lr.at[2 * l + p, index], device_id=sibling, device_id_type=MESH,
        )

    def relay_arrival(l, p, index):
        return pltpu.make_async_remote_copy(
            src_ref=results[p].at[l, other, index], dst_ref=results[p].at[l, other, index], send_sem=ls.at[2 * l + p, index],
            recv_sem=lr.at[2 * l + p, index], device_id=sibling, device_id_type=MESH,
        )

    def to_plane(l, p):
        core_copy(l, p).wait_recv()

        @pl.loop(0, CHUNKS)
        def _(k):
            d = lax.rem(k + 1, CHUNKS)
            index, _ = plane_peer(d)
            v = pays[p][l, core, index] + cores[p][l, index]
            sbufs[p][l, index] = rounded(v, p)

            @pl.when(d > 0)
            def _():
                plane_copy(l, p, d).start()

    def to_z(l, p):
        @pl.loop(1, CHUNKS)
        def _(d):
            plane_copy(l, p, d).wait_recv()

        v = lax.fori_loop(1, CHUNKS, lambda d, v: v + rbufs[p][l, d].astype(F32), sbufs[p][l, me].astype(F32))
        zbufs[p][l, z] = rounded(v, p)

        @pl.loop(1, NZ)
        def _(d):
            z_copy(l, p, d).start()

    def to_all(l, p):
        @pl.loop(1, NZ)
        def _(d):
            z_arrival(l, p, d).wait_recv()

        v = zbufs[p][l, 0].astype(F32)
        for k in range(1, NZ):
            v = v + zbufs[p][l, k].astype(F32)
        results[p][l, core, me] = rounded(v * factor, p)

        @pl.loop(1, CHUNKS)
        def _(d):
            gather_copy(l, p, d).start()

        relay_copy(l, p, me).start()

    def to_sibling(l, p):
        @pl.loop(1, CHUNKS)
        def _(d):
            gather_arrival(l, p, d).wait_recv()
            relay_copy(l, p, plane_peer(d)[0]).start()

    def finish(l, p):
        @pl.loop(0, CHUNKS)
        def _(k):
            relay_arrival(l, p, k).wait_recv()
            relay_copy(l, p, k).wait_send()

        core_copy(l, p).wait_send()

        @pl.loop(1, CHUNKS)
        def _(d):
            plane_copy(l, p, d).wait_send()
            gather_copy(l, p, d).wait_send()

        @pl.loop(1, NZ)
        def _(d):
            z_copy(l, p, d).wait_send()


    def flat_rows(plane, i):
        return plane[i, 3 : 3 + TC].reshape(blk, CH)

    def step_back(l):
        @pl.loop(0, NI)
        def _(i):
            rows = rows_of(i)
            grad[rows] = grad[rows] + conv_rows(i)

    ready(feat, place, edges)
    xp[0, :, 3 : 3 + TC] = nn(place[...], feat[...]).reshape(NI, TC, NS, CH)
    halo_start(0, xp.at[0])
    ready(cot, dw, spread)
    grad[...] = nn(place[...], cot[...])

    @pl.loop(0, TAPS)
    def _(t):
        for l in range(2):
            tap = dw[t, l : l + 1]
            rest = tap[:, LANES:]
            wexp[l, 0, t] = jnp.broadcast_to(tap[:, :LANES], (NS, LANES))
            wexp[l, 1, t] = jnp.broadcast_to(jnp.concatenate([rest, rest], axis=1), (NS, LANES))

    halo_wait(0)
    assemble(0, xp.at[0], qa.at[0])
    convolve(qa.at[0], 0, False)
    ready(up, down)

    def keep(i, new):
        xp[1, i, 3 : 3 + TC] = new.astype(F32).reshape(TC, NS, CH)

    @pl.loop(0, NI, unroll=2)
    def _(i):
        forward(0, xp.at[0], keep, i)

    halo_start(1, xp.at[1])
    halo_wait(1)
    assemble(1, xp.at[1], qa.at[1])
    convolve(qa.at[1], 1, False)

    def keep_out(i, new):
        outq[rows_of(i)] = new

    @pl.loop(0, NI, unroll=2)
    def _(i):
        forward(1, xp.at[1], keep_out, i)

    def leave_all(l):
        return [leave(2 * l + k, v.at[l], to.at[l]) for k, (v, to) in enumerate(
            ((result0, result0_to), (result1, result1_to)))]

    early = branch_grads(1)
    s_ubias = pre_grads(1)
    down_grads(1)
    up_grads(1)
    core_copy(1, 0).start()
    sums = backward(1)
    halo_start(2, gx)
    tap_grads(1, 1)
    to_plane(1, 0)
    tap_grads(1, 0)
    small_grads(1, early, s_ubias, sums)
    core_copy(1, 1).start()
    halo_wait(2)
    assemble(2, gx, qg)
    to_plane(1, 1)
    convolve(qg, 1, True)
    step_back(1)
    early = branch_grads(0)
    s_ubias = pre_grads(0)
    down_grads(0)
    up_grads(0)
    core_copy(0, 0).start()
    to_z(1, 0)
    to_z(1, 1)
    sums = backward(0)
    halo_start(3, gx)
    tap_grads(0, 1)
    to_plane(0, 0)
    tap_grads(0, 0)
    small_grads(0, early, s_ubias, sums)
    core_copy(0, 1).start()
    halo_wait(3)
    assemble(3, gx, qg)
    to_plane(0, 1)
    to_all(1, 0)
    to_all(1, 1)
    convolve(qg, 0, True)
    step_back(0)
    to_z(0, 0)
    to_z(0, 1)
    g = grad[...]
    high = g.astype(BF16)
    g = g - high.astype(F32)
    mid = g.astype(BF16)
    low = (g - mid.astype(F32)).astype(BF16)
    gfeat_ref[...] = tn(place[...], high) + (tn(place[...], mid) + tn(place[...], low))
    leave(4, gfeat_ref, gfeat_to).start()
    out_ref[...] = tn(place[...], outq[...]).astype(BF16)
    leave(5, out_ref, out_to).start()
    to_sibling(1, 0)
    to_sibling(1, 1)
    to_all(0, 0)
    to_all(0, 1)
    for p in range(2):
        finish(1, p)
    for copy in leave_all(1):
        copy.start()
    to_sibling(0, 0)
    for n in range(4):
        halo_done(n)
    to_sibling(0, 1)
    for p in range(2):
        finish(0, p)
    for copy in leave_all(0):
        copy.start()
    for copy in leave_all(0) + leave_all(1):
        copy.wait()
    leave(4, gfeat_ref, gfeat_to).wait()
    leave(5, out_ref, out_to).wait()


def unpack(out_in, gfeat_in, result0_in, result1_in,
           out, gfeat, gtaps, gcbias, ggain, gshift, gup_to, gubias, gdown_to, gdbias, gscale,
           few, result0, result1, gup, gdown, ins, outs):
    copies = [
        pltpu.make_async_copy(src, dst, ins.at[k])
        for k, (src, dst) in enumerate(
            ((result0_in, result0), (result1_in, result1), (gfeat_in, gfeat), (out_in, out))
        )
    ]
    for copy in copies:
        copy.start()
    leaving = [pltpu.make_async_copy(gdown, gdown_to, outs.at[0]), pltpu.make_async_copy(gup, gup_to, outs.at[1])]
    upper = lax.broadcasted_iota(jnp.int32, (8, LANES), 0) < 4

    def place_tile(l, ref, index, tile):
        t, r = divmod(index, CH // 8)
        ref[l, 8 * r : 8 * r + 8, LANES * t : LANES * t + LANES] = tile

    def place_any(l, index, tile):
        if index < TILES:
            place_tile(l, gdown, index, tile)
        else:
            place_tile(l, gup, index - TILES, tile)

    copies[0].wait()
    for l in range(2):
        for chunk in range(2 * CHUNKS):
            v = result0[l, chunk // CHUNKS, chunk % CHUNKS].astype(F32)
            for slot in range(8):
                place_any(l, 8 * chunk + slot, v[8 * slot : 8 * slot + 8])
    leaving[0].start()
    copies[1].wait()
    for l in range(2):
        for chunk in range(2 * CHUNKS):
            place_any(l, 256 + chunk, result1[l, chunk // CHUNKS, chunk % CHUNKS].astype(F32)[:8])
    leaving[1].start()
    for l in range(2):
        pair = []
        for chunk in range(2 * CHUNKS):
            v = result1[l, chunk // CHUNKS, chunk % CHUNKS].astype(F32)[SMALL_AT:]
            pair.append(v + pltpu.roll(v, 4, 0))
            if chunk % 2:
                few[4 * chunk - 4 : 4 * chunk + 4] = jnp.where(upper, pair[-2], pair[-1])
        for t in range(TAPS):
            gtaps[t, l : l + 1, :LANES] = few[t : t + 1]
            gtaps[t, l : l + 1, LANES:] = few[TAPS + t : TAPS + t + 1, :REST]
        for at, ref in ((ROW_CBIAS, gcbias), (ROW_GAIN, ggain), (ROW_SHIFT, gshift),
                        (ROW_DBIAS, gdbias), (ROW_SCALE, gscale)):
            ref[l : l + 1, :LANES] = few[at : at + 1]
            ref[l : l + 1, LANES:] = few[at + 1 : at + 2, :REST]
        for t in range(6):
            gubias[l : l + 1, LANES * t : LANES * t + LANES] = few[ROW_UBIAS + t : ROW_UBIAS + t + 1]
    for copy in copies[2:] + leaving:
        copy.wait()


def on_device(features, cotangent, dw_kernel, conv_bias, ln_gain, ln_shift, up_weight, up_bias,
              down_weight, down_bias, layer_scale):
    depth = dw_kernel.shape[0]
    pixel_total = PX * lax.axis_size("slide") * lax.axis_size("ty") * lax.axis_size("tx")
    place, edges, spread = (jnp.asarray(v, BF16) for v in one_hots())
    taps = dw_kernel.reshape(depth, TAPS, CH).transpose(1, 0, 2)
    vmem = pl.BlockSpec(memory_space=pltpu.VMEM)
    dma = pltpu.SemaphoreType.DMA
    plane = (NI, TC + 6, NS, CH)
    wide = (NI + 6, WIDE, NS, LANES)
    hbm = pl.BlockSpec(memory_space=pltpu.HBM)
    results = tuple(jax.ShapeDtypeStruct((depth, 2, CHUNKS, rows, LANES), BF16) for rows in PARTS)
    out, gfeat, result0, result1 = pl.pallas_call(
        functools.partial(kernel, 1.0 / math.sqrt(pixel_total)),
        out_shape=(
            jax.ShapeDtypeStruct((PX, CH), BF16),
            jax.ShapeDtypeStruct((PX, CH), F32),
            *results,
        ),
        in_specs=[hbm] * 3 + [vmem] * 3 + [hbm, vmem, hbm] + [vmem] * 2 + [hbm] * 3,
        out_specs=(hbm,) * 4,
        scratch_shapes=[
            pltpu.VMEM((PX, CH), BF16),
            pltpu.VMEM((PX, CH), BF16),
            pltpu.VMEM((TAPS, depth, CH), F32),
            pltpu.VMEM((depth, CH, HID), BF16),
            pltpu.VMEM((depth, CH, HID), BF16),
            pltpu.VMEM(place.shape, BF16),
            pltpu.VMEM(edges.shape, BF16),
            pltpu.VMEM(spread.shape, BF16),
            pltpu.VMEM((PX, CH), BF16),
            pltpu.VMEM((PX, CH), F32),
            *(pltpu.VMEM(v.shape, v.dtype) for v in results),
            dma((8,)), dma((6,)),
            pltpu.VMEM((2, *plane), F32),
            pltpu.VMEM(plane, F32),
            pltpu.VMEM((2, *wide), F32),
            pltpu.VMEM(wide, F32),
            pltpu.VMEM((NI, PACK, NS, LANES), F32),
            pltpu.VMEM((NI, TC * NS, CH), F32),
            pltpu.VMEM((2, PX, CH), F32),
            pltpu.VMEM((2, PX, 1), F32),
            pltpu.VMEM((2, PX, CH), BF16),
            pltpu.VMEM((2, PX, HID), BF16),
            pltpu.VMEM((2, PX, HID), F32),
            pltpu.VMEM((2, PX, CH), F32),
            pltpu.VMEM((PX, CH), BF16),
            pltpu.VMEM((PX, HID), BF16),
            pltpu.VMEM((NI, PACK, NS, LANES), F32),
            pltpu.VMEM((2, 3, TC + 6, NS, CH), F32),
            pltpu.VMEM((2, TAPS, NS, LANES), F32),
            pltpu.VMEM((LANES, LANES), F32),
            pltpu.VMEM((PX, CH), F32),
            pltpu.VMEM((PX, CH), BF16),
            pltpu.VMEM((2, 2, TAPS, NS, LANES), F32),
            *(pltpu.VMEM((2, 2, CHUNKS, rows, LANES), F32) for rows in PARTS),
            *(pltpu.VMEM((2, CHUNKS, rows, LANES), F32) for rows in PARTS),
            *(pltpu.VMEM((2, CHUNKS, rows, LANES), BF16) for rows in PARTS),
            *(pltpu.VMEM((2, CHUNKS, rows, LANES), BF16) for rows in PARTS),
            *(pltpu.VMEM((2, NZ, rows, LANES), BF16) for rows in PARTS),
            pltpu.VMEM((4, 2, 3, TR, CH), BF16),
            pltpu.VMEM((4, 2, 3, TC, CH), BF16),
            pltpu.VMEM((4, 2, 3, TR, CH), BF16),
            pltpu.VMEM((4, 6, 3, TC, CH), BF16),
            dma((4, 8)), dma((4, 8)),
            dma((4,)), dma((4,)),
            dma((4, CHUNKS)), dma((4, CHUNKS)),
            dma((4, NZ)), dma((4, NZ)),
            dma((4, CHUNKS)), dma((4, CHUNKS)),
            dma((4, CHUNKS)), dma((4, CHUNKS)),
        ],
        compiler_params=pltpu.CompilerParams(
            collective_id=0, has_side_effects=True, vmem_limit_bytes=56 * 2**20
        ),
    )(
        features.reshape(PX, CH), cotangent.reshape(PX, CH), taps, conv_bias, ln_gain, ln_shift,
        up_weight, up_bias, down_weight.transpose(0, 2, 1), down_bias, layer_scale, place, edges, spread,
    )
    vector = jax.ShapeDtypeStruct((depth, CH), F32)
    weight = jax.ShapeDtypeStruct((depth, CH, HID), F32)
    out, gfeat, gtaps, gcbias, ggain, gshift, gup, gubias, gdown, gdbias, gscale = pl.pallas_call(
        unpack,
        out_shape=(
            jax.ShapeDtypeStruct((PX, CH), BF16),
            jax.ShapeDtypeStruct((PX, CH), F32),
            jax.ShapeDtypeStruct((TAPS, depth, CH), F32),
            vector, vector, vector, weight, jax.ShapeDtypeStruct((depth, HID), F32), weight, vector, vector,
        ),
        in_specs=[hbm] * 4,
        out_specs=(vmem,) * 6 + (hbm, vmem, hbm) + (vmem,) * 2,
        scratch_shapes=[
            pltpu.VMEM((LANES, LANES), F32),
            *(pltpu.VMEM(v.shape, v.dtype) for v in results),
            pltpu.VMEM((depth, CH, HID), F32),
            pltpu.VMEM((depth, CH, HID), F32),
            dma((4,)),
            dma((2,)),
        ],
        compiler_params=pltpu.CompilerParams(vmem_limit_bytes=56 * 2**20),
    )(out, gfeat, result0, result1)
    return (
        out.reshape(1, TR, TC, CH),
        gfeat.reshape(1, TR, TC, CH),
        gtaps.transpose(1, 0, 2).reshape(depth, SPAN, SPAN, CH),
        gcbias,
        ggain,
        gshift,
        gup,
        gubias,
        gdown.transpose(0, 2, 1),
        gdbias,
        gscale,
    )


def solution(mesh):
    tiled = P("slide", "ty", "tx", None)
    return jax.shard_map(
        on_device,
        mesh=mesh,
        in_specs=(tiled, tiled) + (P(),) * 9,
        out_specs=(tiled, tiled) + (P(),) * 9,
        check_vma=False,
    )
```

```python
import functools
import math

import jax
import jax.numpy as jnp
import numpy as np
from jax import lax
from jax.experimental import pallas as pl
from jax.experimental.pallas import tpu as pltpu
from jax.sharding import PartitionSpec as P

MESH = pl.DeviceIdType.MESH
F32 = jnp.float32
BF16 = jnp.bfloat16
ROOT_HALF = 0.7071067811865476
INV_ROOT_TAU = 0.3989422804014327
EPSILON = 1e-06

TR, TC, CH, HID = 32, 16, 192, 768
PX = TR * TC
NI, NS = 4, 8
MARGIN = 3
SPAN = 7
TAPS = SPAN * SPAN
LANES = 128
REST = CH - LANES
PACK = TC + TC // 2
WIDE = (TC + 2 * MARGIN) + (TC // 2 + 2 * MARGIN)
PARTS = (64, 16)
TILES = CH // 8 * (HID // LANES)
SMALL_AT = 8
CHUNKS = 16
NZ = 8
HALOS = ((-1, -1), (-1, 0), (-1, 1), (1, -1), (1, 0), (1, 1), (0, -1), (0, 1))

ROW_CBIAS, ROW_GAIN, ROW_SHIFT, ROW_DBIAS, ROW_SCALE, ROW_UBIAS = 98, 100, 102, 104, 106, 108


def pixel_order():
    q = np.arange(PX)
    return (4 * (q % NS) + q // (TC * NS)) * TC + (q // NS) % TC


def one_hots():
    order = pixel_order()
    place = np.zeros((PX, PX), np.float32)
    place[np.arange(PX), order] = 1.0
    inverse = np.argsort(order)
    edge_rows = np.concatenate([np.arange(3 * TC), np.arange((TR - 3) * TC, TR * TC)])
    edges = np.zeros((6 * TC, PX), np.float32)
    edges[np.arange(6 * TC), inverse[edge_rows]] = 1.0
    spread = np.zeros((2, 3, TC + 6, NS, 3, 3, TC), np.float32)
    for cc in range(TC + 6):
        source, column = (0, TC - 3 + cc) if cc < 3 else (1, cc - 3) if cc < TC + 3 else (2, cc - TC - 3)
        for u in range(3):
            spread[0, u, cc, 0, source, u, column] = 1.0
            spread[1, u, cc, NS - 1, source, u, column] = 1.0
    spread = spread.reshape(2, 3 * (TC + 6) * NS, 9 * TC)
    return place, edges, spread


def tn(a, b):
    return lax.dot_general(a, b, (((0,), (0,)), ((), ())), preferred_element_type=F32)


def nt(a, b):
    return lax.dot_general(a, b, (((1,), (1,)), ((), ())), preferred_element_type=F32)


def nn(a, b):
    return jnp.dot(a, b, preferred_element_type=F32)


def kernel(
    factor,
    feat_in, cot_in, dw_in, cbias, gain, shift, up_in, ubias, down_in, dbias, scale, place_in, edges_in, spread_in,
    out_to, gfeat_to, result0_to, result1_to,
    feat, cot, dw, up, down, place, edges, spread, out_ref, gfeat_ref, result0, result1, ins, outs,
    xp, gx, qa, qg, cbuf, convs, unit, inv, normed, act, slope, branch, gbr, gpre, gcp, tq, taps, small,
    grad, outq, wexp,
    pay0, pay1, core0, core1, sbuf0, sbuf1, rbuf0, rbuf1, zbuf0, zbuf1,
    csend, rsend, crecv, rrecv,
    hs, hr, cs, cr, xs, xr, zs, zr, gs, gr, ls, lr,
):
    yh = lax.axis_index("slide")
    ty = lax.axis_index("ty")
    tx = lax.axis_index("tx")
    core = lax.rem(tx, 2)
    yl = lax.rem(lax.div(tx, 2), 2)
    z = lax.div(tx, 4)
    other = 1 - core
    me = ty * 4 + yh * 2 + yl
    sibling = (yh, ty, z * 4 + yl * 2 + other)

    def plane_peer(d):
        py = lax.rem(ty + lax.div(d, 4), 4)
        ph = lax.rem(yh + lax.rem(lax.div(d, 2), 2), 2)
        pl_ = lax.rem(yl + lax.rem(d, 2), 2)
        return py * 4 + ph * 2 + pl_, (ph, py, z * 4 + pl_ * 2 + core)

    def z_peer(d):
        pz = lax.rem(z + d, NZ)
        return pz, (yh, ty, pz * 4 + yl * 2 + core)

    arrivals = {}
    loads = ((feat_in, feat), (place_in, place), (edges_in, edges), (cot_in, cot), (dw_in, dw), (spread_in, spread),
             (up_in, up), (down_in, down))
    for k, (src, dst) in enumerate(loads):
        arrivals[id(dst)] = pltpu.make_async_copy(src, dst, ins.at[k])
        arrivals[id(dst)].start()

    barrier = pltpu.get_barrier_semaphore()

    def greet(device):
        pl.semaphore_signal(barrier, inc=1, device_id=device, device_id_type=MESH)

    for dy, dx in HALOS:
        greet((yh, lax.rem(ty + dy + 4, 4), lax.rem(tx + dx + 32, 32)))
    greet(sibling)

    @pl.loop(1, CHUNKS)
    def _(d):
        greet(plane_peer(d)[1])

    @pl.loop(1, NZ)
    def _(d):
        greet(z_peer(d)[1])

    def ready(*refs):
        for ref in refs:
            arrivals[id(ref)].wait()

    def leave(k, src, dst):
        return pltpu.make_async_copy(src, dst, outs.at[k])

    def there(dy, dx):
        flags = []
        if dy:
            flags.append(jnp.logical_and(ty + dy >= 0, ty + dy < 4))
        if dx:
            flags.append(jnp.logical_and(tx + dx >= 0, tx + dx < 32))
        return functools.reduce(jnp.logical_and, flags)

    def halo_copy(n, dy, dx):
        if dy == 0:
            slot = 6 if dx > 0 else 7
            src, dst = csend.at[n, 0 if dx < 0 else 1], crecv.at[n, slot - 6]
        else:
            slot = (1 if dy > 0 else 4) - dx
            src, dst = rsend.at[n, 0 if dy < 0 else 1], rrecv.at[n, slot]
        return pltpu.make_async_remote_copy(
            src_ref=src, dst_ref=dst, send_sem=hs.at[n, slot], recv_sem=hr.at[n, slot],
            device_id=(yh, ty + dy, tx + dx), device_id_type=MESH,
        )

    def halo_start(n, plane):
        flat = jnp.concatenate([plane[i, 3 : 3 + TC].reshape(TC * NS, CH) for i in range(NI)], axis=0)
        strips = nn(edges[...], flat.astype(BF16)).astype(BF16)
        rsend[n] = strips.reshape(2, 3, TC, CH)
        for c in range(3):
            csend[n, 0, c] = plane[:, 3 + c].reshape(TR, CH).astype(BF16)
            csend[n, 1, c] = plane[:, TC + c].reshape(TR, CH).astype(BF16)
        if n == 0:
            pl.semaphore_wait(barrier, 8 + 1 + CHUNKS - 1 + NZ - 1)
        for dy, dx in HALOS:

            @pl.when(there(dy, dx))
            def _(dy=dy, dx=dx):
                halo_copy(n, dy, dx).start()

    def halo_wait(n):
        for dy, dx in HALOS:

            @pl.when(there(-dy, -dx))
            def _(dy=dy, dx=dx):
                halo_copy(n, dy, dx).wait_recv()

            @pl.when(jnp.logical_not(there(-dy, -dx)))
            def _(dy=dy, dx=dx):
                if dy == 0:
                    crecv[n, 0 if dx > 0 else 1] = jnp.zeros((3, TR, CH), BF16)
                else:
                    rrecv[n, (1 if dy > 0 else 4) - dx] = jnp.zeros((3, TC, CH), BF16)

    def halo_done(n):
        for dy, dx in HALOS:

            @pl.when(there(dy, dx))
            def _(dy=dy, dx=dx):
                halo_copy(n, dy, dx).wait_send()

    def assemble(n, plane, q):
        for c in range(3):
            plane[:, c] = crecv[n, 0, c].astype(F32).reshape(NI, NS, CH)
            plane[:, TC + 3 + c] = crecv[n, 1, c].astype(F32).reshape(NI, NS, CH)
        for side in range(2):
            strips = jnp.concatenate([rrecv[n, 3 * side + k].reshape(3 * TC, CH) for k in range(3)], axis=0)
            tq[side] = nn(spread[side], strips).reshape(3, TC + 6, NS, CH)
        row = lax.broadcasted_iota(jnp.int32, (3, NS, LANES), 1)

        def fill(slot, mid, top, low):
            q[3:7, slot] = mid
            q[0:3, slot] = jnp.where(row == 0, top, pltpu.roll(mid[1:4], 1, 1))
            q[7:10, slot] = jnp.where(row == NS - 1, low, pltpu.roll(mid[0:3], NS - 1, 1))

        @pl.loop(0, TC + 6, unroll=2)
        def _(cc):
            fill(cc, plane[:, cc, :, :LANES], tq[0, :, cc, :, :LANES], tq[1, :, cc, :, :LANES])

        def pair(ref, *at):
            return jnp.concatenate([ref[(*at[:-1], at[-1], slice(None), slice(LANES, CH))],
                                    ref[(*at[:-1], at[-1] + 8, slice(None), slice(LANES, CH))]], axis=-1)

        @pl.loop(0, TC // 2 + 6, unroll=2)
        def _(k):
            fill(TC + 6 + k, pair(plane, slice(None), k), pair(tq, 0, slice(None), k), pair(tq, 1, slice(None), k))

    def convolve(q, l, flip):
        def columns(part, t, base):
            sums = [[None, None] for _ in range(NI)]
            for j2 in range(SPAN + 1):
                for r in range(NI + SPAN - 1):
                    x = q[r, base + j2]
                    for i in range(NI):
                        if not 0 <= r - i < SPAN:
                            continue
                        for o in range(2):
                            if not 0 <= j2 - o < SPAN:
                                continue
                            tap = (r - i) * SPAN + j2 - o
                            term = x * wexp[l, part, TAPS - 1 - tap if flip else tap]
                            sums[i][o] = term if sums[i][o] is None else sums[i][o] + term
            for i in range(NI):
                for o in range(2):
                    cbuf[i, t + o] = sums[i][o]

        @pl.loop(0, TC // 2)
        def _(k):
            columns(0, 2 * k, 2 * k)

        @pl.loop(0, TC // 4)
        def _(k):
            columns(1, TC + 2 * k, TC + 6 + 2 * k)

    def conv_rows(i):
        half = TC * NS // 2
        conv = convs.at[i]
        conv[:, :LANES] = cbuf[i, :TC].reshape(TC * NS, LANES)
        rest = cbuf[i, TC:].reshape(half, LANES)
        conv[:half, LANES:] = rest[:, :REST]
        conv[half:, LANES:] = rest[:, REST:]
        return conv[...]

    blk = TC * NS

    def rows_of(i):
        return pl.ds(pl.multiple_of(i * blk, blk), blk)

    def forward(l, plane, into, i):
        c = conv_rows(i) + cbias[l : l + 1]
        mid = c - jnp.mean(c, axis=1, keepdims=True)
        rstd = lax.rsqrt(jnp.mean(mid * mid, axis=1, keepdims=True) + EPSILON)
        u = mid * rstd
        rows = rows_of(i)
        unit[l, rows] = u
        inv[l, rows] = rstd
        nb = (u * gain[l : l + 1] + shift[l : l + 1]).astype(BF16)
        normed[l, rows] = nb
        pre = nn(nb, up[l]) + ubias[l : l + 1]
        cdf = 0.5 * (1.0 + lax.erf(pre * ROOT_HALF))
        slope[l, rows] = cdf + pre * INV_ROOT_TAU * jnp.exp(-0.5 * pre * pre)
        ab = (pre * cdf).astype(BF16)
        act[l, rows] = ab
        br = nt(ab, down[l]) + dbias[l : l + 1]
        branch[l, rows] = br
        before = plane[i, 3 : 3 + TC].reshape(blk, CH)
        new = (before + scale[l : l + 1] * br).astype(BF16)
        into(i, new)

    def fold(v):
        return jnp.sum(v.reshape(blk // 8, 8, v.shape[1]), axis=0)

    def branch_grads(l):
        def body(i, sums):
            rows = rows_of(i)
            g = grad[rows]
            gb = (g * scale[l : l + 1]).astype(BF16)
            gbr[rows] = gb
            return sums[0] + fold(gb.astype(F32)), sums[1] + fold(g * branch[l, rows])

        return lax.fori_loop(0, NI, body, (jnp.zeros((8, CH), F32),) * 2, unroll=True)

    def pre_grads(l):
        def body(i, total):
            rows = rows_of(i)
            gp = (nn(gbr[rows], down[l]) * slope[l, rows]).astype(BF16)
            gpre[rows] = gp
            return total + fold(gp.astype(F32))

        return lax.fori_loop(0, NI, body, jnp.zeros((8, HID), F32), unroll=True)

    def backward(l):
        def body(i, sums):
            rows = rows_of(i)
            s_gain, s_shift, s_cbias = sums
            gn = nt(gpre[rows], up[l])
            u = unit[l, rows]
            s_gain = s_gain + fold(gn * u)
            s_shift = s_shift + fold(gn)
            q = gn * gain[l : l + 1]
            centred = q - jnp.mean(q, axis=1, keepdims=True) - u * jnp.mean(q * u, axis=1, keepdims=True)
            gc = (inv[l, rows] * centred).astype(BF16).astype(F32)
            s_cbias = s_cbias + fold(gc)
            gx[i, 3 : 3 + TC] = gc.reshape(TC, NS, CH)
            gcp[i, :TC] = gc[:, :LANES].reshape(TC, NS, LANES)
            half = blk // 2
            gcp[i, TC:, :, :REST] = gc[:half, LANES:].reshape(TC // 2, NS, REST)
            gcp[i, TC:, :, REST:] = gc[half:, LANES:].reshape(TC // 2, NS, REST)
            return s_gain, s_shift, s_cbias

        zero = jnp.zeros((8, CH), F32)
        return lax.fori_loop(0, NI, body, (zero, zero, zero), unroll=True)

    def put(l, index, tile):
        if index < 256:
            chunk, slot = divmod(index, 8)
            pay0[l, chunk // CHUNKS, chunk % CHUNKS, 8 * slot : 8 * slot + 8] = tile
        else:
            chunk = index - 256
            pay1[l, chunk // CHUNKS, chunk % CHUNKS, :8] = tile

    def weight_tiles(a, b, store):
        for t in range(3):
            part = tn(a[...], b[:, 256 * t : 256 * t + 256])
            for v in range(2):
                for r in range(CH // 8):
                    store((2 * t + v) * (CH // 8) + r, part[8 * r : 8 * r + 8, LANES * v : LANES * v + LANES])

    def down_grads(l):
        weight_tiles(gbr, act.at[l], lambda index, tile: put(l, index, tile))

    def up_grads(l):
        weight_tiles(normed.at[l], gpre, lambda index, tile: put(l, TILES + index, tile))

    def tap_grads(l, *parts):
        for part in parts:
            cols, base, first = ((TC, 0, 0), (TC // 2, TC + 6, TC))[part]

            @pl.loop(0, SPAN)
            def _(j):
                def body(c, sums):
                    sums = list(sums)
                    for o in range(2):
                        col = 2 * c + o
                        gcs = [gcp[i, first + col] for i in range(NI)]
                        for r in range(NI + SPAN - 1):
                            x = qa[l, r, base + col + j]
                            for i in range(NI):
                                if 0 <= r - i < SPAN:
                                    sums[r - i] = sums[r - i] + gcs[i] * x
                    return tuple(sums)

                zero = jnp.zeros((NS, LANES), F32)
                sums = lax.fori_loop(0, cols // 2, body, (zero,) * SPAN, unroll=2)
                for r in range(SPAN):
                    taps[part, r * SPAN + j] = sums[r]

    def small_grads(l, early, s_ubias, sums):
        s_dbias, s_scale = early
        s_gain, s_shift, s_cbias = sums
        small[...] = jnp.zeros((LANES, LANES), F32)
        small[:TAPS] = jnp.sum(taps[0], axis=1)
        rest = jnp.sum(taps[1], axis=1)
        small[TAPS : 2 * TAPS, :REST] = rest[:, :REST] + rest[:, REST:]
        for at, v in ((ROW_CBIAS, s_cbias), (ROW_GAIN, s_gain), (ROW_SHIFT, s_shift),
                      (ROW_DBIAS, s_dbias), (ROW_SCALE, s_scale)):
            v = jnp.sum(v, axis=0, keepdims=True)
            small[at : at + 1] = v[:, :LANES]
            small[at + 1 : at + 2, :REST] = v[:, LANES:]
        v = jnp.sum(s_ubias, axis=0, keepdims=True)
        for t in range(6):
            small[ROW_UBIAS + t : ROW_UBIAS + t + 1] = v[:, LANES * t : LANES * t + LANES]
        upper = lax.broadcasted_iota(jnp.int32, (8, LANES), 0) < 4
        for k in range(2 * CHUNKS):
            v = small[8 * (k // 2) : 8 * (k // 2) + 8]
            if k % 2:
                v = pltpu.roll(v, 4, 0)
            pay1[l, k // CHUNKS, k % CHUNKS, SMALL_AT:] = jnp.where(upper, v, 0.0)

    upper = lax.broadcasted_iota(jnp.int32, (8, LANES), 0) < 4

    def rounded(v, part):
        if part == 0:
            return v.astype(BF16)
        s = v[SMALL_AT:]
        s = s + pltpu.roll(s, 4, 0)
        high = s.astype(BF16).astype(F32)
        return jnp.concatenate([v[:SMALL_AT], jnp.where(upper, high, s - high)], axis=0).astype(BF16)

    pays, cores, sbufs, rbufs, zbufs = (pay0, pay1), (core0, core1), (sbuf0, sbuf1), (rbuf0, rbuf1), (zbuf0, zbuf1)
    results = (result0, result1)

    def core_copy(l, p):
        return pltpu.make_async_remote_copy(
            src_ref=pays[p].at[l, other], dst_ref=cores[p].at[l], send_sem=cs.at[2 * l + p], recv_sem=cr.at[2 * l + p],
            device_id=sibling, device_id_type=MESH,
        )

    def plane_copy(l, p, d):
        index, device = plane_peer(d)
        return pltpu.make_async_remote_copy(
            src_ref=sbufs[p].at[l, index], dst_ref=rbufs[p].at[l, d], send_sem=xs.at[2 * l + p, d], recv_sem=xr.at[2 * l + p, d],
            device_id=device, device_id_type=MESH,
        )

    def z_copy(l, p, d):
        return pltpu.make_async_remote_copy(
            src_ref=zbufs[p].at[l, z], dst_ref=zbufs[p].at[l, z], send_sem=zs.at[2 * l + p, d], recv_sem=zr.at[2 * l + p, z],
            device_id=z_peer(d)[1], device_id_type=MESH,
        )

    def z_arrival(l, p, d):
        pz, device = z_peer(d)
        return pltpu.make_async_remote_copy(
            src_ref=zbufs[p].at[l, pz], dst_ref=zbufs[p].at[l, pz], send_sem=zs.at[2 * l + p, d], recv_sem=zr.at[2 * l + p, pz],
            device_id=device, device_id_type=MESH,
        )

    def gather_copy(l, p, d):
        return pltpu.make_async_remote_copy(
            src_ref=results[p].at[l, core, me], dst_ref=results[p].at[l, core, me], send_sem=gs.at[2 * l + p, d],
            recv_sem=gr.at[2 * l + p, me], device_id=plane_peer(d)[1], device_id_type=MESH,
        )

    def gather_arrival(l, p, d):
        index, device = plane_peer(d)
        return pltpu.make_async_remote_copy(
            src_ref=results[p].at[l, core, index], dst_ref=results[p].at[l, core, index], send_sem=gs.at[2 * l + p, d],
            recv_sem=gr.at[2 * l + p, index], device_id=device, device_id_type=MESH,
        )

    def relay_copy(l, p, index):
        return pltpu.make_async_remote_copy(
            src_ref=results[p].at[l, core, index], dst_ref=results[p].at[l, core, index], send_sem=ls.at[2 * l + p, index],
            recv_sem=lr.at[2 * l + p, index], device_id=sibling, device_id_type=MESH,
        )

    def relay_arrival(l, p, index):
        return pltpu.make_async_remote_copy(
            src_ref=results[p].at[l, other, index], dst_ref=results[p].at[l, other, index], send_sem=ls.at[2 * l + p, index],
            recv_sem=lr.at[2 * l + p, index], device_id=sibling, device_id_type=MESH,
        )

    def to_plane(l, p):
        core_copy(l, p).wait_recv()

        @pl.loop(0, CHUNKS)
        def _(k):
            d = lax.rem(k + 1, CHUNKS)
            index, _ = plane_peer(d)
            v = pays[p][l, core, index] + cores[p][l, index]
            sbufs[p][l, index] = rounded(v, p)

            @pl.when(d > 0)
            def _():
                plane_copy(l, p, d).start()

    def to_z(l, p):
        @pl.loop(1, CHUNKS)
        def _(d):
            plane_copy(l, p, d).wait_recv()

        v = lax.fori_loop(1, CHUNKS, lambda d, v: v + rbufs[p][l, d].astype(F32), sbufs[p][l, me].astype(F32))
        zbufs[p][l, z] = rounded(v, p)

        @pl.loop(1, NZ)
        def _(d):
            z_copy(l, p, d).start()

    def to_all(l, p):
        @pl.loop(1, NZ)
        def _(d):
            z_arrival(l, p, d).wait_recv()

        v = zbufs[p][l, 0].astype(F32)
        for k in range(1, NZ):
            v = v + zbufs[p][l, k].astype(F32)
        results[p][l, core, me] = rounded(v * factor, p)

        @pl.loop(1, CHUNKS)
        def _(d):
            gather_copy(l, p, d).start()

        relay_copy(l, p, me).start()

    def to_sibling(l, p):
        @pl.loop(1, CHUNKS)
        def _(d):
            gather_arrival(l, p, d).wait_recv()
            relay_copy(l, p, plane_peer(d)[0]).start()

    def finish(l, p):
        @pl.loop(0, CHUNKS)
        def _(k):
            relay_arrival(l, p, k).wait_recv()
            relay_copy(l, p, k).wait_send()

        core_copy(l, p).wait_send()

        @pl.loop(1, CHUNKS)
        def _(d):
            plane_copy(l, p, d).wait_send()
            gather_copy(l, p, d).wait_send()

        @pl.loop(1, NZ)
        def _(d):
            z_copy(l, p, d).wait_send()


    def flat_rows(plane, i):
        return plane[i, 3 : 3 + TC].reshape(blk, CH)

    def step_back(l):
        @pl.loop(0, NI)
        def _(i):
            rows = rows_of(i)
            grad[rows] = grad[rows] + conv_rows(i)

    ready(feat, place, edges)
    xp[0, :, 3 : 3 + TC] = nn(place[...], feat[...]).reshape(NI, TC, NS, CH)
    halo_start(0, xp.at[0])
    ready(cot, dw, spread)
    grad[...] = nn(place[...], cot[...])

    @pl.loop(0, TAPS)
    def _(t):
        for l in range(2):
            tap = dw[t, l : l + 1]
            rest = tap[:, LANES:]
            wexp[l, 0, t] = jnp.broadcast_to(tap[:, :LANES], (NS, LANES))
            wexp[l, 1, t] = jnp.broadcast_to(jnp.concatenate([rest, rest], axis=1), (NS, LANES))

    halo_wait(0)
    assemble(0, xp.at[0], qa.at[0])
    convolve(qa.at[0], 0, False)
    ready(up, down)

    def keep(i, new):
        xp[1, i, 3 : 3 + TC] = new.astype(F32).reshape(TC, NS, CH)

    @pl.loop(0, NI, unroll=2)
    def _(i):
        forward(0, xp.at[0], keep, i)

    halo_start(1, xp.at[1])
    halo_wait(1)
    assemble(1, xp.at[1], qa.at[1])
    convolve(qa.at[1], 1, False)

    def keep_out(i, new):
        outq[rows_of(i)] = new

    @pl.loop(0, NI, unroll=2)
    def _(i):
        forward(1, xp.at[1], keep_out, i)

    def leave_all(l):
        return [leave(2 * l + k, v.at[l], to.at[l]) for k, (v, to) in enumerate(
            ((result0, result0_to), (result1, result1_to)))]

    early = branch_grads(1)
    s_ubias = pre_grads(1)
    down_grads(1)
    up_grads(1)
    core_copy(1, 0).start()
    sums = backward(1)
    halo_start(2, gx)
    tap_grads(1, 1)
    to_plane(1, 0)
    tap_grads(1, 0)
    small_grads(1, early, s_ubias, sums)
    core_copy(1, 1).start()
    halo_wait(2)
    assemble(2, gx, qg)
    to_plane(1, 1)
    convolve(qg, 1, True)
    step_back(1)
    early = branch_grads(0)
    s_ubias = pre_grads(0)
    down_grads(0)
    up_grads(0)
    core_copy(0, 0).start()
    to_z(1, 0)
    to_z(1, 1)
    sums = backward(0)
    halo_start(3, gx)
    tap_grads(0, 1)
    to_plane(0, 0)
    tap_grads(0, 0)
    small_grads(0, early, s_ubias, sums)
    core_copy(0, 1).start()
    halo_wait(3)
    assemble(3, gx, qg)
    to_plane(0, 1)
    to_all(1, 0)
    to_all(1, 1)
    convolve(qg, 0, True)
    step_back(0)
    to_z(0, 0)
    to_z(0, 1)
    g = grad[...]
    high = g.astype(BF16)
    g = g - high.astype(F32)
    mid = g.astype(BF16)
    low = (g - mid.astype(F32)).astype(BF16)
    gfeat_ref[...] = tn(place[...], high) + (tn(place[...], mid) + tn(place[...], low))
    leave(4, gfeat_ref, gfeat_to).start()
    out_ref[...] = tn(place[...], outq[...]).astype(BF16)
    leave(5, out_ref, out_to).start()
    to_sibling(1, 0)
    to_sibling(1, 1)
    to_all(0, 0)
    to_all(0, 1)
    for p in range(2):
        finish(1, p)
    for copy in leave_all(1):
        copy.start()
    to_sibling(0, 0)
    for n in range(4):
        halo_done(n)
    to_sibling(0, 1)
    for p in range(2):
        finish(0, p)
    for copy in leave_all(0):
        copy.start()
    for copy in leave_all(0) + leave_all(1):
        copy.wait()
    leave(4, gfeat_ref, gfeat_to).wait()
    leave(5, out_ref, out_to).wait()


def unpack(out_in, gfeat_in, result0_in, result1_in,
           out, gfeat, gtaps, gcbias, ggain, gshift, gup, gubias, gdown, gdbias, gscale,
           few, result0, result1, ins):
    copies = [
        pltpu.make_async_copy(src, dst, ins.at[k])
        for k, (src, dst) in enumerate(
            ((result0_in, result0), (result1_in, result1), (gfeat_in, gfeat), (out_in, out))
        )
    ]
    for copy in copies:
        copy.start()
    upper = lax.broadcasted_iota(jnp.int32, (8, LANES), 0) < 4

    def place_tile(l, ref, index, tile):
        t, r = divmod(index, CH // 8)
        ref[l, 8 * r : 8 * r + 8, LANES * t : LANES * t + LANES] = tile

    def place_any(l, index, tile):
        if index < TILES:
            place_tile(l, gdown, index, tile)
        else:
            place_tile(l, gup, index - TILES, tile)

    copies[0].wait()
    for l in range(2):
        for chunk in range(2 * CHUNKS):
            v = result0[l, chunk // CHUNKS, chunk % CHUNKS].astype(F32)
            for slot in range(8):
                place_any(l, 8 * chunk + slot, v[8 * slot : 8 * slot + 8])
    copies[1].wait()
    for l in range(2):
        for chunk in range(2 * CHUNKS):
            place_any(l, 256 + chunk, result1[l, chunk // CHUNKS, chunk % CHUNKS].astype(F32)[:8])
    for l in range(2):
        pair = []
        for chunk in range(2 * CHUNKS):
            v = result1[l, chunk // CHUNKS, chunk % CHUNKS].astype(F32)[SMALL_AT:]
            pair.append(v + pltpu.roll(v, 4, 0))
            if chunk % 2:
                few[4 * chunk - 4 : 4 * chunk + 4] = jnp.where(upper, pair[-2], pair[-1])
        for t in range(TAPS):
            gtaps[t, l : l + 1, :LANES] = few[t : t + 1]
            gtaps[t, l : l + 1, LANES:] = few[TAPS + t : TAPS + t + 1, :REST]
        for at, ref in ((ROW_CBIAS, gcbias), (ROW_GAIN, ggain), (ROW_SHIFT, gshift),
                        (ROW_DBIAS, gdbias), (ROW_SCALE, gscale)):
            ref[l : l + 1, :LANES] = few[at : at + 1]
            ref[l : l + 1, LANES:] = few[at + 1 : at + 2, :REST]
        for t in range(6):
            gubias[l : l + 1, LANES * t : LANES * t + LANES] = few[ROW_UBIAS + t : ROW_UBIAS + t + 1]
    for copy in copies[2:]:
        copy.wait()


def on_device(features, cotangent, dw_kernel, conv_bias, ln_gain, ln_shift, up_weight, up_bias,
              down_weight, down_bias, layer_scale):
    depth = dw_kernel.shape[0]
    pixel_total = PX * lax.axis_size("slide") * lax.axis_size("ty") * lax.axis_size("tx")
    place, edges, spread = (jnp.asarray(v, BF16) for v in one_hots())
    taps = dw_kernel.reshape(depth, TAPS, CH).transpose(1, 0, 2)
    vmem = pl.BlockSpec(memory_space=pltpu.VMEM)
    dma = pltpu.SemaphoreType.DMA
    plane = (NI, TC + 6, NS, CH)
    wide = (NI + 6, WIDE, NS, LANES)
    hbm = pl.BlockSpec(memory_space=pltpu.HBM)
    results = tuple(jax.ShapeDtypeStruct((depth, 2, CHUNKS, rows, LANES), BF16) for rows in PARTS)
    out, gfeat, result0, result1 = pl.pallas_call(
        functools.partial(kernel, 1.0 / math.sqrt(pixel_total)),
        out_shape=(
            jax.ShapeDtypeStruct((PX, CH), BF16),
            jax.ShapeDtypeStruct((PX, CH), F32),
            *results,
        ),
        in_specs=[hbm] * 3 + [vmem] * 3 + [hbm, vmem, hbm] + [vmem] * 2 + [hbm] * 3,
        out_specs=(hbm,) * 4,
        scratch_shapes=[
            pltpu.VMEM((PX, CH), BF16),
            pltpu.VMEM((PX, CH), BF16),
            pltpu.VMEM((TAPS, depth, CH), F32),
            pltpu.VMEM((depth, CH, HID), BF16),
            pltpu.VMEM((depth, CH, HID), BF16),
            pltpu.VMEM(place.shape, BF16),
            pltpu.VMEM(edges.shape, BF16),
            pltpu.VMEM(spread.shape, BF16),
            pltpu.VMEM((PX, CH), BF16),
            pltpu.VMEM((PX, CH), F32),
            *(pltpu.VMEM(v.shape, v.dtype) for v in results),
            dma((8,)), dma((6,)),
            pltpu.VMEM((2, *plane), F32),
            pltpu.VMEM(plane, F32),
            pltpu.VMEM((2, *wide), F32),
            pltpu.VMEM(wide, F32),
            pltpu.VMEM((NI, PACK, NS, LANES), F32),
            pltpu.VMEM((NI, TC * NS, CH), F32),
            pltpu.VMEM((2, PX, CH), F32),
            pltpu.VMEM((2, PX, 1), F32),
            pltpu.VMEM((2, PX, CH), BF16),
            pltpu.VMEM((2, PX, HID), BF16),
            pltpu.VMEM((2, PX, HID), F32),
            pltpu.VMEM((2, PX, CH), F32),
            pltpu.VMEM((PX, CH), BF16),
            pltpu.VMEM((PX, HID), BF16),
            pltpu.VMEM((NI, PACK, NS, LANES), F32),
            pltpu.VMEM((2, 3, TC + 6, NS, CH), F32),
            pltpu.VMEM((2, TAPS, NS, LANES), F32),
            pltpu.VMEM((LANES, LANES), F32),
            pltpu.VMEM((PX, CH), F32),
            pltpu.VMEM((PX, CH), BF16),
            pltpu.VMEM((2, 2, TAPS, NS, LANES), F32),
            *(pltpu.VMEM((2, 2, CHUNKS, rows, LANES), F32) for rows in PARTS),
            *(pltpu.VMEM((2, CHUNKS, rows, LANES), F32) for rows in PARTS),
            *(pltpu.VMEM((2, CHUNKS, rows, LANES), BF16) for rows in PARTS),
            *(pltpu.VMEM((2, CHUNKS, rows, LANES), BF16) for rows in PARTS),
            *(pltpu.VMEM((2, NZ, rows, LANES), BF16) for rows in PARTS),
            pltpu.VMEM((4, 2, 3, TR, CH), BF16),
            pltpu.VMEM((4, 2, 3, TC, CH), BF16),
            pltpu.VMEM((4, 2, 3, TR, CH), BF16),
            pltpu.VMEM((4, 6, 3, TC, CH), BF16),
            dma((4, 8)), dma((4, 8)),
            dma((4,)), dma((4,)),
            dma((4, CHUNKS)), dma((4, CHUNKS)),
            dma((4, NZ)), dma((4, NZ)),
            dma((4, CHUNKS)), dma((4, CHUNKS)),
            dma((4, CHUNKS)), dma((4, CHUNKS)),
        ],
        compiler_params=pltpu.CompilerParams(
            collective_id=0, has_side_effects=True, vmem_limit_bytes=56 * 2**20
        ),
    )(
        features.reshape(PX, CH), cotangent.reshape(PX, CH), taps, conv_bias, ln_gain, ln_shift,
        up_weight, up_bias, down_weight.transpose(0, 2, 1), down_bias, layer_scale, place, edges, spread,
    )
    vector = jax.ShapeDtypeStruct((depth, CH), F32)
    weight = jax.ShapeDtypeStruct((depth, CH, HID), F32)
    out, gfeat, gtaps, gcbias, ggain, gshift, gup, gubias, gdown, gdbias, gscale = pl.pallas_call(
        unpack,
        out_shape=(
            jax.ShapeDtypeStruct((PX, CH), BF16),
            jax.ShapeDtypeStruct((PX, CH), F32),
            jax.ShapeDtypeStruct((TAPS, depth, CH), F32),
            vector, vector, vector, weight, jax.ShapeDtypeStruct((depth, HID), F32), weight, vector, vector,
        ),
        in_specs=[hbm] * 4,
        out_specs=(vmem,) * 11,
        scratch_shapes=[
            pltpu.VMEM((LANES, LANES), F32),
            *(pltpu.VMEM(v.shape, v.dtype) for v in results),
            dma((4,)),
        ],
        compiler_params=pltpu.CompilerParams(vmem_limit_bytes=56 * 2**20),
    )(out, gfeat, result0, result1)
    return (
        out.reshape(1, TR, TC, CH),
        gfeat.reshape(1, TR, TC, CH),
        gtaps.transpose(1, 0, 2).reshape(depth, SPAN, SPAN, CH),
        gcbias,
        ggain,
        gshift,
        gup,
        gubias,
        gdown.transpose(0, 2, 1),
        gdbias,
        gscale,
    )


def solution(mesh):
    tiled = P("slide", "ty", "tx", None)
    return jax.shard_map(
        on_device,
        mesh=mesh,
        in_specs=(tiled, tiled) + (P(),) * 9,
        out_specs=(tiled, tiled) + (P(),) * 9,
        check_vma=False,
    )
```
